128 devices in a mesh: gx: 8 (over x, z_hi), gy: 4 (over z_lo, core), gz: 4 (over y).
Axes of the slice: x: 4, y: 4, z: 4 (z_hi: 2, z_lo: 2; z = z_hi * 2 + z_lo), core: 2. Of those that a mesh axis runs over, the one named last changes fastest.
Arguments:
- rhs_field: float32 [192, 128, 1024], P('gz', 'gy', 'gx'), may hold values from -24 to 24
- stiffness: float32 [192, 128, 1024], P('gz', 'gy', 'gx'), may hold values from 0.03 to 0.3
Outputs:
- solution: float32 [192, 128, 1024], P('gz', 'gy', 'gx')
- residual: float32 [192, 128, 1024], P('gz', 'gy', 'gx')
The draws below stay inside these ranges and needn't reach their ends.
All inputs are finite; a program needn't handle non-finite values.
Results may differ from the reference program's by a relative error of at most 0.0015.
Values sent between devices are 32-bit elements; how exact they have to be, the bound alone decides.
No kernel may reach another device: no remote copies, remote signals or barrier semaphores. Data moves between devices by JAX's collectives and lax.ppermute only.
A program may use at most 128 MiB of HBM per device.

```python
import math
import jax
import jax.numpy as jnp
from jax import lax

CX = 128
CY = 32
CZ = 48
OV = 4
ITERS = 3
NX = 1024
NY = 128
NZ = 192
N_GX = 8
N_GY = 4
N_GZ = 4


def draw_rhs_field(key, part):
    key = jax.random.fold_in(key, 7)
    depth_pos = jnp.arange(NZ, dtype=jnp.float32) / NZ
    row_pos = jnp.arange(NY, dtype=jnp.float32) / NY
    column_pos = jnp.arange(NX, dtype=jnp.float32) / NX
    rising = depth_pos[:, None, None] + row_pos[None, :, None] + column_pos[None, None, :]
    growth = jnp.exp(0.5 * math.log(3.0) * rising)
    jitter = jnp.clip(jax.random.normal(key, (NZ, NY, NX), jnp.float32), -4.5, 4.5)
    return growth * jitter


def block_levels(rng, shape, shards, low, high):
    loudness, own = 1.0, jax.random.fold_in(rng, 6)
    for axis_at, parts in shards:
        steps = jnp.exp(jax.random.uniform(jax.random.fold_in(own, axis_at), (parts,), jnp.float32, low / len(shards), high / len(shards)))
        loudness = loudness * jnp.repeat(steps, shape[axis_at] // parts).reshape([-1 if axis == axis_at else 1 for axis in range(len(shape))])
    return loudness


def setup_inputs(seed: int = 0) -> dict:
    arg_keys = jax.random.split(jax.random.key(seed), 3)
    rhs_field = draw_rhs_field(jax.random.fold_in(arg_keys[2], 71), 0)
    stiffness = jnp.clip(jnp.exp(math.log(0.3) - 2.3025852 * jax.random.uniform(arg_keys[1], (NZ, NY, NX), jnp.float32) ** block_levels(arg_keys[1], (NZ, NY, NX), ((0, 4), (1, 4), (2, 8)), -0.2, 0.2)), 0.03, 0.3)
    return {"rhs_field": rhs_field, "stiffness": stiffness}


mass_term = 1e-05
split_term = 0.5
bend_mean = 0.1
highest = lax.Precision.HIGHEST

def sine_table(length):
    places = jnp.arange(1, length + 1, dtype=jnp.float32)
    factor = jnp.sqrt(2.0 / (length + 1.0))
    return factor * jnp.sin(jnp.pi * places[:, None] * places[None, :] / (length + 1.0))

def eigen_line(length):
    places = jnp.arange(1, length + 1, dtype=jnp.float32)
    return 2.0 - 2.0 * jnp.cos(jnp.pi * places / (length + 1.0))

def transform(values, tables):
    depth_table, row_table, column_table = tables
    values = jnp.einsum('zyx,xc->zyc', values, column_table, precision=highest)
    values = jnp.einsum('zyx,yb->zbx', values, row_table, precision=highest)
    return jnp.einsum('zyx,za->ayx', values, depth_table, precision=highest)

def local_solve(values):
    depth_len, row_len, column_len = values.shape
    tables = (sine_table(depth_len), sine_table(row_len), sine_table(column_len))
    spectrum = eigen_line(depth_len)[:, None, None] + eigen_line(row_len)[None, :, None] + eigen_line(column_len)[None, None, :]
    inverse = 1.0 / (mass_term + bend_mean * spectrum * spectrum + split_term * spectrum)
    return transform(transform(values, tables) * inverse, tables)

def laplace_wrap(values):
    beside = jnp.roll(values, -1, 0) + jnp.roll(values, 1, 0)
    beside = beside + jnp.roll(values, -1, 1) + jnp.roll(values, 1, 1)
    beside = beside + jnp.roll(values, -1, 2) + jnp.roll(values, 1, 2)
    return 6.0 * values - beside

def operate_wrap(values, stiffness):
    flux = laplace_wrap(values)
    return mass_term * values + laplace_wrap(stiffness * flux) + split_term * flux

def wrap_fold(accumulated):
    for axis_dim in range(3):
        extent = accumulated.shape[axis_dim] - 2 * OV
        core_part = lax.slice_in_dim(accumulated, OV, OV + extent, axis=axis_dim)
        before = lax.slice_in_dim(accumulated, 0, OV, axis=axis_dim)
        beyond = lax.slice_in_dim(accumulated, OV + extent, 2 * OV + extent, axis=axis_dim)
        first_cut = [slice(None)] * 3
        first_cut[axis_dim] = slice(0, OV)
        last_cut = [slice(None)] * 3
        last_cut[axis_dim] = slice(extent - OV, extent)
        accumulated = core_part.at[tuple(first_cut)].add(beyond).at[tuple(last_cut)].add(before)
    return accumulated

def precondition(residual):
    padded = jnp.pad(residual, OV, mode='wrap')
    extent = (CZ + 2 * OV, CY + 2 * OV, CX + 2 * OV)

    def visit(turn_index, accumulated):
        brick_z = (turn_index // (N_GY * N_GX)).astype(jnp.int32)
        brick_y = (turn_index // N_GX % N_GY).astype(jnp.int32)
        brick_x = (turn_index % N_GX).astype(jnp.int32)
        corner = (brick_z * CZ, brick_y * CY, brick_x * CX)
        piece = lax.dynamic_slice(padded, corner, extent)
        solved = local_solve(piece)
        present = lax.dynamic_slice(accumulated, corner, extent)
        return lax.dynamic_update_slice(accumulated, present + solved, corner)
    accumulated = lax.fori_loop(0, N_GZ * N_GY * N_GX, visit, jnp.zeros_like(padded))
    return wrap_fold(accumulated)

def reference(rhs_field, stiffness):
    solution = jnp.zeros_like(rhs_field)
    residual = rhs_field
    smoothed = precondition(residual)
    direction = smoothed
    current = jnp.sum(residual * smoothed)
    for turn_index in range(ITERS):
        applied = operate_wrap(direction, stiffness)
        step_size = current / jnp.sum(direction * applied)
        solution = solution + step_size * direction
        residual = residual - step_size * applied
        if turn_index + 1 < ITERS:
            smoothed = precondition(residual)
            following = jnp.sum(residual * smoothed)
            direction = smoothed + following / current * direction
            current = following
    return (solution, residual)
```

```python
import jax
import jax.numpy as jnp
from jax import lax
from jax.sharding import PartitionSpec as P

OV = 4
ITERS = 3
AXES = ("gx", "gy", "gz")

mass_term = 1e-05
split_term = 0.5
bend_mean = 0.1
highest = lax.Precision.HIGHEST


def shifted(block, axis, step):
    count = lax.axis_size(axis)
    return lax.ppermute(block, axis, [(i, (i + step) % count) for i in range(count)])


def extended(block, sides, width):
    for axis, dim in sides:
        low = shifted(
            lax.slice_in_dim(block, block.shape[dim] - width, None, axis=dim), axis, 1
        )
        high = shifted(lax.slice_in_dim(block, 0, width, axis=dim), axis, -1)
        block = jnp.concatenate([low, block, high], axis=dim)
    return block


def sine_table(length):
    places = jnp.arange(1, length + 1, dtype=jnp.float32)
    factor = jnp.sqrt(2.0 / (length + 1.0))
    return factor * jnp.sin(jnp.pi * places[:, None] * places[None, :] / (length + 1.0))


def eigen_line(length):
    places = jnp.arange(1, length + 1, dtype=jnp.float32)
    return 2.0 - 2.0 * jnp.cos(jnp.pi * places / (length + 1.0))


def transform(values, tables):
    depth_table, row_table, column_table = tables
    values = jnp.einsum("zyx,xc->zyc", values, column_table, precision=highest)
    values = jnp.einsum("zyx,yb->zbx", values, row_table, precision=highest)
    return jnp.einsum("zyx,za->ayx", values, depth_table, precision=highest)


def local_solve(values):
    depth_len, row_len, column_len = values.shape
    tables = (sine_table(depth_len), sine_table(row_len), sine_table(column_len))
    spectrum = (
        eigen_line(depth_len)[:, None, None]
        + eigen_line(row_len)[None, :, None]
        + eigen_line(column_len)[None, None, :]
    )
    inverse = 1.0 / (mass_term + bend_mean * spectrum * spectrum + split_term * spectrum)
    return transform(transform(values, tables) * inverse, tables)


def crop(values, margin):
    if margin == 0:
        return values
    return values[margin:-margin, margin:-margin, margin:-margin]


def laplace(values):
    centre = values[1:-1, 1:-1, 1:-1]
    beside = values[2:, 1:-1, 1:-1] + values[:-2, 1:-1, 1:-1]
    beside = beside + values[1:-1, 2:, 1:-1] + values[1:-1, :-2, 1:-1]
    beside = beside + values[1:-1, 1:-1, 2:] + values[1:-1, 1:-1, :-2]
    return 6.0 * centre - beside


def operate(values, value_margin, stiffness, stiff_margin):
    out_margin = value_margin - 2
    flux = laplace(values)
    weighted = crop(stiffness, stiff_margin - out_margin - 1) * flux
    return mass_term * crop(values, 2) + laplace(weighted) + split_term * crop(flux, 1)


def fold(wide, margin):
    rim = OV + margin
    for axis, dim in (("gz", 0), ("gy", 1), ("gx", 2)):
        extent = wide.shape[dim]
        low = shifted(lax.slice_in_dim(wide, extent - rim, extent, axis=dim), axis, 1)
        high = shifted(lax.slice_in_dim(wide, 0, rim, axis=dim), axis, -1)
        length = extent - 2 * OV + 2 * margin
        pads = [(0, 0, 0)] * 3
        grow = margin - OV

        def padded(values, before, after):
            pads[dim] = (before, after, 0)
            return lax.pad(values, jnp.float32(0), pads)

        wide = (
            padded(wide, grow, grow)
            + padded(low, 0, length - rim)
            + padded(high, length - rim, 0)
        )
    return wide


def total(values):
    gz, gy, gx = lax.axis_size("gz"), lax.axis_size("gy"), lax.axis_size("gx")
    for axis, count in (("gx", gx), ("gy", gy), ("gz", gz)):
        hop = 1
        while hop < count:
            values = values + lax.ppermute(values, axis, [(i, i ^ hop) for i in range(count)])
            hop *= 2
    return values


def weights(sums):
    b = sums[:ITERS]
    pair = {}
    at = ITERS
    for i in range(ITERS):
        for j in range(i, ITERS):
            pair[i, j] = pair[j, i] = sums[at]
            at += 1
    sigma = [jnp.float32(0)] * ITERS
    delta = None
    current = None
    for turn in range(ITERS):
        zeta = [jnp.float32(1)] + [-s for s in sigma[:turn]]
        following = sum(z * b[i] for i, z in enumerate(zeta))
        for i, z in enumerate(zeta):
            for j in range(turn):
                following = following - z * sigma[j] * pair[i, j]
        if turn == 0:
            delta = zeta
        else:
            ratio = following / current
            delta = [z + ratio * d for z, d in zip(zeta, delta + [jnp.float32(0)])]
        current = following
        bending = sum(
            delta[i] * delta[j] * pair[i, j] for i in range(turn + 1) for j in range(turn + 1)
        )
        step = current / bending
        sigma = [
            s + step * d for s, d in zip(sigma, delta + [jnp.float32(0)] * (ITERS - turn - 1))
        ]
    return sigma


def per_device(rhs_field, stiffness):
    sides = (("gx", 2), ("gy", 1), ("gz", 0))
    wide = extended(rhs_field, sides, OV)
    stiff_wide = extended(stiffness, sides, OV + 1)
    smooth, image = [], []
    for turn in range(ITERS):
        margin = OV + 2 if turn + 1 < ITERS else 2
        values = fold(local_solve(wide), margin)
        wide = operate(values, margin, stiff_wide, OV + 1)
        smooth.append(crop(values, margin))
        image.append(crop(wide, margin - 2))
    dots = [jnp.sum(rhs_field * u) for u in smooth]
    for i in range(ITERS):
        for j in range(i, ITERS):
            dots.append(jnp.sum(smooth[i] * image[j]))
    sums = total(jnp.stack(dots))
    sigma = weights([sums[i] for i in range(len(dots))])
    solution = sum(s * u for s, u in zip(sigma, smooth))
    residual = rhs_field - sum(s * w for s, w in zip(sigma, image))
    return (solution, residual)


def solution(mesh):
    in_specs = (P("gz", "gy", "gx"), P("gz", "gy", "gx"))
    out_specs = (P("gz", "gy", "gx"), P("gz", "gy", "gx"))
    return jax.shard_map(
        per_device, mesh=mesh, in_specs=in_specs, out_specs=out_specs, check_vma=False
    )
```

```python
import functools

import jax
import jax.numpy as jnp
import numpy as np
from jax import lax
from jax.experimental import pallas as pl
from jax.experimental.pallas import tpu as pltpu
from jax.sharding import PartitionSpec as P

OV = 4
ITERS = 3
CZ, CY, CX = 48, 32, 128
EZ, EY, EX = CZ + 2 * OV, CY + 2 * OV, CX + 2 * OV
HALF = EZ // 2
MARGIN = OV + 2
RIM = OV + MARGIN
UZ, UY, UX = CZ + 2 * MARGIN, 48, 256
X_GROUP = 12
Y_PLANES = UZ + UZ // 4 + 5
X_PLANES = UZ // X_GROUP * 6

mass_term = 1e-05
split_term = 0.5
bend_mean = 0.1
f32, bf16 = jnp.float32, jnp.bfloat16


def sine_table(length):
    places = np.arange(1, length + 1, dtype=np.float64)
    return np.sqrt(2.0 / (length + 1)) * np.sin(
        np.pi * places[:, None] * places[None, :] / (length + 1)
    )


def eigen_line(length):
    places = np.arange(1, length + 1, dtype=np.float64)
    return 2.0 - 2.0 * np.cos(np.pi * places / (length + 1))


def halves(table):
    high = np.asarray(table, np.float32).astype(jnp.bfloat16)
    low = (np.asarray(table, np.float64) - high.astype(np.float64)).astype(jnp.bfloat16)
    return [jnp.asarray(high), jnp.asarray(low)]


def solve_tables():
    column = np.zeros((UX, UX))
    full = sine_table(EX)
    for lane in range(UX):
        place = lane + OV if lane < CX + OV else lane - UX + OV
        if 0 <= place < EX:
            column[lane, :EX] = full[place]
    rows = np.roll(sine_table(EY), -OV, axis=0)
    row_fwd = np.kron(np.eye(4), rows.T)
    depth = sine_table(EZ)
    even = np.kron(depth[0::2, :HALF], np.eye(8))
    odd = np.kron(depth[1::2, :HALF], np.eye(8))
    order = np.concatenate([np.arange(0, EZ, 2), np.arange(1, EZ, 2)])
    spectrum = (
        eigen_line(EZ)[order][:, None, None]
        + eigen_line(EY)[None, :, None]
        + eigen_line(EX)[None, None, :]
    )
    inverse = np.zeros((EZ, EY, UX), np.float32)
    inverse[:, :, :EX] = 1.0 / (mass_term + bend_mean * spectrum**2 + split_term * spectrum)
    tables = []
    for table in (column, column.T, row_fwd, row_fwd.T, even, odd, even.T, odd.T):
        tables += halves(table)
    return tables + [jnp.asarray(inverse)]


def cut(values):
    high = values.astype(bf16)
    return high, (values - high.astype(f32)).astype(bf16)


def mul(a, b):
    return lax.dot_general(a, b, (((1,), (0,)), ((), ())), preferred_element_type=f32)


def mul3(a, b):
    return mul(a[0], b[0]) + (mul(a[0], b[1]) + mul(a[1], b[0]))


def lanes():
    return lax.broadcasted_iota(jnp.int32, (8, 128), 1)


def subs():
    return lax.broadcasted_iota(jnp.int32, (8, 128), 0)


def spin(values, shift, axis):
    size = values.shape[axis]
    shift = shift % size
    return values if shift == 0 else pltpu.roll(values, shift, axis)


def pack(into, values, lead, width, at):
    lane = lax.broadcasted_iota(jnp.int32, values.shape, 1)
    inside = (lane >= width * at) & (lane < width * (at + 1))
    moved = spin(values, lead + width * at, 1)
    return jnp.where(inside, moved, 0.0 if into is None else into)


def unpack(packed, lead, width, at):
    moved = spin(packed, -(lead + width * at), 1)
    lane = lax.broadcasted_iota(jnp.int32, packed.shape, 1)
    return jnp.where((lane >= 128 - lead) | (lane < width - lead), moved, 0.0)


def solve_kernel(
    wide, cfh, cfl, cih, cil, rfh, rfl, rih, ril, eh, el, oh, ol, eth, etl, oth, otl, inverse,
    solved, low, high,
):
    def forward(group, carry):
        at = pl.multiple_of(group * 4, 4)
        values = cut(wide[pl.ds(at, 4)].reshape(4 * EY, UX))
        values = cut(mul3(values, (cfh[...], cfl[...])))
        solved[pl.ds(at, 4)] = mul3((rfh[...], rfl[...]), values).reshape(4, EY, UX)
        return carry

    lax.fori_loop(0, EZ // 4, forward, 0)

    for tile in range(EY // 8):
        rows = slice(8 * tile, 8 * tile + 8)
        near = solved[:HALF, rows, :]
        far = jnp.concatenate([solved[EZ - 1 - i : EZ - i, rows, :] for i in range(HALF)], axis=0)
        even = cut((near + far).reshape(8 * HALF, UX))
        odd = cut((near - far).reshape(8 * HALF, UX))
        even = mul3((eh[...], el[...]), even) * inverse[:HALF, rows, :].reshape(8 * HALF, UX)
        odd = mul3((oh[...], ol[...]), odd) * inverse[HALF:, rows, :].reshape(8 * HALF, UX)
        even = mul3((eth[...], etl[...]), cut(even)).reshape(HALF, 8, UX)
        odd = mul3((oth[...], otl[...]), cut(odd)).reshape(HALF, 8, UX)
        solved[:HALF, rows, :] = even + odd
        far = even - odd
        for i in range(HALF):
            solved[EZ - 1 - i, rows, :] = far[i]

    def backward(group, carry):
        at = pl.multiple_of(group * 4, 4)
        values = cut(solved[pl.ds(at, 4)].reshape(4 * EY, UX))
        values = cut(mul3((rih[...], ril[...]), values))
        solved[pl.ds(at, 4)] = mul3(values, (cih[...], cil[...])).reshape(4, EY, UX)
        return carry

    lax.fori_loop(0, EZ // 4, backward, 0)

    for strip, start in ((low, 0), (high, EZ - RIM)):
        extra = None
        for i in range(RIM):
            strip[i] = solved[start + i, :, :CX]
            extra = pack(extra, solved[start + i, :, CX:], OV, 2 * OV, i)
        strip[RIM] = extra


def depth_folded(solved, from_below, from_above, z, tile, side):
    rows = slice(8 * tile, 8 * tile + 8)
    parts = []
    if 2 <= z < UZ - 2:
        parts.append(solved[z - 2, rows, 128 * side : 128 * side + 128])
    for strip, at in ((from_below, z), (from_above, z - UZ + RIM)):
        if 0 <= at < RIM:
            if side == 0:
                parts.append(strip[at, rows, :])
            else:
                parts.append(unpack(strip[RIM, rows, :], OV, 2 * OV, at))
    return sum(parts[1:], parts[0])


def row_strips_kernel(solved, from_below, from_above, low, high):
    sub = subs()
    fold = functools.partial(depth_folded, solved, from_below, from_above)
    for strip, cut_at, upper, lower, keep in ((low, 4, 4, 0, 4), (high, 2, 3, 4, 2)):
        extra_b = None
        for quad in range(UZ // 4):
            rest = [None, None]
            for j in range(4):
                z = 4 * quad + j
                for side in range(2):
                    lower_tile = fold(z, lower, side)
                    main = jnp.where(sub >= cut_at, fold(z, upper, side), lower_tile)
                    if side == 0:
                        strip[z] = main
                    else:
                        place = UZ + UZ // 4 + z // 16
                        so_far = None if z % 16 == 0 else strip[place]
                        strip[place] = pack(so_far, main, OV, 2 * OV, z % 16)
                    moved = spin(lower_tile, 2 * j - keep, 0)
                    inside = (sub >= 2 * j) & (sub < 2 * j + 2)
                    rest[side] = jnp.where(
                        inside, moved, 0.0 if rest[side] is None else rest[side]
                    )
            strip[UZ + quad] = rest[0]
            extra_b = pack(extra_b, rest[1], OV, 2 * OV, quad)
        strip[Y_PLANES - 1] = extra_b


def row_part(strip, z, side, keep):
    sub = subs()
    if side == 0:
        main, rest = strip[z], strip[UZ + z // 4]
    else:
        main = unpack(strip[UZ + UZ // 4 + z // 16], OV, 2 * OV, z % 16)
        rest = unpack(strip[Y_PLANES - 1], OV, 2 * OV, z // 4)
    moved = spin(rest, keep - 2 * (z % 4), 0)
    return main, jnp.where((sub >= keep) & (sub < keep + 2), moved, 0.0)


def column_strips_kernel(solved, from_below, from_above, from_near, from_far, folded, low, high):
    sub, lane = subs(), lanes()
    fold = functools.partial(depth_folded, solved, from_below, from_above)
    for group in range(UZ // X_GROUP):
        for tile in range(6):
            packed = [None, None]
            for j in range(X_GROUP):
                z = group * X_GROUP + j
                sides = []
                for side in range(2):
                    value = fold(z, min(tile, 4), side)
                    if tile == 4:
                        value = jnp.where(sub < 4, value, 0.0)
                    if tile == 5:
                        value = jnp.where(sub >= 4, value, 0.0)
                    if tile in (0, 5):
                        main, rest = row_part(from_near, z, side, 2)
                        if tile == 0:
                            value = value + jnp.where(sub < 2, main, rest)
                        else:
                            value = value + jnp.where(sub >= 2, main, 0.0)
                    if tile in (3, 4):
                        main, rest = row_part(from_far, z, side, 4)
                        if tile == 3:
                            value = value + jnp.where(sub >= 4, main, 0.0)
                        else:
                            value = value + jnp.where(sub < 4, main, rest)
                    folded[z, 8 * tile : 8 * tile + 8, 128 * side : 128 * side + 128] = value
                    sides.append(value)
                packed[0] = pack(
                    packed[0], jnp.where(lane >= 124, sides[1], sides[0]), OV, RIM, j
                )
                packed[1] = pack(
                    packed[1], jnp.where(lane >= 122, sides[0], sides[1]), MARGIN, RIM, j
                )
            low[6 * group + tile] = packed[0]
            high[6 * group + tile] = packed[1]


def laplace(below, centre, above):
    beside = below + above
    beside = beside + (pltpu.roll(centre, 1, 0) + pltpu.roll(centre, UY - 1, 0))
    beside = beside + (pltpu.roll(centre, 1, 1) + pltpu.roll(centre, UX - 1, 1))
    return 6.0 * centre - beside


def apply_kernel(count, *refs):
    folded, from_left, from_right, stiffness, rhs = refs[:5]
    earlier = refs[5 : 5 + count]
    wide, smooth, image, sums = refs[5 + count : 9 + count]
    full, flux, weighted = refs[9 + count :]
    lane = lanes()
    for group in range(UZ // X_GROUP):
        for tile in range(6):
            rows = slice(8 * tile, 8 * tile + 8)
            left, right = from_left[6 * group + tile], from_right[6 * group + tile]
            for j in range(X_GROUP):
                z = group * X_GROUP + j
                left_part = unpack(left, MARGIN, RIM, j)
                right_part = unpack(right, OV, RIM, j)
                full[z, rows, :CX] = folded[z, rows, :CX] + jnp.where(
                    lane < 64, left_part, right_part
                )
                full[z, rows, CX:] = folded[z, rows, CX:] + jnp.where(
                    lane < 64, right_part, left_part
                )

    def first(z, carry):
        values = laplace(full[z - 1], full[z], full[z + 1])
        flux[z] = values
        weighted[z] = stiffness[z] * values
        return carry

    lax.fori_loop(1, UZ - 1, first, 0)
    sub = lax.broadcasted_iota(jnp.int32, (8, UX), 0)

    def second(z):
        values = laplace(weighted[z - 1], weighted[z], weighted[z + 1])
        values = mass_term * full[z] + values + split_term * flux[z]
        wide[z - 2, :CY, :] = values[:CY]
        wide[z - 2, CY:, :] = jnp.where(sub < 4, values[CY : CY + 8], values[CY + 8 :])
        return values

    def outer(z, carry):
        second(z)
        second(z + CZ + OV)
        return carry

    def add(total, product):
        return total + (product[0:8] + product[8:16]) + (product[16:24] + product[24:32])

    def inner(z, totals):
        core = second(z)[:CY, :CX]
        own = full[z, :CY, :CX]
        smooth[z - MARGIN] = own
        image[z - MARGIN] = core
        new = [add(totals[0], own * rhs[z - MARGIN])]
        for i in range(count):
            new.append(add(totals[1 + i], core * earlier[i][z - MARGIN]))
        new.append(add(totals[1 + count], core * own))
        return tuple(new)

    lax.fori_loop(2, MARGIN, outer, 0)
    zero = jnp.zeros((8, 128), f32)
    totals = lax.fori_loop(MARGIN, MARGIN + CZ, inner, (zero,) * (count + 2))
    for i, value in enumerate(totals):
        sums[i] = value


def combine_kernel(sigma, rhs, u0, u1, u2, w0, w1, w2, answer, rest):
    s = [sigma[i] for i in range(ITERS)]

    def step(z, carry):
        answer[z] = s[0] * u0[z] + s[1] * u1[z] + s[2] * u2[z]
        rest[z] = rhs[z] - (s[0] * w0[z] + s[1] * w1[z] + s[2] * w2[z])
        return carry

    lax.fori_loop(0, CZ, step, 0)


VMEM = pl.BlockSpec(memory_space=pltpu.VMEM)
SMEM = pl.BlockSpec(memory_space=pltpu.SMEM)


def call(kernel, shapes, operands, scratch=(), specs=None):
    return pl.pallas_call(
        kernel,
        out_shape=[jax.ShapeDtypeStruct(shape, f32) for shape in shapes],
        in_specs=specs or [VMEM] * len(operands),
        out_specs=[VMEM] * len(shapes),
        scratch_shapes=[pltpu.VMEM(shape, f32) for shape in scratch],
        compiler_params=pltpu.CompilerParams(vmem_limit_bytes=32 * 2**20),
    )(*operands)


def shifted(block, axis, step):
    count = lax.axis_size(axis)
    return lax.ppermute(block, axis, [(i, (i + step) % count) for i in range(count)])


def swap(low, high, axis):
    return shifted(high, axis, 1), shifted(low, axis, -1)


def extended(block, sides, width):
    for axis, dim in sides:
        low, high = swap(
            lax.slice_in_dim(block, 0, width, axis=dim),
            lax.slice_in_dim(block, block.shape[dim] - width, None, axis=dim),
            axis,
        )
        block = jnp.concatenate([low, block, high], axis=dim)
    return block


def wrapped(block, width, sizes):
    for dim, size in sizes:
        extent = block.shape[dim]
        shape = list(block.shape)
        shape[dim] = size - extent
        block = jnp.concatenate(
            [
                lax.slice_in_dim(block, width, extent, axis=dim),
                jnp.zeros(shape, f32),
                lax.slice_in_dim(block, 0, width, axis=dim),
            ],
            axis=dim,
        )
    return block


def total(values):
    for axis in ("gx", "gy", "gz"):
        count = lax.axis_size(axis)
        hop = 1
        while hop < count:
            values = values + lax.ppermute(values, axis, [(i, i ^ hop) for i in range(count)])
            hop *= 2
    return values


def weights(b, pair):
    sigma = [f32(0)] * ITERS
    delta = None
    current = None
    for turn in range(ITERS):
        zeta = [f32(1)] + [-s for s in sigma[:turn]]
        following = sum(z * b[i] for i, z in enumerate(zeta))
        for i, z in enumerate(zeta):
            for j in range(turn):
                following = following - z * sigma[j] * pair[i, j]
        if turn == 0:
            delta = zeta
        else:
            ratio = following / current
            delta = [z + ratio * d for z, d in zip(zeta, delta + [f32(0)])]
        current = following
        bending = sum(
            delta[i] * delta[j] * pair[i, j] for i in range(turn + 1) for j in range(turn + 1)
        )
        step = current / bending
        sigma = [
            s + step * d for s, d in zip(sigma, delta + [f32(0)] * (ITERS - turn - 1))
        ]
    return jnp.stack(sigma)


def per_device(rhs_field, stiffness):
    sides = (("gx", 2), ("gy", 1), ("gz", 0))
    wide = wrapped(extended(rhs_field, sides, OV), OV, ((1, EY), (2, UX)))
    stiff = wrapped(extended(stiffness, sides, OV + 1), OV + 1, ((1, UY), (2, UX)))
    stiff = jnp.pad(stiff, ((1, 1), (0, 0), (0, 0)))
    tables = solve_tables()
    smooth, image, sums = [], [], []
    for turn in range(ITERS):
        solved, low, high = call(
            solve_kernel,
            [(EZ, EY, UX), (RIM + 1, EY, CX), (RIM + 1, EY, CX)],
            [wide] + tables,
        )
        depth_strips = swap(low, high, "gz")
        low, high = call(
            row_strips_kernel, [(Y_PLANES, 8, 128)] * 2, [solved, *depth_strips]
        )
        row_strips = swap(low, high, "gy")
        folded, low, high = call(
            column_strips_kernel,
            [(UZ, UY, UX)] + [(X_PLANES, 8, 128)] * 2,
            [solved, *depth_strips, *row_strips],
        )
        column_strips = swap(low, high, "gx")
        wide, own, core, part = call(
            functools.partial(apply_kernel, turn),
            [(EZ, EY, UX), (CZ, CY, CX), (CZ, CY, CX), (turn + 2, 8, 128)],
            [folded, *column_strips, stiff, rhs_field, *smooth],
            [(UZ, UY, UX)] * 3,
        )
        smooth.append(own)
        image.append(core)
        sums.append(part)
    sums = total(jnp.sum(jnp.concatenate(sums, axis=0), axis=(1, 2)))
    b, pair, at = [], {}, 0
    for j in range(ITERS):
        b.append(sums[at])
        for i in range(j + 1):
            pair[i, j] = pair[j, i] = sums[at + 1 + i]
        at += j + 2
    sigma = weights(b, pair)
    return tuple(
        call(
            combine_kernel,
            [(CZ, CY, CX)] * 2,
            [sigma, rhs_field, *smooth, *image],
            specs=[SMEM] + [VMEM] * 7,
        )
    )


def solution(mesh):
    in_specs = (P("gz", "gy", "gx"), P("gz", "gy", "gx"))
    out_specs = (P("gz", "gy", "gx"), P("gz", "gy", "gx"))
    return jax.shard_map(
        per_device, mesh=mesh, in_specs=in_specs, out_specs=out_specs, check_vma=False
    )
```

```python
import functools

import jax
import jax.numpy as jnp
import numpy as np
from jax import lax
from jax.experimental import pallas as pl
from jax.experimental.pallas import tpu as pltpu
from jax.sharding import PartitionSpec as P

OV = 4
ITERS = 3
CZ, CY, CX = 48, 32, 128
EZ, EY, EX = CZ + 2 * OV, CY + 2 * OV, CX + 2 * OV
HALF = EZ // 2
MARGIN = OV + 2
RIM = OV + MARGIN
UZ, UY, UX = CZ + 2 * MARGIN, 48, 256
X_GROUP = 12
Y_PLANES = UZ + UZ // 4 + 5
X_PLANES = UZ // X_GROUP * 6

mass_term = 1e-05
split_term = 0.5
bend_mean = 0.1
f32, bf16 = jnp.float32, jnp.bfloat16


def sine_table(length):
    places = np.arange(1, length + 1, dtype=np.float64)
    return np.sqrt(2.0 / (length + 1)) * np.sin(
        np.pi * places[:, None] * places[None, :] / (length + 1)
    )


def eigen_line(length):
    places = np.arange(1, length + 1, dtype=np.float64)
    return 2.0 - 2.0 * np.cos(np.pi * places / (length + 1))


def halves(table):
    high = np.asarray(table, np.float32).astype(jnp.bfloat16)
    low = (np.asarray(table, np.float64) - high.astype(np.float64)).astype(jnp.bfloat16)
    return [jnp.asarray(high), jnp.asarray(low)]


def solve_tables():
    column = np.zeros((UX, UX))
    full = sine_table(EX)
    for lane in range(UX):
        place = lane + OV if lane < CX + OV else lane - UX + OV
        if 0 <= place < EX:
            column[lane, :EX] = full[place]
    rows = np.roll(sine_table(EY), -OV, axis=0)
    row_fwd = np.kron(np.eye(4), rows.T)
    depth = sine_table(EZ)
    even = np.kron(depth[0::2, :HALF], np.eye(8))
    odd = np.kron(depth[1::2, :HALF], np.eye(8))
    order = np.concatenate([np.arange(0, EZ, 2), np.arange(1, EZ, 2)])
    spectrum = (
        eigen_line(EZ)[order][:, None, None]
        + eigen_line(EY)[None, :, None]
        + eigen_line(EX)[None, None, :]
    )
    inverse = np.zeros((EZ, EY, UX), np.float32)
    inverse[:, :, :EX] = 1.0 / (mass_term + bend_mean * spectrum**2 + split_term * spectrum)
    tables = []
    for table in (column, column.T, row_fwd, row_fwd.T, even, odd, even.T, odd.T):
        tables += halves(table)
    return tables + [jnp.asarray(inverse)]


def cut(values):
    high = values.astype(bf16)
    return high, (values - high.astype(f32)).astype(bf16)


def mul(a, b):
    return lax.dot_general(a, b, (((1,), (0,)), ((), ())), preferred_element_type=f32)


def mul3(a, b):
    return mul(a[0], b[0]) + (mul(a[0], b[1]) + mul(a[1], b[0]))


def lanes():
    return lax.broadcasted_iota(jnp.int32, (8, 128), 1)


def subs():
    return lax.broadcasted_iota(jnp.int32, (8, 128), 0)


def spin(values, shift, axis):
    size = values.shape[axis]
    shift = shift % size
    return values if shift == 0 else pltpu.roll(values, shift, axis)


def pack(into, values, lead, width, at):
    lane = lax.broadcasted_iota(jnp.int32, values.shape, 1)
    inside = (lane >= width * at) & (lane < width * (at + 1))
    moved = spin(values, lead + width * at, 1)
    return jnp.where(inside, moved, 0.0 if into is None else into)


def unpack(packed, lead, width, at):
    moved = spin(packed, -(lead + width * at), 1)
    lane = lax.broadcasted_iota(jnp.int32, packed.shape, 1)
    return jnp.where((lane >= 128 - lead) | (lane < width - lead), moved, 0.0)


def solve_kernel(
    wide, cfh, cfl, cih, cil, rfh, rfl, rih, ril, eh, el, oh, ol, eth, etl, oth, otl, inverse,
    solved, low, high,
):
    def forward(group, carry):
        at = pl.multiple_of(group * 4, 4)
        values = cut(wide[pl.ds(at, 4)].reshape(4 * EY, UX))
        values = cut(mul3(values, (cfh[...], cfl[...])))
        solved[pl.ds(at, 4)] = mul3((rfh[...], rfl[...]), values).reshape(4, EY, UX)
        return carry

    lax.fori_loop(0, EZ // 4, forward, 0, unroll=True)

    for tile in range(EY // 8):
        rows = slice(8 * tile, 8 * tile + 8)
        near = solved[:HALF, rows, :]
        far = jnp.concatenate([solved[EZ - 1 - i : EZ - i, rows, :] for i in range(HALF)], axis=0)
        even = cut((near + far).reshape(8 * HALF, UX))
        odd = cut((near - far).reshape(8 * HALF, UX))
        even = mul3((eh[...], el[...]), even) * inverse[:HALF, rows, :].reshape(8 * HALF, UX)
        odd = mul3((oh[...], ol[...]), odd) * inverse[HALF:, rows, :].reshape(8 * HALF, UX)
        even = mul3((eth[...], etl[...]), cut(even)).reshape(HALF, 8, UX)
        odd = mul3((oth[...], otl[...]), cut(odd)).reshape(HALF, 8, UX)
        solved[:HALF, rows, :] = even + odd
        far = even - odd
        for i in range(HALF):
            solved[EZ - 1 - i, rows, :] = far[i]

    def backward(group, carry):
        at = pl.multiple_of(group * 4, 4)
        values = cut(solved[pl.ds(at, 4)].reshape(4 * EY, UX))
        values = cut(mul3((rih[...], ril[...]), values))
        solved[pl.ds(at, 4)] = mul3(values, (cih[...], cil[...])).reshape(4, EY, UX)
        return carry

    lax.fori_loop(0, EZ // 4, backward, 0, unroll=True)

    for strip, start in ((low, 0), (high, EZ - RIM)):
        extra = None
        for i in range(RIM):
            strip[i] = solved[start + i, :, :CX]
            extra = pack(extra, solved[start + i, :, CX:], OV, 2 * OV, i)
        strip[RIM] = extra


def depth_folded(solved, from_below, from_above, z, tile, side):
    rows = slice(8 * tile, 8 * tile + 8)
    parts = []
    if 2 <= z < UZ - 2:
        parts.append(solved[z - 2, rows, 128 * side : 128 * side + 128])
    for strip, at in ((from_below, z), (from_above, z - UZ + RIM)):
        if 0 <= at < RIM:
            if side == 0:
                parts.append(strip[at, rows, :])
            else:
                parts.append(unpack(strip[RIM, rows, :], OV, 2 * OV, at))
    return sum(parts[1:], parts[0])


def row_strips_kernel(solved, from_below, from_above, low, high):
    sub = subs()
    fold = functools.partial(depth_folded, solved, from_below, from_above)
    for strip, cut_at, upper, lower, keep in ((low, 4, 4, 0, 4), (high, 2, 3, 4, 2)):
        extra_b = None
        for quad in range(UZ // 4):
            rest = [None, None]
            for j in range(4):
                z = 4 * quad + j
                for side in range(2):
                    lower_tile = fold(z, lower, side)
                    main = jnp.where(sub >= cut_at, fold(z, upper, side), lower_tile)
                    if side == 0:
                        strip[z] = main
                    else:
                        place = UZ + UZ // 4 + z // 16
                        so_far = None if z % 16 == 0 else strip[place]
                        strip[place] = pack(so_far, main, OV, 2 * OV, z % 16)
                    moved = spin(lower_tile, 2 * j - keep, 0)
                    inside = (sub >= 2 * j) & (sub < 2 * j + 2)
                    rest[side] = jnp.where(
                        inside, moved, 0.0 if rest[side] is None else rest[side]
                    )
            strip[UZ + quad] = rest[0]
            extra_b = pack(extra_b, rest[1], OV, 2 * OV, quad)
        strip[Y_PLANES - 1] = extra_b


def row_part(strip, z, side, keep):
    sub = subs()
    if side == 0:
        main, rest = strip[z], strip[UZ + z // 4]
    else:
        main = unpack(strip[UZ + UZ // 4 + z // 16], OV, 2 * OV, z % 16)
        rest = unpack(strip[Y_PLANES - 1], OV, 2 * OV, z // 4)
    moved = spin(rest, keep - 2 * (z % 4), 0)
    return main, jnp.where((sub >= keep) & (sub < keep + 2), moved, 0.0)


def column_strips_kernel(solved, from_below, from_above, from_near, from_far, folded, low, high):
    sub, lane = subs(), lanes()
    fold = functools.partial(depth_folded, solved, from_below, from_above)
    for z in range(UZ):
        for tile in range(6):
            for side in range(2):
                value = fold(z, min(tile, 4), side)
                if tile == 4:
                    value = jnp.where(sub < 4, value, 0.0)
                if tile == 5:
                    value = jnp.where(sub >= 4, value, 0.0)
                if tile in (0, 5):
                    main, rest = row_part(from_near, z, side, 2)
                    if tile == 0:
                        value = value + jnp.where(sub < 2, main, rest)
                    else:
                        value = value + jnp.where(sub >= 2, main, 0.0)
                if tile in (3, 4):
                    main, rest = row_part(from_far, z, side, 4)
                    if tile == 3:
                        value = value + jnp.where(sub >= 4, main, 0.0)
                    else:
                        value = value + jnp.where(sub < 4, main, rest)
                folded[z, 8 * tile : 8 * tile + 8, 128 * side : 128 * side + 128] = value

    def packing(group, carry):
        for tile in range(6):
            rows = slice(8 * tile, 8 * tile + 8)
            packed = [None, None]
            for j in range(X_GROUP):
                z = group * X_GROUP + j
                near, far = folded[z, rows, :CX], folded[z, rows, CX:]
                packed[0] = pack(packed[0], jnp.where(lane >= 124, far, near), OV, RIM, j)
                packed[1] = pack(packed[1], jnp.where(lane >= 122, near, far), MARGIN, RIM, j)
            low[6 * group + tile] = packed[0]
            high[6 * group + tile] = packed[1]
        return carry

    lax.fori_loop(0, UZ // X_GROUP, packing, 0)


def laplace(below, centre, above):
    beside = below + above
    beside = beside + (pltpu.roll(centre, 1, 0) + pltpu.roll(centre, UY - 1, 0))
    beside = beside + (pltpu.roll(centre, 1, 1) + pltpu.roll(centre, UX - 1, 1))
    return 6.0 * centre - beside


def apply_kernel(count, *refs):
    folded, from_left, from_right, stiffness, rhs = refs[:5]
    earlier, parts = refs[5 : 5 + count], refs[5 + count : 5 + 2 * count]
    wide, smooth, image, sums, full, flux, weighted = refs[5 + 2 * count :]
    lane = lanes()
    for group in range(UZ // X_GROUP):
        for tile in range(6):
            rows = slice(8 * tile, 8 * tile + 8)
            left, right = from_left[6 * group + tile], from_right[6 * group + tile]
            for j in range(X_GROUP):
                z = group * X_GROUP + j
                left_part = unpack(left, MARGIN, RIM, j)
                right_part = unpack(right, OV, RIM, j)
                full[z, rows, :CX] = folded[z, rows, :CX] + jnp.where(
                    lane < 64, left_part, right_part
                )
                full[z, rows, CX:] = folded[z, rows, CX:] + jnp.where(
                    lane < 64, right_part, left_part
                )

    def first(z, carry):
        values = laplace(full[z - 1], full[z], full[z + 1])
        flux[z] = values
        weighted[z] = stiffness[z] * values
        return carry

    lax.fori_loop(1, UZ - 1, first, 0, unroll=4)
    sub = lax.broadcasted_iota(jnp.int32, (8, UX), 0)

    def second(z):
        values = laplace(weighted[z - 1], weighted[z], weighted[z + 1])
        values = mass_term * full[z] + values + split_term * flux[z]
        wide[z - 2, :CY, :] = values[:CY]
        wide[z - 2, CY:, :] = jnp.where(sub < 4, values[CY : CY + 8], values[CY + 8 :])
        return values

    def outer(z, carry):
        second(z)
        second(z + CZ + OV)
        return carry

    def add(total, product):
        return total + (product[0:8] + product[8:16]) + (product[16:24] + product[24:32])

    def inner(z, totals):
        core = second(z)[:CY, :CX]
        own = full[z, :CY, :CX]
        smooth[z - MARGIN] = own
        image[z - MARGIN] = core
        new = [add(totals[0], own * rhs[z - MARGIN])]
        for i in range(count):
            new.append(add(totals[1 + i], core * earlier[i][z - MARGIN]))
        new.append(add(totals[1 + count], core * own))
        return tuple(new)

    lax.fori_loop(2, MARGIN, outer, 0, unroll=2)
    zero = jnp.zeros((8, 128), f32)
    totals = lax.fori_loop(MARGIN, MARGIN + CZ, inner, (zero,) * (count + 2), unroll=4)
    if count + 1 < ITERS:
        for i, value in enumerate(totals):
            sums[i] = value
        return
    values = [part[i] for part in parts for i in range(part.shape[0])] + list(totals)
    gathered = zero
    for i, value in enumerate(values):
        value = jnp.sum(jnp.sum(value, axis=0, keepdims=True), axis=1, keepdims=True)
        gathered = jnp.where(lane == i, value, gathered)
    sums[...] = gathered


def weights(b, pair):
    sigma = [jnp.zeros((1, 1), f32)] * ITERS
    delta = None
    current = None
    for turn in range(ITERS):
        zeta = [jnp.ones((1, 1), f32)] + [-s for s in sigma[:turn]]
        following = sum(z * b[i] for i, z in enumerate(zeta))
        for i, z in enumerate(zeta):
            for j in range(turn):
                following = following - z * sigma[j] * pair[i, j]
        if turn == 0:
            delta = zeta
        else:
            ratio = following / current
            delta = [z + ratio * d for z, d in zip(zeta, delta + [jnp.zeros((1, 1), f32)])]
        current = following
        bending = sum(
            delta[i] * delta[j] * pair[i, j] for i in range(turn + 1) for j in range(turn + 1)
        )
        step = current / bending
        sigma = [
            s + step * d for s, d in zip(sigma, delta + [jnp.zeros((1, 1), f32)] * (ITERS - turn - 1))
        ]
    return sigma


def combine_kernel(sums, rhs, u0, u1, u2, w0, w1, w2, answer, rest):
    picked = [
        jnp.sum(jnp.where(lanes()[:1] == i, sums[:1], 0.0), axis=1, keepdims=True)
        for i in range(ITERS * (ITERS + 3) // 2)
    ]
    b, pair, at = [], {}, 0
    for j in range(ITERS):
        b.append(picked[at])
        for i in range(j + 1):
            pair[i, j] = pair[j, i] = picked[at + 1 + i]
        at += j + 2
    s = weights(b, pair)

    def step(z, carry):
        answer[z] = s[0] * u0[z] + s[1] * u1[z] + s[2] * u2[z]
        rest[z] = rhs[z] - (s[0] * w0[z] + s[1] * w1[z] + s[2] * w2[z])
        return carry

    lax.fori_loop(0, CZ, step, 0, unroll=4)


VMEM = pl.BlockSpec(memory_space=pltpu.VMEM)


def call(kernel, shapes, operands, scratch=()):
    return pl.pallas_call(
        kernel,
        out_shape=[jax.ShapeDtypeStruct(shape, f32) for shape in shapes],
        in_specs=[VMEM] * len(operands),
        out_specs=[VMEM] * len(shapes),
        scratch_shapes=[pltpu.VMEM(shape, f32) for shape in scratch],
        compiler_params=pltpu.CompilerParams(vmem_limit_bytes=16 * 2**20),
    )(*operands)


def shifted(block, axis, step):
    count = lax.axis_size(axis)
    return lax.ppermute(block, axis, [(i, (i + step) % count) for i in range(count)])


def swap(low, high, axis):
    return shifted(high, axis, 1), shifted(low, axis, -1)


def extended(block, sides, width):
    for axis, dim in sides:
        low, high = swap(
            lax.slice_in_dim(block, 0, width, axis=dim),
            lax.slice_in_dim(block, block.shape[dim] - width, None, axis=dim),
            axis,
        )
        block = jnp.concatenate([low, block, high], axis=dim)
    return block


def wrapped(block, width, sizes):
    for dim, size in sizes:
        extent = block.shape[dim]
        shape = list(block.shape)
        shape[dim] = size - extent
        block = jnp.concatenate(
            [
                lax.slice_in_dim(block, width, extent, axis=dim),
                jnp.zeros(shape, f32),
                lax.slice_in_dim(block, 0, width, axis=dim),
            ],
            axis=dim,
        )
    return block


def total(values):
    for axis in ("gx", "gy", "gz"):
        count = lax.axis_size(axis)
        hop = 1
        while hop < count:
            values = values + lax.ppermute(values, axis, [(i, i ^ hop) for i in range(count)])
            hop *= 2
    return values


def per_device(rhs_field, stiffness):
    sides = (("gx", 2), ("gy", 1), ("gz", 0))
    wide = wrapped(extended(rhs_field, sides, OV), OV, ((1, EY), (2, UX)))
    stiff = wrapped(extended(stiffness, sides, OV + 1), OV + 1, ((1, UY), (2, UX)))
    stiff = jnp.pad(stiff, ((1, 1), (0, 0), (0, 0)))
    tables = solve_tables()
    smooth, image, sums = [], [], []
    for turn in range(ITERS):
        solved, low, high = call(
            solve_kernel,
            [(EZ, EY, UX), (RIM + 1, EY, CX), (RIM + 1, EY, CX)],
            [wide] + tables,
        )
        depth_strips = swap(low, high, "gz")
        low, high = call(
            row_strips_kernel, [(Y_PLANES, 8, 128)] * 2, [solved, *depth_strips]
        )
        row_strips = swap(low, high, "gy")
        folded, low, high = call(
            column_strips_kernel,
            [(UZ, UY, UX)] + [(X_PLANES, 8, 128)] * 2,
            [solved, *depth_strips, *row_strips],
        )
        column_strips = swap(low, high, "gx")
        wide, own, core, part = call(
            functools.partial(apply_kernel, turn),
            [(EZ, EY, UX), (CZ, CY, CX), (CZ, CY, CX)]
            + [(turn + 2, 8, 128) if turn + 1 < ITERS else (8, 128)],
            [folded, *column_strips, stiff, rhs_field, *smooth, *sums],
            [(UZ, UY, UX)] * 3,
        )
        smooth.append(own)
        image.append(core)
        sums.append(part)
    operands = [total(sums[-1]), rhs_field, *smooth, *image]
    return tuple(call(combine_kernel, [(CZ, CY, CX)] * 2, operands))


def solution(mesh):
    in_specs = (P("gz", "gy", "gx"), P("gz", "gy", "gx"))
    out_specs = (P("gz", "gy", "gx"), P("gz", "gy", "gx"))
    return jax.shard_map(
        per_device, mesh=mesh, in_specs=in_specs, out_specs=out_specs, check_vma=False
    )
```

```python
import functools

import jax
import jax.numpy as jnp
import numpy as np
from jax import lax
from jax.experimental import pallas as pl
from jax.experimental.pallas import tpu as pltpu
from jax.sharding import PartitionSpec as P

OV = 4
ITERS = 3
CZ, CY, CX = 48, 32, 128
EZ, EY, EX = CZ + 2 * OV, CY + 2 * OV, CX + 2 * OV
HALF = EZ // 2
UZ, UY, UX = CZ + 12, 48, 256
GROUP = 4
INNER = range(12, 44, GROUP)
OUTER = [z for z in range(0, EZ, GROUP) if z not in INNER]


class Shape:
    def __init__(self, last):
        self.rim = 6 if last else 10
        self.halo = 4 if last else 6
        self.width = 4 + self.halo
        self.per = 128 // self.width
        self.x_tiles = -(-EZ // self.per) * 5
        self.extra_per = 128 // (2 * self.halo)
        self.extra_a = EZ if last else EZ + EZ // 4
        self.extra_b = self.extra_a + -(-EZ // self.extra_per)
        self.y_tiles = self.extra_b + (0 if last else -(-(EZ // 4) // self.extra_per))
        self.last = last


mass_term = 1e-05
split_term = 0.5
bend_mean = 0.1
f32, bf16 = jnp.float32, jnp.bfloat16


def sine_table(length):
    places = np.arange(1, length + 1, dtype=np.float64)
    return np.sqrt(2.0 / (length + 1)) * np.sin(
        np.pi * places[:, None] * places[None, :] / (length + 1)
    )


def eigen_line(length):
    places = np.arange(1, length + 1, dtype=np.float64)
    return 2.0 - 2.0 * np.cos(np.pi * places / (length + 1))


def halves(table):
    high = np.asarray(table, np.float32).astype(jnp.bfloat16)
    low = (np.asarray(table, np.float64) - high.astype(np.float64)).astype(jnp.bfloat16)
    return [jnp.asarray(high), jnp.asarray(low)]


def solve_tables():
    column = np.zeros((UX, UX))
    full = sine_table(EX)
    for lane in range(UX):
        place = lane + OV if lane < CX + OV else lane - UX + OV
        if 0 <= place < EX:
            column[lane, :EX] = full[place]
    rows = np.roll(sine_table(EY), -OV, axis=0)
    row_fwd = np.kron(np.eye(4), rows.T)
    depth = sine_table(EZ)
    even = np.kron(depth[0::2, :HALF], np.eye(8))
    odd = np.kron(depth[1::2, :HALF], np.eye(8))
    order = np.concatenate([np.arange(0, EZ, 2), np.arange(1, EZ, 2)])
    spectrum = (
        eigen_line(EZ)[order][:, None, None]
        + eigen_line(EY)[None, :, None]
        + eigen_line(EX)[None, None, :]
    )
    inverse = np.zeros((EZ, EY, UX), np.float32)
    inverse[:, :, :EX] = 1.0 / (mass_term + bend_mean * spectrum**2 + split_term * spectrum)
    tables = []
    for table in (column, column.T, row_fwd, row_fwd.T, even, odd, even.T, odd.T):
        tables += halves(table)
    return tables + [jnp.asarray(inverse)]


def cut(values):
    high = values.astype(bf16)
    return high, (values - high.astype(f32)).astype(bf16)


def mul(a, b):
    return lax.dot_general(a, b, (((1,), (0,)), ((), ())), preferred_element_type=f32)


def mul3(a, b):
    return mul(a[0], b[0]) + (mul(a[0], b[1]) + mul(a[1], b[0]))


def lanes():
    return lax.broadcasted_iota(jnp.int32, (8, 128), 1)


def subs():
    return lax.broadcasted_iota(jnp.int32, (8, 128), 0)


def spin(values, shift, axis):
    size = values.shape[axis]
    shift = shift % size
    return values if shift == 0 else pltpu.roll(values, shift, axis)


def pack(into, values, lead, width, at):
    lane = lax.broadcasted_iota(jnp.int32, values.shape, 1)
    inside = (lane >= width * at) & (lane < width * (at + 1))
    moved = spin(values, lead + width * at, 1)
    return jnp.where(inside, moved, 0.0 if into is None else into)


def unpack(packed, lead, width, at):
    moved = spin(packed, -(lead + width * at), 1)
    lane = lax.broadcasted_iota(jnp.int32, packed.shape, 1)
    return jnp.where((lane >= 128 - lead) | (lane < width - lead), moved, 0.0)


def forward(values, tables):
    column, row = (tables[0][...], tables[1][...]), (tables[4][...], tables[5][...])
    return mul3(row, cut(mul3(cut(values.reshape(GROUP * EY, UX)), column))).reshape(GROUP, EY, UX)


def finish_solve(solved, tables, inverse, shape, low, high):
    pairs = [(tables[2 * i][...], tables[2 * i + 1][...]) for i in range(8)]
    _, column, _, row, even_fwd, odd_fwd, even_bwd, odd_bwd = pairs
    for tile in range(EY // 8):
        rows = slice(8 * tile, 8 * tile + 8)
        near = solved[:HALF, rows, :]
        far = jnp.concatenate([solved[EZ - 1 - i : EZ - i, rows, :] for i in range(HALF)], axis=0)
        even = cut((near + far).reshape(8 * HALF, UX))
        odd = cut((near - far).reshape(8 * HALF, UX))
        even = mul3(even_fwd, even) * inverse[:HALF, rows, :].reshape(8 * HALF, UX)
        odd = mul3(odd_fwd, odd) * inverse[HALF:, rows, :].reshape(8 * HALF, UX)
        even = mul3(even_bwd, cut(even)).reshape(HALF, 8, UX)
        odd = mul3(odd_bwd, cut(odd)).reshape(HALF, 8, UX)
        solved[:HALF, rows, :] = even + odd
        far = even - odd
        for i in range(HALF):
            solved[EZ - 1 - i, rows, :] = far[i]

    for z in range(0, EZ, GROUP):
        values = cut(mul3(row, cut(solved[z : z + GROUP].reshape(GROUP * EY, UX))))
        solved[z : z + GROUP] = mul3(values, column).reshape(GROUP, EY, UX)

    lane = lanes()
    for first in range(0, EZ, shape.per):
        for tile in range(5):
            rows = slice(8 * tile, 8 * tile + 8)
            packed = [None, None]
            for j in range(min(shape.per, EZ - first)):
                near, far = solved[first + j, rows, :CX], solved[first + j, rows, CX:]
                packed[0] = pack(
                    packed[0], jnp.where(lane >= 124, far, near), OV, shape.width, j
                )
                packed[1] = pack(
                    packed[1],
                    jnp.where(lane >= 128 - shape.halo, near, far),
                    shape.halo,
                    shape.width,
                    j,
                )
            low[first // shape.per * 5 + tile] = packed[0]
            high[first // shape.per * 5 + tile] = packed[1]


def column_folded(solved, from_left, from_right, shape, z, tile):
    lane, rows = lanes(), slice(8 * tile, 8 * tile + 8)
    at, j = z // shape.per * 5 + tile, z % shape.per
    left = unpack(from_left[at], shape.halo, shape.width, j)
    right = unpack(from_right[at], OV, shape.width, j)
    return (
        solved[z, rows, :CX] + jnp.where(lane < 64, left, right),
        solved[z, rows, CX:] + jnp.where(lane < 64, right, left),
    )


def row_strips_kernel(shape, solved, from_left, from_right, low, high):
    sub = subs()
    extras = {}

    def add_extra(strip, name, place, values, at):
        extras[name, place] = pack(
            extras.get((name, place)), values, shape.halo, 2 * shape.halo, at
        )
        strip[place] = extras[name, place]

    rest = {}
    for z in range(EZ):
        tiles = {
            t: column_folded(solved, from_left, from_right, shape, z, t) for t in (0, 3, 4)
        }
        parts = (
            ("low", low, 4, 4, 0, 4),
            ("high", high, 4 if shape.last else 2, 3, 4, 2),
        )
        for name, strip, cut_at, upper, lower, keep in parts:
            main, extra = [jnp.where(sub >= cut_at, tiles[upper][i], tiles[lower][i]) for i in (0, 1)]
            strip[z] = main
            per = shape.extra_per
            add_extra(strip, name, shape.extra_a + z // per, extra, z % per)
            if shape.last:
                continue
            j = z % 4
            inside = (sub >= 2 * j) & (sub < 2 * j + 2)
            for i in (0, 1):
                moved = spin(tiles[lower][i], 2 * j - keep, 0)
                rest[name, i] = jnp.where(inside, moved, rest[name, i] if j else 0.0)
            if j == 3:
                strip[EZ + z // 4] = rest[name, 0]
                quad = z // 4
                add_extra(strip, name, shape.extra_b + quad // per, rest[name, 1], quad % per)


def widen_kernel(shape, solved, from_left, from_right, folded):
    sub = subs()
    for z in range(EZ):
        for tile in range(5):
            values = column_folded(solved, from_left, from_right, shape, z, tile)
            for side in (0, 1):
                columns = slice(128 * side, 128 * side + 128)
                value = values[side]
                if tile == 4:
                    folded[z, 40:48, columns] = jnp.where(sub >= 4, value, 0.0)
                    value = jnp.where(sub < 4, value, 0.0)
                folded[z, 8 * tile : 8 * tile + 8, columns] = value


def row_part(strip, shape, z, side, keep):
    sub, per = subs(), shape.extra_per
    if side == 0:
        main = strip[z]
    else:
        main = unpack(strip[shape.extra_a + z // per], shape.halo, 2 * shape.halo, z % per)
    if shape.last:
        return main, jnp.zeros((8, 128), f32)
    if side == 0:
        rest = strip[EZ + z // 4]
    else:
        quad = z // 4
        rest = unpack(
            strip[shape.extra_b + quad // per], shape.halo, 2 * shape.halo, quad % per
        )
    moved = spin(rest, keep - 2 * (z % 4), 0)
    return main, jnp.where((sub >= keep) & (sub < keep + 2), moved, 0.0)


def depth_strips_kernel(shape, widened, from_near, from_far, folded, low, high):
    sub = subs()
    cut_at = 4 if shape.last else 2
    for z in range(EZ):
        for side in (0, 1):
            columns = slice(128 * side, 128 * side + 128)
            main, rest = row_part(from_near, shape, z, side, 2)
            new = {
                0: jnp.where(sub < cut_at, main, rest),
                5: jnp.where(sub >= cut_at, main, 0.0),
            }
            main, rest = row_part(from_far, shape, z, side, 4)
            new[3] = jnp.where(sub >= 4, main, 0.0)
            new[4] = jnp.where(sub < 4, main, rest)
            for tile in range(6):
                rows = slice(8 * tile, 8 * tile + 8)
                if tile in new:
                    folded[z, rows, columns] = widened[z, rows, columns] + new[tile]
                else:
                    folded[z, rows, columns] = widened[z, rows, columns]
    for strip, start in ((low, 0), (high, EZ - shape.rim)):
        extra = None
        for i in range(shape.rim):
            strip[i] = folded[start + i, :, :CX]
            extra = pack(extra, folded[start + i, :, CX:], shape.halo, 2 * shape.halo, i)
        strip[shape.rim] = extra


def laplace(below, centre, above):
    beside = below + above
    beside = beside + (pltpu.roll(centre, 1, 0) + pltpu.roll(centre, UY - 1, 0))
    beside = beside + (pltpu.roll(centre, 1, 1) + pltpu.roll(centre, UX - 1, 1))
    return 6.0 * centre - beside


def operate(get, shift, span, flux, weighted, stiffness, wide, core):
    unroll = 4
    start, stop = span

    def first(z, carry):
        values = laplace(get(z - 1), get(z), get(z + 1))
        flux[z - shift] = values
        weighted[z - shift] = stiffness[z] * values
        return carry

    lax.fori_loop(start - 1, stop + 1, first, 0, unroll=unroll)
    sub = lax.broadcasted_iota(jnp.int32, (8, UX), 0)

    def second(z, carry):
        own = get(z)
        at = z - shift
        values = laplace(weighted[at - 1], weighted[at], weighted[at + 1])
        values = mass_term * own + values + split_term * flux[at]
        if wide is not None:
            wide[z - 2, :CY, :] = values[:CY]
            wide[z - 2, CY:, :] = jnp.where(sub < 4, values[CY : CY + 8], values[CY + 8 :])
        return core(z, own[:CY, :CX], values[:CY, :CX], carry)

    return lambda first_z, last_z, carry, use_core: lax.fori_loop(
        first_z,
        last_z,
        second if use_core else lambda z, c: (second(z, None), c)[1],
        carry,
        unroll=unroll,
    )


def add_up(total, product):
    return total + ((product[0:8] + product[8:16]) + (product[16:24] + product[24:32]))


def core_step(count, rhs, earlier, smooth, image):
    def step(z, own, core, totals):
        if totals is None:
            return None
        at = z - 6
        smooth[at] = own
        image[at] = core
        new = [add_up(totals[0], own * rhs[at])]
        for i in range(count):
            new.append(add_up(totals[1 + i], core * earlier[i][at]))
        new.append(add_up(totals[1 + count], core * own))
        return tuple(new)

    return step


def inner_kernel(count, shape, *refs):
    folded, stiffness, rhs = refs[:3]
    earlier, refs = refs[3 : 3 + count], refs[3 + count :]
    tables = ()
    if not shape.last:
        tables, refs = refs[:16], refs[16:]
    smooth, image, sums = refs[:3]
    wide, solved = (None, None) if shape.last else refs[3:5]
    flux, weighted = refs[-2:]
    step = core_step(count, rhs, earlier, smooth, image)
    run = operate(
        lambda z: folded[z - 2], 10, (12, 48), flux, weighted, stiffness, wide, step
    )
    totals = run(12, 48, (jnp.zeros((8, 128), f32),) * (count + 2), True)
    for i, value in enumerate(totals):
        sums[i] = value
    if not shape.last:
        for z in INNER:
            solved[z : z + GROUP] = forward(wide[z : z + GROUP], tables)


def outer_kernel(count, shape, *refs):
    folded, from_below, from_above, stiffness, rhs = refs[:5]
    earlier, refs = refs[5 : 5 + count], refs[5 + count :]
    smooth_in, image_in, sums_in = refs[:3]
    refs = refs[3:]
    wide = None
    if shape.last:
        parts, refs = refs[:count], refs[count:]
    else:
        wide_in, solved_in, inverse = refs[:3]
        tables, refs = refs[3:19], refs[19:]
        wide = refs[-4]
        for z in (10, 11, 44, 45):
            wide[z] = wide_in[z]
    smooth, image, sums = refs[:3]
    full, flux, weighted = refs[-3:]
    smooth[6:42] = smooth_in[6:42]
    image[6:42] = image_in[6:42]
    edge = 10 - shape.rim
    step = core_step(count, rhs, earlier, smooth, image)
    totals = tuple(sums_in[i] for i in range(count + 2))
    first_z = 6 if shape.last else 2
    for strip, base, shift in ((from_below, edge, 0), (from_above, 50, 46)):
        for z in range(14):
            layer = z + shift
            if not (4 if shape.last else 0) <= layer < (56 if shape.last else 60):
                continue
            at = layer - base
            inside = 2 <= layer < UZ - 2
            if 0 <= at < shape.rim:
                extra = unpack(strip[shape.rim], shape.halo, 2 * shape.halo, at)
                if inside:
                    full[z, :, :CX] = folded[layer - 2, :, :CX] + strip[at]
                    full[z, :, CX:] = folded[layer - 2, :, CX:] + extra
                else:
                    full[z, :, :CX] = strip[at]
                    full[z, :, CX:] = extra
            else:
                full[z] = folded[layer - 2]
        span = (first_z, 12) if shift == 0 else (48, UZ - first_z)
        run = operate(
            lambda z, shift=shift: full[z - shift], shift, span, flux, weighted, stiffness, wide, step
        )
        if shift == 0:
            if not shape.last:
                run(2, 6, 0, False)
            totals = run(6, 12, totals, True)
        else:
            totals = run(48, 54, totals, True)
            if not shape.last:
                run(54, 58, 0, False)
    if not shape.last:
        for i, value in enumerate(totals):
            sums[i] = value
        solved, low, high = refs[3:6]
        solved[12:44] = solved_in[12:44]
        for z in OUTER:
            solved[z : z + GROUP] = forward(wide[z : z + GROUP], tables)
        finish_solve(solved, tables, inverse, Shape(count + 2 == ITERS), low, high)
        return
    lane = lanes()
    values = [part[i] for part in parts for i in range(part.shape[0])] + list(totals)
    gathered = jnp.zeros((8, 128), f32)
    for i, value in enumerate(values):
        value = jnp.sum(jnp.sum(value, axis=0, keepdims=True), axis=1, keepdims=True)
        gathered = jnp.where(lane == i, value, gathered)
    sums[...] = gathered


def start_columns_kernel(rhs, stiffness, low, high):
    for source, base, width in ((rhs, 0, 4), (stiffness, 8, 5)):
        per = 128 // width
        for first in range(0, CZ, per):
            for tile in range(4):
                packed = [None, None]
                for j in range(min(per, CZ - first)):
                    values = source[first + j, 8 * tile : 8 * tile + 8, :]
                    packed[0] = pack(packed[0], values, 0, width, j)
                    packed[1] = pack(packed[1], values, width, width, j)
                low[base + first // per * 4 + tile] = packed[0]
                high[base + first // per * 4 + tile] = packed[1]


def start_extra(from_left, from_right, base, width, z, tile):
    per, lane = 128 // width, lanes()
    at, j = base + z // per * 4 + tile, z % per
    left = spin(from_left[at], -(width + width * j), 1)
    right = spin(from_right[at], -width * j, 1)
    return jnp.where(lane >= 128 - width, left, jnp.where(lane < width, right, 0.0))


START_RHS, START_RHS_X = 0, 24
START_ST, START_ST_X, START_ONE, START_ONE_X = 26, 50, 52, 58
START_Y = 59


def start_rows_kernel(rhs, stiffness, from_left, from_right, low, high):
    sub = subs()

    def both(source, base, width, z, tile):
        return (
            source[z, 8 * tile : 8 * tile + 8, :],
            start_extra(from_left, from_right, base, width, z, tile),
        )

    for strip, tile in ((low, 0), (high, 3)):
        for source, base, width, main_at, extra_at in (
            (rhs, 0, 4, START_RHS, START_RHS_X),
            (stiffness, 8, 5, START_ST, START_ST_X),
        ):
            per = 128 // (2 * width)
            extra = None
            for k in range(CZ // 2):
                a = both(source, base, width, 2 * k, tile)
                b = both(source, base, width, 2 * k + 1, tile)
                if tile == 0:
                    pair = [jnp.where(sub < 4, a[i], spin(b[i], 4, 0)) for i in (0, 1)]
                else:
                    pair = [jnp.where(sub < 4, spin(a[i], -4, 0), b[i]) for i in (0, 1)]
                strip[main_at + k] = pair[0]
                extra = pack(extra if k % per else None, pair[1], width, 2 * width, k % per)
                strip[extra_at + k // per] = extra
        extra = None
        for k in range(CZ // 8):
            row = [None, None]
            for j in range(8):
                values = both(stiffness, 8, 5, 8 * k + j, tile)
                for i in (0, 1):
                    moved = spin(values[i], j - (4 if tile == 0 else 3), 0)
                    row[i] = jnp.where(sub == j, moved, 0.0 if row[i] is None else row[i])
            strip[START_ONE + k] = row[0]
            extra = pack(extra, row[1], 5, 10, k)
        strip[START_ONE_X] = extra


def start_depth_kernel(
    rhs, stiffness, from_left, from_right, from_near, from_far, wide, stiff, low, high
):
    sub = subs()

    def pair_part(strip, main_at, extra_at, width, z, side):
        per = 128 // (2 * width)
        if side == 0:
            pair = strip[main_at + z // 2]
        else:
            k = z // 2
            pair = unpack(strip[extra_at + k // per], width, 2 * width, k % per)
        return pair

    def one_part(strip, z, side, row):
        values = strip[START_ONE + z // 8]
        if side == 1:
            values = unpack(strip[START_ONE_X], 5, 10, z // 8)
        return spin(values, row - z % 8, 0)

    for z in range(CZ):
        for side in (0, 1):
            columns = slice(128 * side, 128 * side + 128)
            for tile in range(4):
                rows = slice(8 * tile, 8 * tile + 8)
                if side == 0:
                    wide[z, rows, columns] = rhs[z, rows, :]
                    stiff[z + 6, rows, columns] = stiffness[z, rows, :]
                else:
                    wide[z, rows, columns] = start_extra(from_left, from_right, 0, 4, z, tile)
                    stiff[z + 6, rows, columns] = start_extra(
                        from_left, from_right, 8, 5, z, tile
                    )
            odd = z % 2
            far = pair_part(from_far, START_RHS, START_RHS_X, 4, z, side)
            near = pair_part(from_near, START_RHS, START_RHS_X, 4, z, side)
            far = spin(far, 4, 0) if odd else far
            near = near if odd else spin(near, 4, 0)
            wide[z, 32:40, columns] = jnp.where(sub < 4, far, near)
            far = pair_part(from_far, START_ST, START_ST_X, 5, z, side)
            far = spin(far, 4, 0) if odd else far
            one = one_part(from_far, z, side, 4)
            stiff[z + 6, 32:40, columns] = jnp.where(
                sub < 4, far, jnp.where(sub == 4, one, 0.0)
            )
            near = pair_part(from_near, START_ST, START_ST_X, 5, z, side)
            near = near if odd else spin(near, 4, 0)
            one = one_part(from_near, z, side, 3)
            stiff[z + 6, 40:48, columns] = jnp.where(
                sub >= 4, near, jnp.where(sub == 3, one, 0.0)
            )
    blank = jnp.zeros((8, 128), f32)
    for strip, wide_at, stiff_at in ((low, 0, 6), (high, CZ - 4, CZ + 1)):
        extra = None
        for i in range(4):
            strip[i, :40] = wide[wide_at + i, :, :CX]
            strip[i, 40:48] = blank
        for i in range(5):
            strip[4 + i] = stiff[stiff_at + i, :, :CX]
            extra = pack(extra, stiff[stiff_at + i, :, CX:], 5, 10, i)
        strip[9] = extra
        for tile in range(5):
            rows = slice(8 * tile, 8 * tile + 8)
            extra = strip[9, rows, :]
            for i in range(4):
                lane = lanes()
                moved = spin(wide[wide_at + i, rows, CX:], 4 + 64 + 8 * i, 1)
                inside = (lane >= 64 + 8 * i) & (lane < 72 + 8 * i)
                extra = jnp.where(inside, moved, extra)
            strip[9, rows, :] = extra


def start_inner_kernel(wide, *refs):
    tables, solved = refs[:16], refs[16]
    for z in range(4, 52, GROUP):
        solved[z : z + GROUP] = forward(wide[z - 4 : z], tables)


def start_outer_kernel(from_below, from_above, stiff_in, solved_in, inverse, *refs):
    tables, (solved, stiff, low, high, edge) = refs[:16], refs[16:]
    solved[4:52] = solved_in[4:52]
    stiff[6:54] = stiff_in[6:54]
    for strip, first, stiff_at in ((from_below, 0, 1), (from_above, 52, 54)):
        lane = lax.broadcasted_iota(jnp.int32, (EY, CX), 1)
        for i in range(4):
            edge[i, :, :CX] = strip[i, :40]
            moved = spin(strip[9, :40], -(4 + 64 + 8 * i), 1)
            edge[i, :, CX:] = jnp.where((lane >= 124) | (lane < 4), moved, 0.0)
        for i in range(5):
            stiff[stiff_at + i, :, :CX] = strip[4 + i]
            stiff[stiff_at + i, :, CX:] = unpack(strip[9], 5, 10, i)
        solved[first : first + GROUP] = forward(edge[...], tables)
    finish_solve(solved, tables, inverse, Shape(False), low, high)


def weights(b, pair):
    sigma = [jnp.zeros((1, 1), f32)] * ITERS
    delta = None
    current = None
    for turn in range(ITERS):
        zeta = [jnp.ones((1, 1), f32)] + [-s for s in sigma[:turn]]
        following = sum(z * b[i] for i, z in enumerate(zeta))
        for i, z in enumerate(zeta):
            for j in range(turn):
                following = following - z * sigma[j] * pair[i, j]
        if turn == 0:
            delta = zeta
        else:
            ratio = following / current
            delta = [z + ratio * d for z, d in zip(zeta, delta + [jnp.zeros((1, 1), f32)])]
        current = following
        bending = sum(
            delta[i] * delta[j] * pair[i, j] for i in range(turn + 1) for j in range(turn + 1)
        )
        step = current / bending
        sigma = [
            s + step * d for s, d in zip(sigma, delta + [jnp.zeros((1, 1), f32)] * (ITERS - turn - 1))
        ]
    return sigma


def combine_kernel(sums, rhs, u0, u1, u2, w0, w1, w2, answer, rest):
    picked = [
        jnp.sum(jnp.where(lanes()[:1] == i, sums[:1], 0.0), axis=1, keepdims=True)
        for i in range(ITERS * (ITERS + 3) // 2)
    ]
    b, pair, at = [], {}, 0
    for j in range(ITERS):
        b.append(picked[at])
        for i in range(j + 1):
            pair[i, j] = pair[j, i] = picked[at + 1 + i]
        at += j + 2
    s = weights(b, pair)

    def step(z, carry):
        answer[z] = s[0] * u0[z] + s[1] * u1[z] + s[2] * u2[z]
        rest[z] = rhs[z] - (s[0] * w0[z] + s[1] * w1[z] + s[2] * w2[z])
        return carry

    lax.fori_loop(0, CZ, step, 0, unroll=4)


VMEM = pl.BlockSpec(memory_space=pltpu.VMEM)


def call(kernel, shapes, operands, scratch=(), cost=2.0):
    return pl.pallas_call(
        kernel,
        out_shape=[jax.ShapeDtypeStruct(shape, f32) for shape in shapes],
        in_specs=[VMEM] * len(operands),
        out_specs=[VMEM] * len(shapes),
        scratch_shapes=[pltpu.VMEM(shape, f32) for shape in scratch],
        cost_estimate=pl.CostEstimate(
            flops=0, bytes_accessed=int(cost * 3.6e6), transcendentals=0
        ),
        compiler_params=pltpu.CompilerParams(vmem_limit_bytes=20 * 2**20),
    )(*operands)


def shifted(block, axis, step):
    count = lax.axis_size(axis)
    return lax.ppermute(block, axis, [(i, (i + step) % count) for i in range(count)])


def swap(low, high, axis):
    return shifted(high, axis, 1), shifted(low, axis, -1)


def total(values):
    for axis in ("gx", "gy", "gz"):
        count = lax.axis_size(axis)
        hop = 1
        while hop < count:
            values = values + lax.ppermute(values, axis, [(i, i ^ hop) for i in range(count)])
            hop *= 2
    return values


CORE = (CZ, CY, CX)
FIELD = (EZ, EY, UX)


def per_device(rhs_field, stiffness):
    *tables, inverse = solve_tables()
    strips = call(start_columns_kernel, [(16, 8, 128)] * 2, [rhs_field, stiffness])
    columns = swap(*strips, "gx")
    fields = [rhs_field, stiffness, *columns]
    strips = call(start_rows_kernel, [(START_Y, 8, 128)] * 2, fields)
    rows = swap(*strips, "gy")
    wide, stiff, *strips = call(
        start_depth_kernel,
        [(CZ, EY, UX), (UZ, UY, UX)] + [(10, UY, CX)] * 2,
        [*fields, *rows],
    )
    depths = swap(*strips, "gz")
    solved = call(start_inner_kernel, [FIELD], [wide, *tables], cost=4.0)[0]
    shape = Shape(False)
    solved, stiff, *strips = call(
        start_outer_kernel,
        [FIELD, (UZ, UY, UX)] + [(shape.x_tiles, 8, 128)] * 2,
        [*depths, stiff, solved, inverse, *tables],
        [(4, EY, UX)],
        cost=6.0,
    )
    smooth, image, sums = [], [], []
    for turn in range(ITERS):
        shape = Shape(turn + 1 == ITERS)
        columns = swap(*strips, "gx")
        strips = call(
            functools.partial(row_strips_kernel, shape),
            [(shape.y_tiles, 8, 128)] * 2,
            [solved, *columns],
        )
        rows = swap(*strips, "gy")
        widened = call(
            functools.partial(widen_kernel, shape), [(EZ, UY, UX)], [solved, *columns], cost=4.0
        )[0]
        folded, *strips = call(
            functools.partial(depth_strips_kernel, shape),
            [(EZ, UY, UX)] + [(shape.rim + 1, UY, CX)] * 2,
            [widened, *rows],
        )
        depths = swap(*strips, "gz")
        products = (turn + 2, 8, 128)
        outs = [CORE, CORE, products]
        if not shape.last:
            outs += [FIELD, FIELD]
        own, core, part, *fields = call(
            functools.partial(inner_kernel, turn, shape),
            outs,
            [folded, stiff, rhs_field, *smooth] + ([] if shape.last else tables),
            [(40, UY, UX)] * 2,
            cost=6.0,
        )
        operands = [folded, *depths, stiff, rhs_field, *smooth]
        operands += [own, core, part]
        scratch = [(14, UY, UX)] * 3
        if shape.last:
            operands += sums
            outs = [CORE, CORE, (8, 128)]
        else:
            operands += [*fields, inverse, *tables]
            following = Shape(turn + 2 == ITERS)
            outs = [CORE, CORE, products, FIELD] + [(following.x_tiles, 8, 128)] * 2
            scratch = [FIELD] + scratch
        own, core, part, *rest = call(
            functools.partial(outer_kernel, turn, shape),
            outs,
            operands,
            scratch,
            cost=8.0,
        )
        if rest:
            solved, *strips = rest
        smooth.append(own)
        image.append(core)
        sums.append(part)
    operands = [total(sums[-1]), rhs_field, *smooth, *image]
    return tuple(call(combine_kernel, [CORE] * 2, operands))


def solution(mesh):
    in_specs = (P("gz", "gy", "gx"), P("gz", "gy", "gx"))
    out_specs = (P("gz", "gy", "gx"), P("gz", "gy", "gx"))
    return jax.shard_map(
        per_device, mesh=mesh, in_specs=in_specs, out_specs=out_specs, check_vma=False
    )
```

```python
import functools

import jax
import jax.numpy as jnp
import numpy as np
from jax import lax
from jax.experimental import pallas as pl
from jax.experimental.pallas import tpu as pltpu
from jax.sharding import PartitionSpec as P

OV = 4
ITERS = 3
CZ, CY, CX = 48, 32, 128
EZ, EY, EX = CZ + 2 * OV, CY + 2 * OV, CX + 2 * OV
HALF = EZ // 2
UZ, UY, UX = CZ + 12, 48, 256
GROUP = 4
CHUNK = 2
CHUNK_UNROLL = 2
INNER = range(12, 44, GROUP)
OUTER = [z for z in range(0, EZ, GROUP) if z not in INNER]


class Shape:
    def __init__(self, last):
        self.rim = 6 if last else 10
        self.halo = 4 if last else 6
        self.width = 4 + self.halo
        self.per = 128 // self.width
        self.x_tiles = -(-EZ // self.per) * 5
        self.x_groups = self.x_tiles // 5
        self.extra_a = EZ if last else EZ + EZ // 4
        self.extra_b = self.extra_a + -(-EZ // 16)
        self.y_tiles = self.extra_b + (0 if last else 1)
        self.cut_near = 4 if last else 2
        self.c_tiles = 2 * self.x_groups + (0 if last else -(-self.x_groups // 2))
        self.last = last


mass_term = 1e-05
split_term = 0.5
bend_mean = 0.1
f32, bf16 = jnp.float32, jnp.bfloat16


def sine_table(length):
    places = np.arange(1, length + 1, dtype=np.float64)
    return np.sqrt(2.0 / (length + 1)) * np.sin(
        np.pi * places[:, None] * places[None, :] / (length + 1)
    )


def eigen_line(length):
    places = np.arange(1, length + 1, dtype=np.float64)
    return 2.0 - 2.0 * np.cos(np.pi * places / (length + 1))


def halves(table):
    high = np.asarray(table, np.float32).astype(jnp.bfloat16)
    low = (np.asarray(table, np.float64) - high.astype(np.float64)).astype(jnp.bfloat16)
    return [jnp.asarray(high), jnp.asarray(low)]


def solve_tables():
    column = np.zeros((UX, UX))
    full = sine_table(EX)
    for lane in range(UX):
        place = lane + OV if lane < CX + OV else lane - UX + OV
        if 0 <= place < EX:
            column[lane, :EX] = full[place]
    rows = np.roll(sine_table(EY), -OV, axis=0)
    row_fwd = np.kron(np.eye(2), rows.T)
    depth = sine_table(EZ)
    even = np.kron(depth[0::2, :HALF], np.eye(8))
    odd = np.kron(depth[1::2, :HALF], np.eye(8))
    order = np.concatenate([np.arange(0, EZ, 2), np.arange(1, EZ, 2)])
    spectrum = (
        eigen_line(EZ)[order][:, None, None]
        + eigen_line(EY)[None, :, None]
        + eigen_line(EX)[None, None, :]
    )
    inverse = np.zeros((EZ, EY, UX), np.float32)
    inverse[:, :, :EX] = 1.0 / (mass_term + bend_mean * spectrum**2 + split_term * spectrum)
    tables = []
    for table in (column, column.T):
        tables += halves(table)
    for table in (row_fwd, row_fwd.T):
        high, low = halves(table)
        tables.append(jnp.concatenate([high, low, high], axis=1))
    for table in (even, odd, even.T, odd.T):
        tables += halves(table)
    return tables + [jnp.asarray(inverse)]


def cut(values):
    high = values.astype(bf16)
    return high, (values - high.astype(f32)).astype(bf16)


def mul(a, b):
    return lax.dot_general(a, b, (((1,), (0,)), ((), ())), preferred_element_type=f32)


def mul3(a, b):
    return mul(a[0], b[0]) + (mul(a[0], b[1]) + mul(a[1], b[0]))


def lanes():
    return lax.broadcasted_iota(jnp.int32, (8, 128), 1)


def subs():
    return lax.broadcasted_iota(jnp.int32, (8, 128), 0)


def spin(values, shift, axis):
    size = values.shape[axis]
    shift = shift % size
    return values if shift == 0 else pltpu.roll(values, shift, axis)


def pack(into, values, lead, width, at):
    lane = lax.broadcasted_iota(jnp.int32, values.shape, 1)
    inside = (lane >= width * at) & (lane < width * (at + 1))
    moved = spin(values, lead + width * at, 1)
    return jnp.where(inside, moved, 0.0 if into is None else into)


def unpack(packed, lead, width, at):
    moved = spin(packed, -(lead + width * at), 1)
    lane = lax.broadcasted_iota(jnp.int32, packed.shape, 1)
    return jnp.where((lane >= 128 - lead) | (lane < width - lead), moved, 0.0)


def row_product(table, values):
    out, step = [], 2 * EY
    for at in range(0, values.shape[0], step):
        high, low = cut(values[at : at + step])
        out.append(mul(table, jnp.concatenate([high, high, low], axis=0)))
    return jnp.concatenate(out, axis=0)


def forward(values, tables):
    values = mul3(cut(values.reshape(GROUP * EY, UX)), (tables[0][...], tables[1][...]))
    return row_product(tables[4][...], values).reshape(GROUP, EY, UX)


def finish_solve(solved, tables, inverse, shape, low, high):
    column, row = (tables[2][...], tables[3][...]), tables[5][...]
    even_fwd, odd_fwd, even_bwd, odd_bwd = [
        (tables[i][...], tables[i + 1][...]) for i in (6, 8, 10, 12)
    ]
    for tile in range(EY // 8):
        rows = slice(8 * tile, 8 * tile + 8)
        near = solved[:HALF, rows, :]
        far = jnp.concatenate([solved[EZ - 1 - i : EZ - i, rows, :] for i in range(HALF)], axis=0)
        even = cut((near + far).reshape(8 * HALF, UX))
        odd = cut((near - far).reshape(8 * HALF, UX))
        even = mul3(even_fwd, even) * inverse[:HALF, rows, :].reshape(8 * HALF, UX)
        odd = mul3(odd_fwd, odd) * inverse[HALF:, rows, :].reshape(8 * HALF, UX)
        even = mul3(even_bwd, cut(even)).reshape(HALF, 8, UX)
        odd = mul3(odd_bwd, cut(odd)).reshape(HALF, 8, UX)
        solved[:HALF, rows, :] = even + odd
        far = even - odd
        for i in range(HALF):
            solved[EZ - 1 - i, rows, :] = far[i]

    later = Later()
    for z in range(0, EZ, GROUP):
        values = cut(row_product(row, solved[z : z + GROUP].reshape(GROUP * EY, UX)))
        values = mul3(values, column).reshape(GROUP, EY, UX)
        later.flush()
        later.put(solved, slice(z, z + GROUP), values)
    later.flush()

    lane = lanes()
    for first in range(0, EZ, shape.per):
        for tile in range(5):
            rows = slice(8 * tile, 8 * tile + 8)
            packed = [None, None]
            for j in range(min(shape.per, EZ - first)):
                near, far = solved[first + j, rows, :CX], solved[first + j, rows, CX:]
                packed[0] = pack(
                    packed[0], jnp.where(lane >= 124, far, near), OV, shape.width, j
                )
                packed[1] = pack(
                    packed[1],
                    jnp.where(lane >= 128 - shape.halo, near, far),
                    shape.halo,
                    shape.width,
                    j,
                )
            low[first // shape.per * 5 + tile] = packed[0]
            high[first // shape.per * 5 + tile] = packed[1]


def column_folded(solved, from_left, from_right, shape, z, tile):
    lane, rows = lanes(), slice(8 * tile, 8 * tile + 8)
    at, j = z // shape.per * 5 + tile, z % shape.per
    left = unpack(from_left[at], shape.halo, shape.width, j)
    right = unpack(from_right[at], OV, shape.width, j)
    return (
        solved[z, rows, :CX] + jnp.where(lane < 64, left, right),
        solved[z, rows, CX:] + jnp.where(lane < 64, right, left),
    )


class Later:
    def __init__(self):
        self.kept = []

    def put(self, ref, index, values):
        self.kept.append((ref, index, values))

    def flush(self):
        for ref, index, values in self.kept:
            ref[index] = values
        self.kept = []


def row_strips_kernel(shape, solved, low, high):
    sub = subs()
    for strip, cut_at, upper, lower, keep in (
        (low, 4, 4, 0, 4),
        (high, shape.cut_near, 3, 4, 2),
    ):
        extra_a = extra_b = None
        for quad in range(EZ // 4):
            rest = [None, None]
            for j in range(4):
                z = 4 * quad + j
                for side in (0, 1):
                    columns = slice(128 * side, 128 * side + 128)
                    lower_tile = solved[z, 8 * lower : 8 * lower + 8, columns]
                    upper_tile = solved[z, 8 * upper : 8 * upper + 8, columns]
                    main = jnp.where(sub >= cut_at, upper_tile, lower_tile)
                    if side == 0:
                        strip[z] = main
                    else:
                        extra_a = pack(extra_a if z % 16 else None, main, OV, 2 * OV, z % 16)
                        if z % 16 == 15 or z + 1 == EZ:
                            strip[shape.extra_a + z // 16] = extra_a
                    if not shape.last:
                        inside = (sub >= 2 * j) & (sub < 2 * j + 2)
                        moved = spin(lower_tile, 2 * j - keep, 0)
                        rest[side] = jnp.where(inside, moved, rest[side] if j else 0.0)
            if not shape.last:
                strip[EZ + quad] = rest[0]
                extra_b = pack(extra_b, rest[1], OV, 2 * OV, quad)
        if not shape.last:
            strip[shape.extra_b] = extra_b


def corners_kernel(shape, from_left, from_right, low, high):
    sub, groups = subs(), shape.x_groups
    for strip, cut_at, upper, lower, keep in (
        (low, 4, 4, 0, 4),
        (high, shape.cut_near, 3, 4, 2),
    ):
        rest = None
        for k in range(2 * groups):
            source = (from_left, from_right)[k // groups]
            lower_tile = source[k % groups * 5 + lower]
            strip[k] = jnp.where(sub >= cut_at, source[k % groups * 5 + upper], lower_tile)
            if shape.last:
                continue
            j = k % 4
            inside = (sub >= 2 * j) & (sub < 2 * j + 2)
            rest = jnp.where(inside, spin(lower_tile, 2 * j - keep, 0), rest if j else 0.0)
            if j == 3 or k + 1 == 2 * groups:
                strip[2 * groups + k // 4] = rest


def widen_kernel(shape, solved, from_left, from_right, folded):
    sub = subs()
    for z in range(EZ):
        for tile in range(5):
            values = column_folded(solved, from_left, from_right, shape, z, tile)
            for side in (0, 1):
                columns = slice(128 * side, 128 * side + 128)
                value = values[side]
                if tile == 4:
                    folded[z, 40:48, columns] = jnp.where(sub >= 4, value, 0.0)
                    value = jnp.where(sub < 4, value, 0.0)
                folded[z, 8 * tile : 8 * tile + 8, columns] = value


def row_part(strip, shape, z, side, keep):
    sub = subs()
    if side == 0:
        main = strip[z]
    else:
        main = unpack(strip[shape.extra_a + z // 16], OV, 2 * OV, z % 16)
    if shape.last:
        return main, jnp.zeros((8, 128), f32)
    if side == 0:
        rest = strip[EZ + z // 4]
    else:
        rest = unpack(strip[shape.extra_b], OV, 2 * OV, z // 4)
    moved = spin(rest, keep - 2 * (z % 4), 0)
    return main, jnp.where((sub >= keep) & (sub < keep + 2), moved, 0.0)


def depth_strips_kernel(
    shape, widened, from_near, from_far, corner_near, corner_far, folded, low, high, corners
):
    sub, lane, cut_at = subs(), lanes(), shape.cut_near
    groups = shape.x_groups
    for k in range(2 * groups):
        for strip, keep in ((corner_near, 2), (corner_far, 4)):
            main, rest = strip[k], 0.0
            if not shape.last:
                moved = spin(strip[2 * groups + k // 4], keep - 2 * (k % 4), 0)
                rest = jnp.where((sub >= keep) & (sub < keep + 2), moved, 0.0)
            if keep == 2:
                corners[0, k] = jnp.where(sub < cut_at, main, rest)
                corners[1, k] = jnp.where(sub >= cut_at, main, 0.0)
            else:
                corners[2, k] = jnp.where(sub >= 4, main, 0.0)
                corners[3, k] = jnp.where(sub < 4, main, rest)
    for z in range(EZ):
        group, j = z // shape.per, z % shape.per
        new = {}
        for side in (0, 1):
            main, rest = row_part(from_near, shape, z, side, 2)
            new[0, side] = jnp.where(sub < cut_at, main, rest)
            new[5, side] = jnp.where(sub >= cut_at, main, 0.0)
            main, rest = row_part(from_far, shape, z, side, 4)
            new[3, side] = jnp.where(sub >= 4, main, 0.0)
            new[4, side] = jnp.where(sub < 4, main, rest)
        for at, tile in enumerate((0, 5, 3, 4)):
            left = unpack(corners[at, group], shape.halo, shape.width, j)
            right = unpack(corners[at, groups + group], OV, shape.width, j)
            new[tile, 0] += jnp.where(lane < 64, left, right)
            new[tile, 1] += jnp.where(lane < 64, right, left)
        for side in (0, 1):
            columns = slice(128 * side, 128 * side + 128)
            for tile in range(6):
                rows = slice(8 * tile, 8 * tile + 8)
                value = widened[z, rows, columns]
                if (tile, side) in new:
                    value = value + new[tile, side]
                folded[z, rows, columns] = value
    for strip, start in ((low, 0), (high, EZ - shape.rim)):
        extra = None
        for i in range(shape.rim):
            strip[i] = folded[start + i, :, :CX]
            extra = pack(extra, folded[start + i, :, CX:], shape.halo, 2 * shape.halo, i)
        strip[shape.rim] = extra


def laplace(below, centre, above):
    beside = below + above
    beside = beside + (pltpu.roll(centre, 1, 0) + pltpu.roll(centre, UY - 1, 0))
    beside = beside + (pltpu.roll(centre, 1, 1) + pltpu.roll(centre, UX - 1, 1))
    return 6.0 * centre - beside


def operate(get, shift, span, flux, weighted, stiffness, wide, core):
    start, stop = span

    def chunks(body, start, stop, carry):
        size = CHUNK
        while (stop - start) % size:
            size -= 1
        return lax.fori_loop(
            0,
            (stop - start) // size,
            lambda i, c: body(start + size * i, size, c),
            carry,
            unroll=CHUNK_UNROLL,
        )

    def first(at, size, carry):
        later = Later()
        for z in [at + i for i in range(size)]:
            values = laplace(get(z - 1), get(z), get(z + 1))
            later.put(flux, z - shift, values)
            later.put(weighted, z - shift, stiffness[z] * values)
        later.flush()
        return carry

    chunks(first, start - 1, stop + 1, 0)
    sub = lax.broadcasted_iota(jnp.int32, (8, UX), 0)

    def second(base, size, carry, use_core):
        later = Later()
        for z in [base + i for i in range(size)]:
            own = get(z)
            at = z - shift
            values = laplace(weighted[at - 1], weighted[at], weighted[at + 1])
            values = mass_term * own + values + split_term * flux[at]
            if wide is not None:
                later.put(wide, (z - 2, slice(0, CY)), values[:CY])
                last = jnp.where(sub < 4, values[CY : CY + 8], values[CY + 8 :])
                later.put(wide, (z - 2, slice(CY, EY)), last)
            if use_core:
                carry = core(z, own[:CY, :CX], values[:CY, :CX], carry, later)
        later.flush()
        return carry

    return lambda first_z, last_z, carry, use_core: chunks(
        lambda z, size, c: second(z, size, c, use_core), first_z, last_z, carry
    )


def add_up(total, product):
    return total + ((product[0:8] + product[8:16]) + (product[16:24] + product[24:32]))


def core_step(count, rhs, earlier, smooth, image):
    def step(z, own, core, totals, later):
        at = z - 6
        later.put(smooth, at, own)
        later.put(image, at, core)
        new = [add_up(totals[0], own * rhs[at])]
        for i in range(count):
            new.append(add_up(totals[1 + i], core * earlier[i][at]))
        new.append(add_up(totals[1 + count], core * own))
        return tuple(new)

    return step


def inner_kernel(count, shape, *refs):
    folded, stiffness, rhs = refs[:3]
    earlier, refs = refs[3 : 3 + count], refs[3 + count :]
    tables = ()
    if not shape.last:
        tables, refs = refs[:14], refs[14:]
    smooth, image, sums = refs[:3]
    wide, solved = (None, None) if shape.last else refs[3:5]
    flux, weighted = refs[-2:]
    step = core_step(count, rhs, earlier, smooth, image)
    run = operate(
        lambda z: folded[z - 2], 10, (12, 48), flux, weighted, stiffness, wide, step
    )
    totals = run(12, 48, (jnp.zeros((8, 128), f32),) * (count + 2), True)
    for i, value in enumerate(totals):
        sums[i] = value
    if not shape.last:
        later = Later()
        for z in INNER:
            values = forward(wide[z : z + GROUP], tables)
            later.flush()
            later.put(solved, slice(z, z + GROUP), values)
        later.flush()


def outer_kernel(count, shape, *refs):
    folded, from_below, from_above, stiffness, rhs = refs[:5]
    earlier, refs = refs[5 : 5 + count], refs[5 + count :]
    smooth_in, image_in, sums_in = refs[:3]
    refs = refs[3:]
    wide = None
    if shape.last:
        parts, refs = refs[:count], refs[count:]
    else:
        wide_in, solved_in, inverse = refs[:3]
        tables, refs = refs[3:17], refs[17:]
        wide = refs[-4]
        for z in (10, 11, 44, 45):
            wide[z] = wide_in[z]
    smooth, image, sums = refs[:3]
    full, flux, weighted = refs[-3:]
    smooth[6:42] = smooth_in[6:42]
    image[6:42] = image_in[6:42]
    edge = 10 - shape.rim
    step = core_step(count, rhs, earlier, smooth, image)
    totals = tuple(sums_in[i] for i in range(count + 2))
    first_z = 6 if shape.last else 2
    for strip, base, shift in ((from_below, edge, 0), (from_above, 50, 46)):
        for z in range(14):
            layer = z + shift
            if not (4 if shape.last else 0) <= layer < (56 if shape.last else 60):
                continue
            at = layer - base
            inside = 2 <= layer < UZ - 2
            if 0 <= at < shape.rim:
                extra = unpack(strip[shape.rim], shape.halo, 2 * shape.halo, at)
                if inside:
                    full[z, :, :CX] = folded[layer - 2, :, :CX] + strip[at]
                    full[z, :, CX:] = folded[layer - 2, :, CX:] + extra
                else:
                    full[z, :, :CX] = strip[at]
                    full[z, :, CX:] = extra
            else:
                full[z] = folded[layer - 2]
        span = (first_z, 12) if shift == 0 else (48, UZ - first_z)
        run = operate(
            lambda z, shift=shift: full[z - shift], shift, span, flux, weighted, stiffness, wide, step
        )
        if shift == 0:
            if not shape.last:
                run(2, 6, 0, False)
            totals = run(6, 12, totals, True)
        else:
            totals = run(48, 54, totals, True)
            if not shape.last:
                run(54, 58, 0, False)
    if not shape.last:
        for i, value in enumerate(totals):
            sums[i] = value
        solved, low, high = refs[3:6]
        solved[12:44] = solved_in[12:44]
        later = Later()
        for z in OUTER:
            values = forward(wide[z : z + GROUP], tables)
            later.flush()
            later.put(solved, slice(z, z + GROUP), values)
        later.flush()
        finish_solve(solved, tables, inverse, Shape(count + 2 == ITERS), low, high)
        return
    lane = lanes()
    values = [part[i] for part in parts for i in range(part.shape[0])] + list(totals)
    gathered = jnp.zeros((8, 128), f32)
    for i, value in enumerate(values):
        value = jnp.sum(jnp.sum(value, axis=0, keepdims=True), axis=1, keepdims=True)
        gathered = jnp.where(lane == i, value, gathered)
    sums[...] = gathered


def start_columns_kernel(rhs, stiffness, low, high):
    for source, base, width in ((rhs, 0, 4), (stiffness, 8, 5)):
        per = 128 // width
        for first in range(0, CZ, per):
            for tile in range(4):
                packed = [None, None]
                for j in range(min(per, CZ - first)):
                    values = source[first + j, 8 * tile : 8 * tile + 8, :]
                    packed[0] = pack(packed[0], values, 0, width, j)
                    packed[1] = pack(packed[1], values, width, width, j)
                low[base + first // per * 4 + tile] = packed[0]
                high[base + first // per * 4 + tile] = packed[1]


def start_extra(from_left, from_right, base, width, z, tile):
    per, lane = 128 // width, lanes()
    at, j = base + z // per * 4 + tile, z % per
    left = spin(from_left[at], -(width + width * j), 1)
    right = spin(from_right[at], -width * j, 1)
    return jnp.where(lane >= 128 - width, left, jnp.where(lane < width, right, 0.0))


START_RHS, START_RHS_X = 0, 24
START_ST, START_ST_X, START_ONE, START_ONE_X = 26, 50, 52, 58
START_Y = 59


START_PLACES = ((0, 4, START_RHS, START_RHS_X), (8, 5, START_ST, START_ST_X))


def start_rows_kernel(rhs, stiffness, from_left, from_right, low, high, ends, pairs, ones):
    sub = subs()
    sources, strips = (rhs, stiffness), ((low, 0), (high, 3))
    for i, (base, width, _, _) in enumerate(START_PLACES):
        for n, (_, tile) in enumerate(strips):
            for z in range(CZ):
                ends[i, n, z] = start_extra(from_left, from_right, base, width, z, tile)

    def pairing(k, carry):
        for i, (_, _, main_at, _) in enumerate(START_PLACES):
            for n, (strip, tile) in enumerate(strips):
                rows = slice(8 * tile, 8 * tile + 8)
                for side in (0, 1):
                    if side == 0:
                        a, b = sources[i][2 * k, rows, :], sources[i][2 * k + 1, rows, :]
                    else:
                        a, b = ends[i, n, 2 * k], ends[i, n, 2 * k + 1]
                    if tile == 0:
                        pair = jnp.where(sub < 4, a, spin(b, 4, 0))
                    else:
                        pair = jnp.where(sub < 4, spin(a, -4, 0), b)
                    if side == 0:
                        strip[main_at + k] = pair
                    else:
                        pairs[i, n, k] = pair
        return carry

    lax.fori_loop(0, CZ // 2, pairing, 0, unroll=2)

    def single(k, carry):
        for n, (strip, tile) in enumerate(strips):
            for side in (0, 1):
                row = None
                for j in range(8):
                    if side == 0:
                        values = stiffness[8 * k + j, 8 * tile : 8 * tile + 8, :]
                    else:
                        values = ends[1, n, 8 * k + j]
                    moved = spin(values, j - (4 if tile == 0 else 3), 0)
                    row = jnp.where(sub == j, moved, 0.0 if row is None else row)
                if side == 0:
                    strip[START_ONE + k] = row
                else:
                    ones[n, k] = row
        return carry

    lax.fori_loop(0, CZ // 8, single, 0)
    for n, (strip, _) in enumerate(strips):
        for i, (_, width, _, extra_at) in enumerate(START_PLACES):
            per = 128 // (2 * width)
            for first in range(0, CZ // 2, per):
                extra = None
                for j in range(min(per, CZ // 2 - first)):
                    extra = pack(extra, pairs[i, n, first + j], width, 2 * width, j)
                strip[extra_at + first // per] = extra
        extra = None
        for k in range(CZ // 8):
            extra = pack(extra, ones[n, k], 5, 10, k)
        strip[START_ONE_X] = extra


def start_depth_kernel(
    rhs, stiffness, from_left, from_right, from_near, from_far, wide, stiff, low, high
):
    sub = subs()

    def pair_part(strip, main_at, extra_at, width, z, side):
        per = 128 // (2 * width)
        if side == 0:
            pair = strip[main_at + z // 2]
        else:
            k = z // 2
            pair = unpack(strip[extra_at + k // per], width, 2 * width, k % per)
        return pair

    def one_part(strip, z, side, row):
        values = strip[START_ONE + z // 8]
        if side == 1:
            values = unpack(strip[START_ONE_X], 5, 10, z // 8)
        return spin(values, row - z % 8, 0)

    for z in range(CZ):
        for side in (0, 1):
            columns = slice(128 * side, 128 * side + 128)
            for tile in range(4):
                rows = slice(8 * tile, 8 * tile + 8)
                if side == 0:
                    wide[z, rows, columns] = rhs[z, rows, :]
                    stiff[z + 6, rows, columns] = stiffness[z, rows, :]
                else:
                    wide[z, rows, columns] = start_extra(from_left, from_right, 0, 4, z, tile)
                    stiff[z + 6, rows, columns] = start_extra(
                        from_left, from_right, 8, 5, z, tile
                    )
            odd = z % 2
            far = pair_part(from_far, START_RHS, START_RHS_X, 4, z, side)
            near = pair_part(from_near, START_RHS, START_RHS_X, 4, z, side)
            far = spin(far, 4, 0) if odd else far
            near = near if odd else spin(near, 4, 0)
            wide[z, 32:40, columns] = jnp.where(sub < 4, far, near)
            far = pair_part(from_far, START_ST, START_ST_X, 5, z, side)
            far = spin(far, 4, 0) if odd else far
            one = one_part(from_far, z, side, 4)
            stiff[z + 6, 32:40, columns] = jnp.where(
                sub < 4, far, jnp.where(sub == 4, one, 0.0)
            )
            near = pair_part(from_near, START_ST, START_ST_X, 5, z, side)
            near = near if odd else spin(near, 4, 0)
            one = one_part(from_near, z, side, 3)
            stiff[z + 6, 40:48, columns] = jnp.where(
                sub >= 4, near, jnp.where(sub == 3, one, 0.0)
            )
    blank = jnp.zeros((8, 128), f32)
    for strip, wide_at, stiff_at in ((low, 0, 6), (high, CZ - 4, CZ + 1)):
        extra = None
        for i in range(4):
            strip[i, :40] = wide[wide_at + i, :, :CX]
            strip[i, 40:48] = blank
        for i in range(5):
            strip[4 + i] = stiff[stiff_at + i, :, :CX]
            extra = pack(extra, stiff[stiff_at + i, :, CX:], 5, 10, i)
        strip[9] = extra
        for tile in range(5):
            rows = slice(8 * tile, 8 * tile + 8)
            extra = strip[9, rows, :]
            for i in range(4):
                lane = lanes()
                moved = spin(wide[wide_at + i, rows, CX:], 4 + 64 + 8 * i, 1)
                inside = (lane >= 64 + 8 * i) & (lane < 72 + 8 * i)
                extra = jnp.where(inside, moved, extra)
            strip[9, rows, :] = extra


def start_inner_kernel(wide, *refs):
    tables, solved = refs[:14], refs[14]
    later = Later()
    for z in range(4, 52, GROUP):
        values = forward(wide[z - 4 : z], tables)
        later.flush()
        later.put(solved, slice(z, z + GROUP), values)
    later.flush()


def start_outer_kernel(from_below, from_above, stiff_in, solved_in, inverse, *refs):
    tables, (solved, stiff, low, high, edge) = refs[:14], refs[14:]
    solved[4:52] = solved_in[4:52]
    stiff[6:54] = stiff_in[6:54]
    for strip, first, stiff_at in ((from_below, 0, 1), (from_above, 52, 54)):
        lane = lax.broadcasted_iota(jnp.int32, (EY, CX), 1)
        for i in range(4):
            edge[i, :, :CX] = strip[i, :40]
            moved = spin(strip[9, :40], -(4 + 64 + 8 * i), 1)
            edge[i, :, CX:] = jnp.where((lane >= 124) | (lane < 4), moved, 0.0)
        for i in range(5):
            stiff[stiff_at + i, :, :CX] = strip[4 + i]
            stiff[stiff_at + i, :, CX:] = unpack(strip[9], 5, 10, i)
        solved[first : first + GROUP] = forward(edge[...], tables)
    finish_solve(solved, tables, inverse, Shape(False), low, high)


def weights(b, pair):
    sigma = [jnp.zeros((1, 1), f32)] * ITERS
    delta = None
    current = None
    for turn in range(ITERS):
        zeta = [jnp.ones((1, 1), f32)] + [-s for s in sigma[:turn]]
        following = sum(z * b[i] for i, z in enumerate(zeta))
        for i, z in enumerate(zeta):
            for j in range(turn):
                following = following - z * sigma[j] * pair[i, j]
        if turn == 0:
            delta = zeta
        else:
            ratio = following / current
            delta = [z + ratio * d for z, d in zip(zeta, delta + [jnp.zeros((1, 1), f32)])]
        current = following
        bending = sum(
            delta[i] * delta[j] * pair[i, j] for i in range(turn + 1) for j in range(turn + 1)
        )
        step = current / bending
        sigma = [
            s + step * d for s, d in zip(sigma, delta + [jnp.zeros((1, 1), f32)] * (ITERS - turn - 1))
        ]
    return sigma


def combine_kernel(sums, rhs, u0, u1, u2, w0, w1, w2, answer, rest):
    picked = [
        jnp.sum(jnp.where(lanes()[:1] == i, sums[:1], 0.0), axis=1, keepdims=True)
        for i in range(ITERS * (ITERS + 3) // 2)
    ]
    b, pair, at = [], {}, 0
    for j in range(ITERS):
        b.append(picked[at])
        for i in range(j + 1):
            pair[i, j] = pair[j, i] = picked[at + 1 + i]
        at += j + 2
    s = weights(b, pair)

    def step(z, carry):
        answer[z] = s[0] * u0[z] + s[1] * u1[z] + s[2] * u2[z]
        rest[z] = rhs[z] - (s[0] * w0[z] + s[1] * w1[z] + s[2] * w2[z])
        return carry

    lax.fori_loop(0, CZ, step, 0, unroll=4)


VMEM = pl.BlockSpec(memory_space=pltpu.VMEM)


def call(kernel, shapes, operands, scratch=(), cost=2.0):
    return pl.pallas_call(
        kernel,
        out_shape=[jax.ShapeDtypeStruct(shape, f32) for shape in shapes],
        in_specs=[VMEM] * len(operands),
        out_specs=[VMEM] * len(shapes),
        scratch_shapes=[pltpu.VMEM(shape, f32) for shape in scratch],
        cost_estimate=pl.CostEstimate(
            flops=0, bytes_accessed=int(cost * 3.6e6), transcendentals=0
        ),
        compiler_params=pltpu.CompilerParams(vmem_limit_bytes=20 * 2**20),
    )(*operands)


def shifted(block, axis, step):
    count = lax.axis_size(axis)
    return lax.ppermute(block, axis, [(i, (i + step) % count) for i in range(count)])


def swap(low, high, axis):
    return shifted(high, axis, 1), shifted(low, axis, -1)


def ring(values, axes, count, low, size):
    parts = []
    for step in range(1, size):
        route = []
        for i in range(count):
            place = i // low % size
            route.append((i, i + ((place + step) % size - place) * low))
        parts.append(lax.ppermute(values, axes, route))
    return values + sum(parts[1:], parts[0])


def total(values):
    values = ring(values, "gy", 4, 1, 2)
    values = ring(values, ("gx", "gy"), 32, 2, 4)
    values = ring(values, "gx", 8, 2, 4)
    return ring(values, "gz", 4, 1, 4)


CORE = (CZ, CY, CX)
FIELD = (EZ, EY, UX)


def per_device(rhs_field, stiffness):
    *tables, inverse = solve_tables()
    strips = call(start_columns_kernel, [(16, 8, 128)] * 2, [rhs_field, stiffness])
    columns = swap(*strips, "gx")
    fields = [rhs_field, stiffness, *columns]
    strips = call(
        start_rows_kernel,
        [(START_Y, 8, 128)] * 2,
        fields,
        [(2, 2, CZ, 8, 128), (2, 2, CZ // 2, 8, 128), (2, CZ // 8, 8, 128)],
    )
    rows = swap(*strips, "gy")
    wide, stiff, *strips = call(
        start_depth_kernel,
        [(CZ, EY, UX), (UZ, UY, UX)] + [(10, UY, CX)] * 2,
        [*fields, *rows],
    )
    depths = swap(*strips, "gz")
    solved = call(start_inner_kernel, [FIELD], [wide, *tables], cost=4.0)[0]
    shape = Shape(False)
    solved, stiff, *strips = call(
        start_outer_kernel,
        [FIELD, (UZ, UY, UX)] + [(shape.x_tiles, 8, 128)] * 2,
        [*depths, stiff, solved, inverse, *tables],
        [(4, EY, UX)],
        cost=6.0,
    )
    smooth, image, sums = [], [], []
    for turn in range(ITERS):
        shape = Shape(turn + 1 == ITERS)
        columns = swap(*strips, "gx")
        strips = call(
            functools.partial(row_strips_kernel, shape), [(shape.y_tiles, 8, 128)] * 2, [solved]
        )
        rows = swap(*strips, "gy")
        strips = call(
            functools.partial(corners_kernel, shape), [(shape.c_tiles, 8, 128)] * 2, columns, cost=0.5
        )
        corners = swap(*strips, "gy")
        widened = call(
            functools.partial(widen_kernel, shape), [(EZ, UY, UX)], [solved, *columns]
        )[0]
        folded, *strips = call(
            functools.partial(depth_strips_kernel, shape),
            [(EZ, UY, UX)] + [(shape.rim + 1, UY, CX)] * 2,
            [widened, *rows, *corners],
            [(4, 2 * shape.x_groups, 8, 128)],
        )
        depths = swap(*strips, "gz")
        products = (turn + 2, 8, 128)
        outs = [CORE, CORE, products]
        if not shape.last:
            outs += [FIELD, FIELD]
        own, core, part, *fields = call(
            functools.partial(inner_kernel, turn, shape),
            outs,
            [folded, stiff, rhs_field, *smooth] + ([] if shape.last else tables),
            [(40, UY, UX)] * 2,
            cost=6.0,
        )
        operands = [folded, *depths, stiff, rhs_field, *smooth]
        operands += [own, core, part]
        scratch = [(14, UY, UX)] * 3
        if shape.last:
            operands += sums
            outs = [CORE, CORE, (8, 128)]
        else:
            operands += [*fields, inverse, *tables]
            following = Shape(turn + 2 == ITERS)
            outs = [CORE, CORE, products, FIELD] + [(following.x_tiles, 8, 128)] * 2
            scratch = [FIELD] + scratch
        own, core, part, *rest = call(
            functools.partial(outer_kernel, turn, shape),
            outs,
            operands,
            scratch,
            cost=8.0,
        )
        if rest:
            solved, *strips = rest
        smooth.append(own)
        image.append(core)
        sums.append(part)
    operands = [total(sums[-1]), rhs_field, *smooth, *image]
    return tuple(call(combine_kernel, [CORE] * 2, operands))


def solution(mesh):
    in_specs = (P("gz", "gy", "gx"), P("gz", "gy", "gx"))
    out_specs = (P("gz", "gy", "gx"), P("gz", "gy", "gx"))
    return jax.shard_map(
        per_device, mesh=mesh, in_specs=in_specs, out_specs=out_specs, check_vma=False
    )
```

```python
import functools

import jax
import jax.numpy as jnp
import numpy as np
from jax import lax
from jax.experimental import pallas as pl
from jax.experimental.pallas import tpu as pltpu
from jax.sharding import PartitionSpec as P

OV = 4
ITERS = 3
CZ, CY, CX = 48, 32, 128
EZ, EY, EX = CZ + 2 * OV, CY + 2 * OV, CX + 2 * OV
HALF = EZ // 2
UZ, UY, UX = CZ + 12, 48, 256
GROUP = 4
CHUNK = 2
CHUNK_UNROLL = 2
INNER = range(12, 44, GROUP)
OUTER = [z for z in range(0, EZ, GROUP) if z not in INNER]


class Shape:
    def __init__(self, last):
        self.rim = 6 if last else 10
        self.halo = 4 if last else 6
        self.width = 4 + self.halo
        self.per = 128 // self.width
        self.x_tiles = -(-EZ // self.per) * 5
        self.x_groups = self.x_tiles // 5
        self.extra_a = EZ if last else EZ + EZ // 4
        self.extra_b = self.extra_a + -(-EZ // 16)
        self.y_tiles = self.extra_b + (0 if last else 1)
        self.cut_near = 4 if last else 2
        self.c_tiles = 2 * self.x_groups + (0 if last else -(-self.x_groups // 2))
        self.last = last


mass_term = 1e-05
split_term = 0.5
bend_mean = 0.1
f32, bf16 = jnp.float32, jnp.bfloat16


def sine_table(length):
    places = np.arange(1, length + 1, dtype=np.float64)
    return np.sqrt(2.0 / (length + 1)) * np.sin(
        np.pi * places[:, None] * places[None, :] / (length + 1)
    )


def eigen_line(length):
    places = np.arange(1, length + 1, dtype=np.float64)
    return 2.0 - 2.0 * np.cos(np.pi * places / (length + 1))


def halves(table):
    high = np.asarray(table, np.float32).astype(jnp.bfloat16)
    low = (np.asarray(table, np.float64) - high.astype(np.float64)).astype(jnp.bfloat16)
    return [jnp.asarray(high), jnp.asarray(low)]


def solve_tables():
    column = np.zeros((UX, UX))
    full = sine_table(EX)
    for lane in range(UX):
        place = lane + OV if lane < CX + OV else lane - UX + OV
        if 0 <= place < EX:
            column[lane, :EX] = full[place]
    rows = np.roll(sine_table(EY), -OV, axis=0)
    row_fwd = np.kron(np.eye(2), rows.T)
    depth = sine_table(EZ)
    even = np.kron(depth[0::2, :HALF], np.eye(8))
    odd = np.kron(depth[1::2, :HALF], np.eye(8))
    order = np.concatenate([np.arange(0, EZ, 2), np.arange(1, EZ, 2)])
    spectrum = (
        eigen_line(EZ)[order][:, None, None]
        + eigen_line(EY)[None, :, None]
        + eigen_line(EX)[None, None, :]
    )
    inverse = np.zeros((EZ, EY, UX), np.float32)
    inverse[:, :, :EX] = 1.0 / (mass_term + bend_mean * spectrum**2 + split_term * spectrum)
    tables = []
    for table in (column, column.T):
        tables += halves(table)
    for table in (row_fwd, row_fwd.T):
        high, low = halves(table)
        tables.append(jnp.concatenate([high, low, high], axis=1))
    for table in (even, odd, even.T, odd.T):
        tables += halves(table)
    return tables + [jnp.asarray(inverse)]


def cut(values):
    high = values.astype(bf16)
    return high, (values - high.astype(f32)).astype(bf16)


def mul(a, b):
    return lax.dot_general(a, b, (((1,), (0,)), ((), ())), preferred_element_type=f32)


def mul3(a, b):
    return mul(a[0], b[0]) + (mul(a[0], b[1]) + mul(a[1], b[0]))


def lanes():
    return lax.broadcasted_iota(jnp.int32, (8, 128), 1)


def subs():
    return lax.broadcasted_iota(jnp.int32, (8, 128), 0)


def spin(values, shift, axis):
    size = values.shape[axis]
    shift = shift % size
    return values if shift == 0 else pltpu.roll(values, shift, axis)


def pack(into, values, lead, width, at):
    lane = lax.broadcasted_iota(jnp.int32, values.shape, 1)
    inside = (lane >= width * at) & (lane < width * (at + 1))
    moved = spin(values, lead + width * at, 1)
    return jnp.where(inside, moved, 0.0 if into is None else into)


def unpack(packed, lead, width, at):
    moved = spin(packed, -(lead + width * at), 1)
    lane = lax.broadcasted_iota(jnp.int32, packed.shape, 1)
    return jnp.where((lane >= 128 - lead) | (lane < width - lead), moved, 0.0)


def row_product(table, values):
    out, step = [], 2 * EY
    for at in range(0, values.shape[0], step):
        high, low = cut(values[at : at + step])
        out.append(mul(table, jnp.concatenate([high, high, low], axis=0)))
    return jnp.concatenate(out, axis=0)


def forward(values, tables):
    values = mul3(cut(values.reshape(GROUP * EY, UX)), (tables[0][...], tables[1][...]))
    return row_product(tables[4][...], values).reshape(GROUP, EY, UX)


def finish_solve(solved, tables, inverse, shape, low, high):
    column, row = (tables[2][...], tables[3][...]), tables[5][...]
    even_fwd, odd_fwd, even_bwd, odd_bwd = [
        (tables[i][...], tables[i + 1][...]) for i in (6, 8, 10, 12)
    ]
    for tile in range(EY // 8):
        rows = slice(8 * tile, 8 * tile + 8)
        near = solved[:HALF, rows, :]
        far = jnp.concatenate([solved[EZ - 1 - i : EZ - i, rows, :] for i in range(HALF)], axis=0)
        even = cut((near + far).reshape(8 * HALF, UX))
        odd = cut((near - far).reshape(8 * HALF, UX))
        even = mul3(even_fwd, even) * inverse[:HALF, rows, :].reshape(8 * HALF, UX)
        odd = mul3(odd_fwd, odd) * inverse[HALF:, rows, :].reshape(8 * HALF, UX)
        even = mul3(even_bwd, cut(even)).reshape(HALF, 8, UX)
        odd = mul3(odd_bwd, cut(odd)).reshape(HALF, 8, UX)
        solved[:HALF, rows, :] = even + odd
        far = even - odd
        for i in range(HALF):
            solved[EZ - 1 - i, rows, :] = far[i]

    later = Later()
    for z in range(0, EZ, GROUP):
        values = cut(row_product(row, solved[z : z + GROUP].reshape(GROUP * EY, UX)))
        values = mul3(values, column).reshape(GROUP, EY, UX)
        later.flush()
        later.put(solved, slice(z, z + GROUP), values)
    later.flush()

    lane = lanes()
    for first in range(0, EZ, shape.per):
        for tile in range(5):
            rows = slice(8 * tile, 8 * tile + 8)
            packed = [None, None]
            for j in range(min(shape.per, EZ - first)):
                near, far = solved[first + j, rows, :CX], solved[first + j, rows, CX:]
                packed[0] = pack(
                    packed[0], jnp.where(lane >= 124, far, near), OV, shape.width, j
                )
                packed[1] = pack(
                    packed[1],
                    jnp.where(lane >= 128 - shape.halo, near, far),
                    shape.halo,
                    shape.width,
                    j,
                )
            low[first // shape.per * 5 + tile] = packed[0]
            high[first // shape.per * 5 + tile] = packed[1]


def column_folded(solved, from_left, from_right, shape, z, tile):
    lane, rows = lanes(), slice(8 * tile, 8 * tile + 8)
    at, j = z // shape.per * 5 + tile, z % shape.per
    left = unpack(from_left[at], shape.halo, shape.width, j)
    right = unpack(from_right[at], OV, shape.width, j)
    return (
        solved[z, rows, :CX] + jnp.where(lane < 64, left, right),
        solved[z, rows, CX:] + jnp.where(lane < 64, right, left),
    )


class Later:
    def __init__(self):
        self.kept = []

    def put(self, ref, index, values):
        self.kept.append((ref, index, values))

    def flush(self):
        for ref, index, values in self.kept:
            ref[index] = values
        self.kept = []


def row_strips_kernel(shape, solved, low, high):
    sub = subs()
    for strip, cut_at, upper, lower, keep in (
        (low, 4, 4, 0, 4),
        (high, shape.cut_near, 3, 4, 2),
    ):
        extra_a = extra_b = None
        for quad in range(EZ // 4):
            rest = [None, None]
            for j in range(4):
                z = 4 * quad + j
                for side in (0, 1):
                    columns = slice(128 * side, 128 * side + 128)
                    lower_tile = solved[z, 8 * lower : 8 * lower + 8, columns]
                    upper_tile = solved[z, 8 * upper : 8 * upper + 8, columns]
                    main = jnp.where(sub >= cut_at, upper_tile, lower_tile)
                    if side == 0:
                        strip[z] = main
                    else:
                        extra_a = pack(extra_a if z % 16 else None, main, OV, 2 * OV, z % 16)
                        if z % 16 == 15 or z + 1 == EZ:
                            strip[shape.extra_a + z // 16] = extra_a
                    if not shape.last:
                        inside = (sub >= 2 * j) & (sub < 2 * j + 2)
                        moved = spin(lower_tile, 2 * j - keep, 0)
                        rest[side] = jnp.where(inside, moved, rest[side] if j else 0.0)
            if not shape.last:
                strip[EZ + quad] = rest[0]
                extra_b = pack(extra_b, rest[1], OV, 2 * OV, quad)
        if not shape.last:
            strip[shape.extra_b] = extra_b


def corners_kernel(shape, from_left, from_right, low, high):
    sub, groups = subs(), shape.x_groups
    for strip, cut_at, upper, lower, keep in (
        (low, 4, 4, 0, 4),
        (high, shape.cut_near, 3, 4, 2),
    ):
        rest = None
        for k in range(2 * groups):
            source = (from_left, from_right)[k // groups]
            lower_tile = source[k % groups * 5 + lower]
            strip[k] = jnp.where(sub >= cut_at, source[k % groups * 5 + upper], lower_tile)
            if shape.last:
                continue
            j = k % 4
            inside = (sub >= 2 * j) & (sub < 2 * j + 2)
            rest = jnp.where(inside, spin(lower_tile, 2 * j - keep, 0), rest if j else 0.0)
            if j == 3 or k + 1 == 2 * groups:
                strip[2 * groups + k // 4] = rest


def widen_kernel(shape, solved, from_left, from_right, folded):
    sub = subs()
    for z in range(EZ):
        for tile in range(5):
            values = column_folded(solved, from_left, from_right, shape, z, tile)
            for side in (0, 1):
                columns = slice(128 * side, 128 * side + 128)
                value = values[side]
                if tile == 4:
                    folded[z, 40:48, columns] = jnp.where(sub >= 4, value, 0.0)
                    value = jnp.where(sub < 4, value, 0.0)
                folded[z, 8 * tile : 8 * tile + 8, columns] = value


def row_part(strip, shape, z, side, keep):
    sub = subs()
    if side == 0:
        main = strip[z]
    else:
        main = unpack(strip[shape.extra_a + z // 16], OV, 2 * OV, z % 16)
    if shape.last:
        return main, jnp.zeros((8, 128), f32)
    if side == 0:
        rest = strip[EZ + z // 4]
    else:
        rest = unpack(strip[shape.extra_b], OV, 2 * OV, z // 4)
    moved = spin(rest, keep - 2 * (z % 4), 0)
    return main, jnp.where((sub >= keep) & (sub < keep + 2), moved, 0.0)


def depth_strips_kernel(
    shape, widened, from_near, from_far, corner_near, corner_far, folded, low, high, corners
):
    sub, lane, cut_at = subs(), lanes(), shape.cut_near
    groups = shape.x_groups
    for k in range(2 * groups):
        for strip, keep in ((corner_near, 2), (corner_far, 4)):
            main, rest = strip[k], 0.0
            if not shape.last:
                moved = spin(strip[2 * groups + k // 4], keep - 2 * (k % 4), 0)
                rest = jnp.where((sub >= keep) & (sub < keep + 2), moved, 0.0)
            if keep == 2:
                corners[0, k] = jnp.where(sub < cut_at, main, rest)
                corners[1, k] = jnp.where(sub >= cut_at, main, 0.0)
            else:
                corners[2, k] = jnp.where(sub >= 4, main, 0.0)
                corners[3, k] = jnp.where(sub < 4, main, rest)
    for z in range(EZ):
        group, j = z // shape.per, z % shape.per
        new = {}
        for side in (0, 1):
            main, rest = row_part(from_near, shape, z, side, 2)
            new[0, side] = jnp.where(sub < cut_at, main, rest)
            new[5, side] = jnp.where(sub >= cut_at, main, 0.0)
            main, rest = row_part(from_far, shape, z, side, 4)
            new[3, side] = jnp.where(sub >= 4, main, 0.0)
            new[4, side] = jnp.where(sub < 4, main, rest)
        for at, tile in enumerate((0, 5, 3, 4)):
            left = unpack(corners[at, group], shape.halo, shape.width, j)
            right = unpack(corners[at, groups + group], OV, shape.width, j)
            new[tile, 0] += jnp.where(lane < 64, left, right)
            new[tile, 1] += jnp.where(lane < 64, right, left)
        for side in (0, 1):
            columns = slice(128 * side, 128 * side + 128)
            for tile in range(6):
                rows = slice(8 * tile, 8 * tile + 8)
                value = widened[z, rows, columns]
                if (tile, side) in new:
                    value = value + new[tile, side]
                folded[z, rows, columns] = value
    for strip, start in ((low, 0), (high, EZ - shape.rim)):
        extra = None
        for i in range(shape.rim):
            strip[i] = folded[start + i, :, :CX]
            extra = pack(extra, folded[start + i, :, CX:], shape.halo, 2 * shape.halo, i)
        strip[shape.rim] = extra


def laplace(below, centre, above):
    beside = below + above
    beside = beside + (pltpu.roll(centre, 1, 0) + pltpu.roll(centre, UY - 1, 0))
    beside = beside + (pltpu.roll(centre, 1, 1) + pltpu.roll(centre, UX - 1, 1))
    return 6.0 * centre - beside


def operate(get, shift, span, flux, weighted, stiffness, wide, core):
    start, stop = span

    def chunks(body, start, stop, carry):
        size = CHUNK
        while (stop - start) % size:
            size -= 1
        return lax.fori_loop(
            0,
            (stop - start) // size,
            lambda i, c: body(start + size * i, size, c),
            carry,
            unroll=CHUNK_UNROLL,
        )

    def first(at, size, carry):
        later = Later()
        for z in [at + i for i in range(size)]:
            values = laplace(get(z - 1), get(z), get(z + 1))
            later.put(flux, z - shift, values)
            later.put(weighted, z - shift, stiffness[z] * values)
        later.flush()
        return carry

    chunks(first, start - 1, stop + 1, 0)
    sub = lax.broadcasted_iota(jnp.int32, (8, UX), 0)

    def second(base, size, carry, use_core):
        later = Later()
        for z in [base + i for i in range(size)]:
            own = get(z)
            at = z - shift
            values = laplace(weighted[at - 1], weighted[at], weighted[at + 1])
            values = mass_term * own + values + split_term * flux[at]
            if wide is not None:
                later.put(wide, (z - 2, slice(0, CY)), values[:CY])
                last = jnp.where(sub < 4, values[CY : CY + 8], values[CY + 8 :])
                later.put(wide, (z - 2, slice(CY, EY)), last)
            if use_core:
                carry = core(z, own[:CY, :CX], values[:CY, :CX], carry, later)
        later.flush()
        return carry

    return lambda first_z, last_z, carry, use_core: chunks(
        lambda z, size, c: second(z, size, c, use_core), first_z, last_z, carry
    )


def add_up(total, product):
    return total + ((product[0:8] + product[8:16]) + (product[16:24] + product[24:32]))


def core_step(count, rhs, earlier, smooth, image):
    def step(z, own, core, totals, later):
        at = z - 6
        later.put(smooth, at, own)
        later.put(image, at, core)
        new = [add_up(totals[0], own * rhs[at])]
        for i in range(count):
            new.append(add_up(totals[1 + i], core * earlier[i][at]))
        new.append(add_up(totals[1 + count], core * own))
        return tuple(new)

    return step


def inner_kernel(count, shape, *refs):
    folded, stiffness, rhs = refs[:3]
    earlier, refs = refs[3 : 3 + count], refs[3 + count :]
    tables = ()
    if not shape.last:
        tables, refs = refs[:14], refs[14:]
    smooth, image, sums = refs[:3]
    wide, solved = (None, None) if shape.last else refs[3:5]
    flux, weighted = refs[-2:]
    step = core_step(count, rhs, earlier, smooth, image)
    run = operate(
        lambda z: folded[z - 2], 10, (12, 48), flux, weighted, stiffness, wide, step
    )
    totals = run(12, 48, (jnp.zeros((8, 128), f32),) * (count + 2), True)
    for i, value in enumerate(totals):
        sums[i] = value
    if not shape.last:
        later = Later()
        for z in INNER:
            values = forward(wide[z : z + GROUP], tables)
            later.flush()
            later.put(solved, slice(z, z + GROUP), values)
        later.flush()


def outer_kernel(count, shape, *refs):
    folded, from_below, from_above, stiffness, rhs = refs[:5]
    earlier, refs = refs[5 : 5 + count], refs[5 + count :]
    smooth_in, image_in, sums_in = refs[:3]
    refs = refs[3:]
    wide = None
    if shape.last:
        parts, refs = refs[:count], refs[count:]
    else:
        wide_in, solved_in, inverse = refs[:3]
        tables, refs = refs[3:17], refs[17:]
        wide = refs[-4]
        for z in (10, 11, 44, 45):
            wide[z] = wide_in[z]
    smooth, image, sums = refs[:3]
    full, flux, weighted = refs[-3:]
    smooth[6:42] = smooth_in[6:42]
    image[6:42] = image_in[6:42]
    edge = 10 - shape.rim
    step = core_step(count, rhs, earlier, smooth, image)
    totals = tuple(sums_in[i] for i in range(count + 2))
    first_z = 6 if shape.last else 2
    for strip, base, shift in ((from_below, edge, 0), (from_above, 50, 46)):
        for z in range(14):
            layer = z + shift
            if not (4 if shape.last else 0) <= layer < (56 if shape.last else 60):
                continue
            at = layer - base
            inside = 2 <= layer < UZ - 2
            if 0 <= at < shape.rim:
                extra = unpack(strip[shape.rim], shape.halo, 2 * shape.halo, at)
                if inside:
                    full[z, :, :CX] = folded[layer - 2, :, :CX] + strip[at]
                    full[z, :, CX:] = folded[layer - 2, :, CX:] + extra
                else:
                    full[z, :, :CX] = strip[at]
                    full[z, :, CX:] = extra
            else:
                full[z] = folded[layer - 2]
        span = (first_z, 12) if shift == 0 else (48, UZ - first_z)
        run = operate(
            lambda z, shift=shift: full[z - shift], shift, span, flux, weighted, stiffness, wide, step
        )
        if shift == 0:
            if not shape.last:
                run(2, 6, 0, False)
            totals = run(6, 12, totals, True)
        else:
            totals = run(48, 54, totals, True)
            if not shape.last:
                run(54, 58, 0, False)
    if not shape.last:
        for i, value in enumerate(totals):
            sums[i] = value
        solved, low, high = refs[3:6]
        solved[12:44] = solved_in[12:44]
        later = Later()
        for z in OUTER:
            values = forward(wide[z : z + GROUP], tables)
            later.flush()
            later.put(solved, slice(z, z + GROUP), values)
        later.flush()
        finish_solve(solved, tables, inverse, Shape(count + 2 == ITERS), low, high)
        return
    lane = lanes()
    values = [part[i] for part in parts for i in range(part.shape[0])] + list(totals)
    gathered = jnp.zeros((8, 128), f32)
    for i, value in enumerate(values):
        value = jnp.sum(jnp.sum(value, axis=0, keepdims=True), axis=1, keepdims=True)
        gathered = jnp.where(lane == i, value, gathered)
    sums[...] = gathered


def start_columns_kernel(rhs, stiffness, low, high):
    for source, base, width in ((rhs, 0, 4), (stiffness, 8, 5)):
        per = 128 // width
        for first in range(0, CZ, per):
            for tile in range(4):
                packed = [None, None]
                for j in range(min(per, CZ - first)):
                    values = source[first + j, 8 * tile : 8 * tile + 8, :]
                    packed[0] = pack(packed[0], values, 0, width, j)
                    packed[1] = pack(packed[1], values, width, width, j)
                low[base + first // per * 4 + tile] = packed[0]
                high[base + first // per * 4 + tile] = packed[1]


def start_extra(from_left, from_right, base, width, z, tile):
    per, lane = 128 // width, lanes()
    at, j = base + z // per * 4 + tile, z % per
    left = spin(from_left[at], -(width + width * j), 1)
    right = spin(from_right[at], -width * j, 1)
    return jnp.where(lane >= 128 - width, left, jnp.where(lane < width, right, 0.0))


START_RHS, START_RHS_X = 0, 24
START_ST, START_ST_X, START_ONE, START_ONE_X = 26, 50, 52, 58
START_Y = 59


START_PLACES = ((0, 4, START_RHS, START_RHS_X), (8, 5, START_ST, START_ST_X))


def start_rows_kernel(rhs, stiffness, from_left, from_right, low, high, ends, pairs, ones):
    sub = subs()
    sources, strips = (rhs, stiffness), ((low, 0), (high, 3))
    for i, (base, width, _, _) in enumerate(START_PLACES):
        for n, (_, tile) in enumerate(strips):
            for z in range(CZ):
                ends[i, n, z] = start_extra(from_left, from_right, base, width, z, tile)

    def pairing(k, carry):
        for i, (_, _, main_at, _) in enumerate(START_PLACES):
            for n, (strip, tile) in enumerate(strips):
                rows = slice(8 * tile, 8 * tile + 8)
                for side in (0, 1):
                    if side == 0:
                        a, b = sources[i][2 * k, rows, :], sources[i][2 * k + 1, rows, :]
                    else:
                        a, b = ends[i, n, 2 * k], ends[i, n, 2 * k + 1]
                    if tile == 0:
                        pair = jnp.where(sub < 4, a, spin(b, 4, 0))
                    else:
                        pair = jnp.where(sub < 4, spin(a, -4, 0), b)
                    if side == 0:
                        strip[main_at + k] = pair
                    else:
                        pairs[i, n, k] = pair
        return carry

    lax.fori_loop(0, CZ // 2, pairing, 0, unroll=2)

    def single(k, carry):
        for n, (strip, tile) in enumerate(strips):
            for side in (0, 1):
                row = None
                for j in range(8):
                    if side == 0:
                        values = stiffness[8 * k + j, 8 * tile : 8 * tile + 8, :]
                    else:
                        values = ends[1, n, 8 * k + j]
                    moved = spin(values, j - (4 if tile == 0 else 3), 0)
                    row = jnp.where(sub == j, moved, 0.0 if row is None else row)
                if side == 0:
                    strip[START_ONE + k] = row
                else:
                    ones[n, k] = row
        return carry

    lax.fori_loop(0, CZ // 8, single, 0)
    for n, (strip, _) in enumerate(strips):
        for i, (_, width, _, extra_at) in enumerate(START_PLACES):
            per = 128 // (2 * width)
            for first in range(0, CZ // 2, per):
                extra = None
                for j in range(min(per, CZ // 2 - first)):
                    extra = pack(extra, pairs[i, n, first + j], width, 2 * width, j)
                strip[extra_at + first // per] = extra
        extra = None
        for k in range(CZ // 8):
            extra = pack(extra, ones[n, k], 5, 10, k)
        strip[START_ONE_X] = extra


def start_depth_kernel(
    rhs, stiffness, from_left, from_right, from_near, from_far, wide, stiff, low, high
):
    sub = subs()

    def pair_part(strip, main_at, extra_at, width, z, side):
        per = 128 // (2 * width)
        if side == 0:
            pair = strip[main_at + z // 2]
        else:
            k = z // 2
            pair = unpack(strip[extra_at + k // per], width, 2 * width, k % per)
        return pair

    def one_part(strip, z, side, row):
        values = strip[START_ONE + z // 8]
        if side == 1:
            values = unpack(strip[START_ONE_X], 5, 10, z // 8)
        return spin(values, row - z % 8, 0)

    for z in range(CZ):
        for side in (0, 1):
            columns = slice(128 * side, 128 * side + 128)
            for tile in range(4):
                rows = slice(8 * tile, 8 * tile + 8)
                if side == 0:
                    wide[z, rows, columns] = rhs[z, rows, :]
                    stiff[z + 6, rows, columns] = stiffness[z, rows, :]
                else:
                    wide[z, rows, columns] = start_extra(from_left, from_right, 0, 4, z, tile)
                    stiff[z + 6, rows, columns] = start_extra(
                        from_left, from_right, 8, 5, z, tile
                    )
            odd = z % 2
            far = pair_part(from_far, START_RHS, START_RHS_X, 4, z, side)
            near = pair_part(from_near, START_RHS, START_RHS_X, 4, z, side)
            far = spin(far, 4, 0) if odd else far
            near = near if odd else spin(near, 4, 0)
            wide[z, 32:40, columns] = jnp.where(sub < 4, far, near)
            far = pair_part(from_far, START_ST, START_ST_X, 5, z, side)
            far = spin(far, 4, 0) if odd else far
            one = one_part(from_far, z, side, 4)
            stiff[z + 6, 32:40, columns] = jnp.where(
                sub < 4, far, jnp.where(sub == 4, one, 0.0)
            )
            near = pair_part(from_near, START_ST, START_ST_X, 5, z, side)
            near = near if odd else spin(near, 4, 0)
            one = one_part(from_near, z, side, 3)
            stiff[z + 6, 40:48, columns] = jnp.where(
                sub >= 4, near, jnp.where(sub == 3, one, 0.0)
            )
    blank = jnp.zeros((8, 128), f32)
    for strip, wide_at, stiff_at in ((low, 0, 6), (high, CZ - 4, CZ + 1)):
        extra = None
        for i in range(4):
            strip[i, :40] = wide[wide_at + i, :, :CX]
            strip[i, 40:48] = blank
        for i in range(5):
            strip[4 + i] = stiff[stiff_at + i, :, :CX]
            extra = pack(extra, stiff[stiff_at + i, :, CX:], 5, 10, i)
        strip[9] = extra
        for tile in range(5):
            rows = slice(8 * tile, 8 * tile + 8)
            extra = strip[9, rows, :]
            for i in range(4):
                lane = lanes()
                moved = spin(wide[wide_at + i, rows, CX:], 4 + 64 + 8 * i, 1)
                inside = (lane >= 64 + 8 * i) & (lane < 72 + 8 * i)
                extra = jnp.where(inside, moved, extra)
            strip[9, rows, :] = extra


def start_inner_kernel(wide, *refs):
    tables, solved = refs[:14], refs[14]
    later = Later()
    for z in range(4, 52, GROUP):
        values = forward(wide[z - 4 : z], tables)
        later.flush()
        later.put(solved, slice(z, z + GROUP), values)
    later.flush()


def start_outer_kernel(from_below, from_above, stiff_in, solved_in, inverse, *refs):
    tables, (solved, stiff, low, high, edge) = refs[:14], refs[14:]
    solved[4:52] = solved_in[4:52]
    stiff[6:54] = stiff_in[6:54]
    for strip, first, stiff_at in ((from_below, 0, 1), (from_above, 52, 54)):
        lane = lax.broadcasted_iota(jnp.int32, (EY, CX), 1)
        for i in range(4):
            edge[i, :, :CX] = strip[i, :40]
            moved = spin(strip[9, :40], -(4 + 64 + 8 * i), 1)
            edge[i, :, CX:] = jnp.where((lane >= 124) | (lane < 4), moved, 0.0)
        for i in range(5):
            stiff[stiff_at + i, :, :CX] = strip[4 + i]
            stiff[stiff_at + i, :, CX:] = unpack(strip[9], 5, 10, i)
        solved[first : first + GROUP] = forward(edge[...], tables)
    finish_solve(solved, tables, inverse, Shape(False), low, high)


def weights(b, pair):
    sigma = [jnp.zeros((1, 1), f32)] * ITERS
    delta = None
    current = None
    for turn in range(ITERS):
        zeta = [jnp.ones((1, 1), f32)] + [-s for s in sigma[:turn]]
        following = sum(z * b[i] for i, z in enumerate(zeta))
        for i, z in enumerate(zeta):
            for j in range(turn):
                following = following - z * sigma[j] * pair[i, j]
        if turn == 0:
            delta = zeta
        else:
            ratio = following / current
            delta = [z + ratio * d for z, d in zip(zeta, delta + [jnp.zeros((1, 1), f32)])]
        current = following
        bending = sum(
            delta[i] * delta[j] * pair[i, j] for i in range(turn + 1) for j in range(turn + 1)
        )
        step = current / bending
        sigma = [
            s + step * d for s, d in zip(sigma, delta + [jnp.zeros((1, 1), f32)] * (ITERS - turn - 1))
        ]
    return sigma


def combine_kernel(sums, rhs, u0, u1, u2, w0, w1, w2, answer, rest):
    picked = [
        jnp.sum(jnp.where(lanes()[:1] == i, sums[:1], 0.0), axis=1, keepdims=True)
        for i in range(ITERS * (ITERS + 3) // 2)
    ]
    b, pair, at = [], {}, 0
    for j in range(ITERS):
        b.append(picked[at])
        for i in range(j + 1):
            pair[i, j] = pair[j, i] = picked[at + 1 + i]
        at += j + 2
    s = weights(b, pair)

    def step(z, carry):
        answer[z] = s[0] * u0[z] + s[1] * u1[z] + s[2] * u2[z]
        rest[z] = rhs[z] - (s[0] * w0[z] + s[1] * w1[z] + s[2] * w2[z])
        return carry

    lax.fori_loop(0, CZ, step, 0, unroll=4)


VMEM = pl.BlockSpec(memory_space=pltpu.VMEM)


def call(kernel, shapes, operands, scratch=(), cost=2.0):
    return pl.pallas_call(
        kernel,
        out_shape=[jax.ShapeDtypeStruct(shape, f32) for shape in shapes],
        in_specs=[VMEM] * len(operands),
        out_specs=[VMEM] * len(shapes),
        scratch_shapes=[pltpu.VMEM(shape, f32) for shape in scratch],
        cost_estimate=pl.CostEstimate(
            flops=int(cost * 1e9), bytes_accessed=int(cost * 3.6e6), transcendentals=0
        ),
        compiler_params=pltpu.CompilerParams(vmem_limit_bytes=20 * 2**20),
    )(*operands)


def shifted(block, axis, step):
    count = lax.axis_size(axis)
    return lax.ppermute(block, axis, [(i, (i + step) % count) for i in range(count)])


def swap(low, high, axis):
    return shifted(high, axis, 1), shifted(low, axis, -1)


def ring(values, axes, count, low, size):
    parts = []
    for step in range(1, size):
        route = []
        for i in range(count):
            place = i // low % size
            route.append((i, i + ((place + step) % size - place) * low))
        parts.append(lax.ppermute(values, axes, route))
    return values + sum(parts[1:], parts[0])


def total(values):
    values = ring(values, "gy", 4, 1, 2)
    values = ring(values, ("gx", "gy"), 32, 2, 4)
    values = ring(values, "gx", 8, 2, 4)
    return ring(values, "gz", 4, 1, 4)


CORE = (CZ, CY, CX)
FIELD = (EZ, EY, UX)


def per_device(rhs_field, stiffness):
    *tables, inverse = solve_tables()
    strips = call(start_columns_kernel, [(16, 8, 128)] * 2, [rhs_field, stiffness])
    columns = swap(*strips, "gx")
    fields = [rhs_field, stiffness, *columns]
    strips = call(
        start_rows_kernel,
        [(START_Y, 8, 128)] * 2,
        fields,
        [(2, 2, CZ, 8, 128), (2, 2, CZ // 2, 8, 128), (2, CZ // 8, 8, 128)],
    )
    rows = swap(*strips, "gy")
    wide, stiff, *strips = call(
        start_depth_kernel,
        [(CZ, EY, UX), (UZ, UY, UX)] + [(10, UY, CX)] * 2,
        [*fields, *rows],
    )
    depths = swap(*strips, "gz")
    solved = call(start_inner_kernel, [FIELD], [wide, *tables], cost=4.0)[0]
    shape = Shape(False)
    solved, stiff, *strips = call(
        start_outer_kernel,
        [FIELD, (UZ, UY, UX)] + [(shape.x_tiles, 8, 128)] * 2,
        [*depths, stiff, solved, inverse, *tables],
        [(4, EY, UX)],
        cost=6.0,
    )
    smooth, image, sums = [], [], []
    for turn in range(ITERS):
        shape = Shape(turn + 1 == ITERS)
        columns = swap(*strips, "gx")
        strips = call(
            functools.partial(row_strips_kernel, shape),
            [(shape.y_tiles, 8, 128)] * 2,
            [solved],
            cost=1.0,
        )
        rows = swap(*strips, "gy")
        strips = call(
            functools.partial(corners_kernel, shape), [(shape.c_tiles, 8, 128)] * 2, columns, cost=5.0
        )
        corners = swap(*strips, "gy")
        widened = call(
            functools.partial(widen_kernel, shape), [(EZ, UY, UX)], [solved, *columns]
        )[0]
        folded, *strips = call(
            functools.partial(depth_strips_kernel, shape),
            [(EZ, UY, UX)] + [(shape.rim + 1, UY, CX)] * 2,
            [widened, *rows, *corners],
            [(4, 2 * shape.x_groups, 8, 128)],
        )
        depths = swap(*strips, "gz")
        products = (turn + 2, 8, 128)
        outs = [CORE, CORE, products]
        if not shape.last:
            outs += [FIELD, FIELD]
        own, core, part, *fields = call(
            functools.partial(inner_kernel, turn, shape),
            outs,
            [folded, stiff, rhs_field, *smooth] + ([] if shape.last else tables),
            [(40, UY, UX)] * 2,
            cost=6.0,
        )
        operands = [folded, *depths, stiff, rhs_field, *smooth]
        operands += [own, core, part]
        scratch = [(14, UY, UX)] * 3
        if shape.last:
            operands += sums
            outs = [CORE, CORE, (8, 128)]
        else:
            operands += [*fields, inverse, *tables]
            following = Shape(turn + 2 == ITERS)
            outs = [CORE, CORE, products, FIELD] + [(following.x_tiles, 8, 128)] * 2
            scratch = [FIELD] + scratch
        own, core, part, *rest = call(
            functools.partial(outer_kernel, turn, shape),
            outs,
            operands,
            scratch,
            cost=8.0,
        )
        if rest:
            solved, *strips = rest
        smooth.append(own)
        image.append(core)
        sums.append(part)
    operands = [total(sums[-1]), rhs_field, *smooth, *image]
    return tuple(call(combine_kernel, [CORE] * 2, operands))


def solution(mesh):
    in_specs = (P("gz", "gy", "gx"), P("gz", "gy", "gx"))
    out_specs = (P("gz", "gy", "gx"), P("gz", "gy", "gx"))
    return jax.shard_map(
        per_device, mesh=mesh, in_specs=in_specs, out_specs=out_specs, check_vma=False
    )
```

```python
import functools

import jax
import jax.numpy as jnp
import numpy as np
from jax import lax
from jax.experimental import pallas as pl
from jax.experimental.pallas import tpu as pltpu
from jax.sharding import PartitionSpec as P

OV = 4
ITERS = 3
CZ, CY, CX = 48, 32, 128
EZ, EY, EX = CZ + 2 * OV, CY + 2 * OV, CX + 2 * OV
HALF = EZ // 2
UZ, UY, UX = CZ + 12, 48, 256
GROUP = 4
CHUNK = 2
INNER = [(z, 4) for z in range(10, 46, 4)]
OUTER = [(0, 4), (4, 4), (8, 2), (46, 4), (50, 4), (54, 2)]


class Shape:
    def __init__(self, last):
        self.rim = 6 if last else 10
        self.halo = 4 if last else 6
        self.width = 4 + self.halo
        self.per = 128 // self.width
        self.x_tiles = -(-EZ // self.per) * 5
        self.x_groups = self.x_tiles // 5
        self.extra_a = EZ if last else EZ + EZ // 4
        self.extra_b = self.extra_a + -(-EZ // 16)
        self.y_tiles = self.extra_b + (0 if last else 1)
        self.cut_near = 4 if last else 2
        self.c_tiles = 2 * self.x_groups + (0 if last else -(-self.x_groups // 2))
        self.last = last


mass_term = 1e-05
split_term = 0.5
bend_mean = 0.1
f32, bf16 = jnp.float32, jnp.bfloat16


def sine_table(length):
    places = np.arange(1, length + 1, dtype=np.float64)
    return np.sqrt(2.0 / (length + 1)) * np.sin(
        np.pi * places[:, None] * places[None, :] / (length + 1)
    )


def eigen_line(length):
    places = np.arange(1, length + 1, dtype=np.float64)
    return 2.0 - 2.0 * np.cos(np.pi * places / (length + 1))


def halves(table):
    high = np.asarray(table, np.float32).astype(jnp.bfloat16)
    low = (np.asarray(table, np.float64) - high.astype(np.float64)).astype(jnp.bfloat16)
    return [jnp.asarray(high), jnp.asarray(low)]


def solve_tables():
    column = np.zeros((UX, UX))
    full = sine_table(EX)
    for lane in range(UX):
        place = lane + OV if lane < CX + OV else lane - UX + OV
        if 0 <= place < EX:
            column[lane, :EX] = full[place]
    rows = np.roll(sine_table(EY), -OV, axis=0)
    row_fwd = np.kron(np.eye(2), rows.T)
    depth = sine_table(EZ)
    even = np.kron(depth[0::2, :HALF], np.eye(8))
    odd = np.kron(depth[1::2, :HALF], np.eye(8))
    order = np.concatenate([np.arange(0, EZ, 2), np.arange(1, EZ, 2)])
    spectrum = (
        eigen_line(EZ)[order][:, None, None]
        + eigen_line(EY)[None, :, None]
        + eigen_line(EX)[None, None, :]
    )
    inverse = np.zeros((EZ, EY, UX), np.float32)
    inverse[:, :, :EX] = 1.0 / (mass_term + bend_mean * spectrum**2 + split_term * spectrum)
    tables = []
    for table in (column, column.T):
        tables += halves(table)
    for table in (row_fwd, row_fwd.T):
        high, low = halves(table)
        tables.append(jnp.concatenate([high, low, high], axis=1))
    for table in (even, odd, even.T, odd.T):
        tables += halves(table)
    return tables + [jnp.asarray(inverse)]


def cut(values):
    high = values.astype(bf16)
    return high, (values - high.astype(f32)).astype(bf16)


def mul(a, b):
    return lax.dot_general(a, b, (((1,), (0,)), ((), ())), preferred_element_type=f32)


def mul3(a, b):
    return mul(a[0], b[0]) + (mul(a[0], b[1]) + mul(a[1], b[0]))


def lanes():
    return lax.broadcasted_iota(jnp.int32, (8, 128), 1)


def subs():
    return lax.broadcasted_iota(jnp.int32, (8, 128), 0)


def spin(values, shift, axis):
    size = values.shape[axis]
    shift = shift % size
    return values if shift == 0 else pltpu.roll(values, shift, axis)


def pack(into, values, lead, width, at):
    lane = lax.broadcasted_iota(jnp.int32, values.shape, 1)
    inside = (lane >= width * at) & (lane < width * (at + 1))
    moved = spin(values, lead + width * at, 1)
    return jnp.where(inside, moved, 0.0 if into is None else into)


def unpack(packed, lead, width, at):
    moved = spin(packed, -(lead + width * at), 1)
    lane = lax.broadcasted_iota(jnp.int32, packed.shape, 1)
    return jnp.where((lane >= 128 - lead) | (lane < width - lead), moved, 0.0)


def row_product(table, values):
    out, step = [], 2 * EY
    for at in range(0, values.shape[0], step):
        high, low = cut(values[at : at + step])
        out.append(mul(table, jnp.concatenate([high, high, low], axis=0)))
    return jnp.concatenate(out, axis=0)


def forward(values, tables):
    layers = values.shape[0]
    values = mul3(cut(values.reshape(layers * EY, UX)), (tables[0][...], tables[1][...]))
    return row_product(tables[4][...], values).reshape(layers, EY, UX)


def finish_solve(solved, tables, inverse, shape, low, high):
    column, row = (tables[2][...], tables[3][...]), tables[5][...]
    even_fwd, odd_fwd, even_bwd, odd_bwd = [
        (tables[i][...], tables[i + 1][...]) for i in (6, 8, 10, 12)
    ]
    for tile in range(EY // 8):
        rows = slice(8 * tile, 8 * tile + 8)
        near = solved[:HALF, rows, :]
        far = jnp.concatenate([solved[EZ - 1 - i : EZ - i, rows, :] for i in range(HALF)], axis=0)
        even = cut((near + far).reshape(8 * HALF, UX))
        odd = cut((near - far).reshape(8 * HALF, UX))
        even = mul3(even_fwd, even) * inverse[:HALF, rows, :].reshape(8 * HALF, UX)
        odd = mul3(odd_fwd, odd) * inverse[HALF:, rows, :].reshape(8 * HALF, UX)
        even = mul3(even_bwd, cut(even)).reshape(HALF, 8, UX)
        odd = mul3(odd_bwd, cut(odd)).reshape(HALF, 8, UX)
        solved[:HALF, rows, :] = even + odd
        far = even - odd
        for i in range(HALF):
            solved[EZ - 1 - i, rows, :] = far[i]

    later = Later()
    for z in range(0, EZ, GROUP):
        values = cut(row_product(row, solved[z : z + GROUP].reshape(GROUP * EY, UX)))
        values = mul3(values, column).reshape(GROUP, EY, UX)
        later.flush()
        later.put(solved, slice(z, z + GROUP), values)
    later.flush()

    lane = lanes()
    for first in range(0, EZ, shape.per):
        for tile in range(5):
            rows = slice(8 * tile, 8 * tile + 8)
            packed = [None, None]
            for j in range(min(shape.per, EZ - first)):
                near, far = solved[first + j, rows, :CX], solved[first + j, rows, CX:]
                packed[0] = pack(
                    packed[0], jnp.where(lane >= 124, far, near), OV, shape.width, j
                )
                packed[1] = pack(
                    packed[1],
                    jnp.where(lane >= 128 - shape.halo, near, far),
                    shape.halo,
                    shape.width,
                    j,
                )
            low[first // shape.per * 5 + tile] = packed[0]
            high[first // shape.per * 5 + tile] = packed[1]


def column_folded(solved, from_left, from_right, shape, z, tile):
    lane, rows = lanes(), slice(8 * tile, 8 * tile + 8)
    at, j = z // shape.per * 5 + tile, z % shape.per
    left = unpack(from_left[at], shape.halo, shape.width, j)
    right = unpack(from_right[at], OV, shape.width, j)
    return (
        solved[z, rows, :CX] + jnp.where(lane < 64, left, right),
        solved[z, rows, CX:] + jnp.where(lane < 64, right, left),
    )


class Later:
    def __init__(self):
        self.kept = []

    def put(self, ref, index, values):
        self.kept.append((ref, index, values))

    def flush(self):
        for ref, index, values in self.kept:
            ref[index] = values
        self.kept = []


def row_strips_kernel(shape, solved, low, high):
    sub = subs()
    for strip, cut_at, upper, lower, keep in (
        (low, 4, 4, 0, 4),
        (high, shape.cut_near, 3, 4, 2),
    ):
        extra_a = extra_b = None
        for quad in range(EZ // 4):
            rest = [None, None]
            for j in range(4):
                z = 4 * quad + j
                for side in (0, 1):
                    columns = slice(128 * side, 128 * side + 128)
                    lower_tile = solved[z, 8 * lower : 8 * lower + 8, columns]
                    upper_tile = solved[z, 8 * upper : 8 * upper + 8, columns]
                    main = jnp.where(sub >= cut_at, upper_tile, lower_tile)
                    if side == 0:
                        strip[z] = main
                    else:
                        extra_a = pack(extra_a if z % 16 else None, main, OV, 2 * OV, z % 16)
                        if z % 16 == 15 or z + 1 == EZ:
                            strip[shape.extra_a + z // 16] = extra_a
                    if not shape.last:
                        inside = (sub >= 2 * j) & (sub < 2 * j + 2)
                        moved = spin(lower_tile, 2 * j - keep, 0)
                        rest[side] = jnp.where(inside, moved, rest[side] if j else 0.0)
            if not shape.last:
                strip[EZ + quad] = rest[0]
                extra_b = pack(extra_b, rest[1], OV, 2 * OV, quad)
        if not shape.last:
            strip[shape.extra_b] = extra_b


def corners_kernel(shape, from_left, from_right, low, high):
    sub, groups = subs(), shape.x_groups
    for strip, cut_at, upper, lower, keep in (
        (low, 4, 4, 0, 4),
        (high, shape.cut_near, 3, 4, 2),
    ):
        rest = None
        for k in range(2 * groups):
            source = (from_left, from_right)[k // groups]
            lower_tile = source[k % groups * 5 + lower]
            strip[k] = jnp.where(sub >= cut_at, source[k % groups * 5 + upper], lower_tile)
            if shape.last:
                continue
            j = k % 4
            inside = (sub >= 2 * j) & (sub < 2 * j + 2)
            rest = jnp.where(inside, spin(lower_tile, 2 * j - keep, 0), rest if j else 0.0)
            if j == 3 or k + 1 == 2 * groups:
                strip[2 * groups + k // 4] = rest


def widen_kernel(shape, solved, from_left, from_right, folded):
    sub = subs()
    for z in range(EZ):
        for tile in range(5):
            values = column_folded(solved, from_left, from_right, shape, z, tile)
            for side in (0, 1):
                columns = slice(128 * side, 128 * side + 128)
                value = values[side]
                if tile == 4:
                    folded[z, 40:48, columns] = jnp.where(sub >= 4, value, 0.0)
                    value = jnp.where(sub < 4, value, 0.0)
                folded[z, 8 * tile : 8 * tile + 8, columns] = value


def row_part(strip, shape, z, side, keep):
    sub = subs()
    if side == 0:
        main = strip[z]
    else:
        main = unpack(strip[shape.extra_a + z // 16], OV, 2 * OV, z % 16)
    if shape.last:
        return main, jnp.zeros((8, 128), f32)
    if side == 0:
        rest = strip[EZ + z // 4]
    else:
        rest = unpack(strip[shape.extra_b], OV, 2 * OV, z // 4)
    moved = spin(rest, keep - 2 * (z % 4), 0)
    return main, jnp.where((sub >= keep) & (sub < keep + 2), moved, 0.0)


def depth_strips_kernel(
    shape, widened, from_near, from_far, corner_near, corner_far, folded, low, high, corners
):
    sub, lane, cut_at = subs(), lanes(), shape.cut_near
    groups = shape.x_groups
    for k in range(2 * groups):
        for strip, keep in ((corner_near, 2), (corner_far, 4)):
            main, rest = strip[k], 0.0
            if not shape.last:
                moved = spin(strip[2 * groups + k // 4], keep - 2 * (k % 4), 0)
                rest = jnp.where((sub >= keep) & (sub < keep + 2), moved, 0.0)
            if keep == 2:
                corners[0, k] = jnp.where(sub < cut_at, main, rest)
                corners[1, k] = jnp.where(sub >= cut_at, main, 0.0)
            else:
                corners[2, k] = jnp.where(sub >= 4, main, 0.0)
                corners[3, k] = jnp.where(sub < 4, main, rest)
    for z in range(EZ):
        group, j = z // shape.per, z % shape.per
        new = {}
        for side in (0, 1):
            main, rest = row_part(from_near, shape, z, side, 2)
            new[0, side] = jnp.where(sub < cut_at, main, rest)
            new[5, side] = jnp.where(sub >= cut_at, main, 0.0)
            main, rest = row_part(from_far, shape, z, side, 4)
            new[3, side] = jnp.where(sub >= 4, main, 0.0)
            new[4, side] = jnp.where(sub < 4, main, rest)
        for at, tile in enumerate((0, 5, 3, 4)):
            left = unpack(corners[at, group], shape.halo, shape.width, j)
            right = unpack(corners[at, groups + group], OV, shape.width, j)
            new[tile, 0] += jnp.where(lane < 64, left, right)
            new[tile, 1] += jnp.where(lane < 64, right, left)
        for side in (0, 1):
            columns = slice(128 * side, 128 * side + 128)
            for tile in range(6):
                rows = slice(8 * tile, 8 * tile + 8)
                value = widened[z, rows, columns]
                if (tile, side) in new:
                    value = value + new[tile, side]
                folded[z, rows, columns] = value
    for strip, start in ((low, 0), (high, EZ - shape.rim)):
        extra = None
        for i in range(shape.rim):
            strip[i] = folded[start + i, :, :CX]
            extra = pack(extra, folded[start + i, :, CX:], shape.halo, 2 * shape.halo, i)
        strip[shape.rim] = extra


def laplace(below, centre, above):
    beside = below + above
    beside = beside + (pltpu.roll(centre, 1, 0) + pltpu.roll(centre, UY - 1, 0))
    beside = beside + (pltpu.roll(centre, 1, 1) + pltpu.roll(centre, UX - 1, 1))
    return 6.0 * centre - beside


def operate(get, shift, span, flux, weighted, stiffness, wide, core, unroll):
    start, stop = span

    def chunks(body, start, stop, carry):
        size = CHUNK
        while (stop - start) % size:
            size -= 1
        return lax.fori_loop(
            0,
            (stop - start) // size,
            lambda i, c: body(start + size * i, size, c),
            carry,
            unroll=unroll,
        )

    def first(at, size, carry):
        later = Later()
        for z in [at + i for i in range(size)]:
            values = laplace(get(z - 1), get(z), get(z + 1))
            later.put(flux, z - shift, values)
            later.put(weighted, z - shift, stiffness[z] * values)
        later.flush()
        return carry

    chunks(first, start - 1, stop + 1, 0)
    sub = lax.broadcasted_iota(jnp.int32, (8, UX), 0)

    def second(base, size, carry, use_core):
        later = Later()
        for z in [base + i for i in range(size)]:
            own = get(z)
            at = z - shift
            values = laplace(weighted[at - 1], weighted[at], weighted[at + 1])
            values = mass_term * own + values + split_term * flux[at]
            if wide is not None:
                later.put(wide, (z - 2, slice(0, CY)), values[:CY])
                last = jnp.where(sub < 4, values[CY : CY + 8], values[CY + 8 :])
                later.put(wide, (z - 2, slice(CY, EY)), last)
            if use_core:
                carry = core(z, own[:CY, :CX], values[:CY, :CX], carry, later)
        later.flush()
        return carry

    return lambda first_z, last_z, carry, use_core: chunks(
        lambda z, size, c: second(z, size, c, use_core), first_z, last_z, carry
    )


def add_up(total, product):
    return total + ((product[0:8] + product[8:16]) + (product[16:24] + product[24:32]))


def core_step(count, rhs, earlier, smooth, image):
    def step(z, own, core, totals, later):
        at = z - 6
        later.put(smooth, at, own)
        later.put(image, at, core)
        new = [add_up(totals[0], own * rhs[at])]
        for i in range(count):
            new.append(add_up(totals[1 + i], core * earlier[i][at]))
        new.append(add_up(totals[1 + count], core * own))
        return tuple(new)

    return step


def inner_kernel(count, shape, *refs):
    folded, stiffness, rhs = refs[:3]
    earlier, refs = refs[3 : 3 + count], refs[3 + count :]
    tables = ()
    if not shape.last:
        tables, refs = refs[:14], refs[14:]
    smooth, image, sums = refs[:3]
    wide, solved = (None, None) if shape.last else (refs[-3], refs[3])
    flux, weighted = refs[-2:]
    step = core_step(count, rhs, earlier, smooth, image)
    run = operate(
        lambda z: folded[z - 2], 10, (12, 48), flux, weighted, stiffness, wide, step, 6
    )
    totals = run(12, 48, (jnp.zeros((8, 128), f32),) * (count + 2), True)
    for i, value in enumerate(totals):
        sums[i] = value
    if not shape.last:
        later = Later()
        for z, layers in INNER:
            values = forward(wide[z : z + layers], tables)
            later.flush()
            later.put(solved, slice(z, z + layers), values)
        later.flush()


def outer_kernel(count, shape, *refs):
    folded, from_below, from_above, stiffness, rhs = refs[:5]
    earlier, refs = refs[5 : 5 + count], refs[5 + count :]
    smooth_in, image_in, sums_in = refs[:3]
    refs = refs[3:]
    wide = None
    if shape.last:
        parts, refs = refs[:count], refs[count:]
    else:
        solved_in, inverse = refs[:2]
        tables, refs = refs[2:16], refs[16:]
        wide = refs[-4]
    smooth, image, sums = refs[:3]
    full, flux, weighted = refs[-3:]
    smooth[6:42] = smooth_in[6:42]
    image[6:42] = image_in[6:42]
    edge = 10 - shape.rim
    step = core_step(count, rhs, earlier, smooth, image)
    totals = tuple(sums_in[i] for i in range(count + 2))
    first_z = 6 if shape.last else 2
    for strip, base, shift in ((from_below, edge, 0), (from_above, 50, 46)):
        for z in range(14):
            layer = z + shift
            if not (4 if shape.last else 0) <= layer < (56 if shape.last else 60):
                continue
            at = layer - base
            inside = 2 <= layer < UZ - 2
            if 0 <= at < shape.rim:
                extra = unpack(strip[shape.rim], shape.halo, 2 * shape.halo, at)
                if inside:
                    full[z, :, :CX] = folded[layer - 2, :, :CX] + strip[at]
                    full[z, :, CX:] = folded[layer - 2, :, CX:] + extra
                else:
                    full[z, :, :CX] = strip[at]
                    full[z, :, CX:] = extra
            else:
                full[z] = folded[layer - 2]
        span = (first_z, 12) if shift == 0 else (48, UZ - first_z)
        run = operate(
            lambda z, shift=shift: full[z - shift],
            shift,
            span,
            flux,
            weighted,
            stiffness,
            wide,
            step,
            3,
        )
        if shift == 0:
            if not shape.last:
                run(2, 6, 0, False)
            totals = run(6, 12, totals, True)
        else:
            totals = run(48, 54, totals, True)
            if not shape.last:
                run(54, 58, 0, False)
    if not shape.last:
        for i, value in enumerate(totals):
            sums[i] = value
        solved, low, high = refs[3:6]
        solved[10:46] = solved_in[10:46]
        later = Later()
        for z, layers in OUTER:
            values = forward(wide[z : z + layers], tables)
            later.flush()
            later.put(solved, slice(z, z + layers), values)
        later.flush()
        finish_solve(solved, tables, inverse, Shape(count + 2 == ITERS), low, high)
        return
    lane = lanes()
    values = [part[i] for part in parts for i in range(part.shape[0])] + list(totals)
    gathered = jnp.zeros((8, 128), f32)
    for i, value in enumerate(values):
        value = jnp.sum(jnp.sum(value, axis=0, keepdims=True), axis=1, keepdims=True)
        gathered = jnp.where(lane == i, value, gathered)
    sums[...] = gathered


def start_columns_kernel(rhs, stiffness, low, high):
    for source, base, width in ((rhs, 0, 4), (stiffness, 8, 5)):
        per = 128 // width
        for first in range(0, CZ, per):
            for tile in range(4):
                packed = [None, None]
                for j in range(min(per, CZ - first)):
                    values = source[first + j, 8 * tile : 8 * tile + 8, :]
                    packed[0] = pack(packed[0], values, 0, width, j)
                    packed[1] = pack(packed[1], values, width, width, j)
                low[base + first // per * 4 + tile] = packed[0]
                high[base + first // per * 4 + tile] = packed[1]


def ends(left, right, width, j):
    lane = lanes()
    left = spin(left, -(width + width * j), 1)
    right = spin(right, -width * j, 1)
    return jnp.where(lane >= 128 - width, left, jnp.where(lane < width, right, 0.0))


def start_extra(from_left, from_right, base, width, z, tile):
    per = 128 // width
    at = base + z // per * 4 + tile
    return ends(from_left[at], from_right[at], width, z % per)


START_RHS, START_ST, START_ONE, START_Y = 0, 24, 48, 54


def start_rows_kernel(rhs, stiffness, low, high):
    sub = subs()
    strips = ((low, 0), (high, 3))

    def pairing(k, carry):
        for source, main_at in ((rhs, START_RHS), (stiffness, START_ST)):
            for strip, tile in strips:
                rows = slice(8 * tile, 8 * tile + 8)
                a, b = source[2 * k, rows, :], source[2 * k + 1, rows, :]
                if tile == 0:
                    strip[main_at + k] = jnp.where(sub < 4, a, spin(b, 4, 0))
                else:
                    strip[main_at + k] = jnp.where(sub < 4, spin(a, -4, 0), b)
        return carry

    lax.fori_loop(0, CZ // 2, pairing, 0, unroll=4)

    def single(k, carry):
        for strip, tile in strips:
            row = jnp.zeros((8, 128), f32)
            for j in range(8):
                values = stiffness[8 * k + j, 8 * tile : 8 * tile + 8, :]
                moved = spin(values, j - (4 if tile == 0 else 3), 0)
                row = jnp.where(sub == j, moved, row)
            strip[START_ONE + k] = row
        return carry

    lax.fori_loop(0, CZ // 8, single, 0, unroll=2)


def start_corners_kernel(from_left, from_right, low, high):
    for strip, tile in ((low, 0), (high, 3)):
        for group in range(4):
            strip[group] = from_left[4 * group + tile]
            strip[4 + group] = from_right[4 * group + tile]


def start_depth_kernel(
    rhs,
    stiffness,
    from_left,
    from_right,
    from_near,
    from_far,
    corner_near,
    corner_far,
    wide,
    stiff,
    low,
    high,
):
    sub = subs()

    def corner(strip, first, width, z):
        per = 128 // width
        at = first + z // per
        return ends(strip[at], strip[4 + at], width, z % per)

    for z in range(CZ):
        for tile in range(4):
            rows = slice(8 * tile, 8 * tile + 8)
            wide[z, rows, :CX] = rhs[z, rows, :]
            stiff[z + 6, rows, :CX] = stiffness[z, rows, :]
            wide[z, rows, CX:] = start_extra(from_left, from_right, 0, 4, z, tile)
            stiff[z + 6, rows, CX:] = start_extra(from_left, from_right, 8, 5, z, tile)
        odd = z % 2
        far, near = from_far[START_RHS + z // 2], from_near[START_RHS + z // 2]
        far, near = (spin(far, 4, 0), near) if odd else (far, spin(near, 4, 0))
        wide[z, 32:40, :CX] = jnp.where(sub < 4, far, near)
        far, near = corner(corner_far, 0, 4, z), corner(corner_near, 0, 4, z)
        wide[z, 32:40, CX:] = jnp.where(sub < 4, far, near)
        far, near = from_far[START_ST + z // 2], from_near[START_ST + z // 2]
        far, near = (spin(far, 4, 0), near) if odd else (far, spin(near, 4, 0))
        one = spin(from_far[START_ONE + z // 8], 4 - z % 8, 0)
        stiff[z + 6, 32:40, :CX] = jnp.where(sub < 4, far, jnp.where(sub == 4, one, 0.0))
        one = spin(from_near[START_ONE + z // 8], 3 - z % 8, 0)
        stiff[z + 6, 40:48, :CX] = jnp.where(sub >= 4, near, jnp.where(sub == 3, one, 0.0))
        far, near = corner(corner_far, 2, 5, z), corner(corner_near, 2, 5, z)
        stiff[z + 6, 32:40, CX:] = jnp.where(sub <= 4, far, 0.0)
        stiff[z + 6, 40:48, CX:] = jnp.where(sub >= 3, near, 0.0)
    blank = jnp.zeros((8, 128), f32)
    for strip, wide_at, stiff_at in ((low, 0, 6), (high, CZ - 4, CZ + 1)):
        extra = None
        for i in range(4):
            strip[i, :40] = wide[wide_at + i, :, :CX]
            strip[i, 40:48] = blank
        for i in range(5):
            strip[4 + i] = stiff[stiff_at + i, :, :CX]
            extra = pack(extra, stiff[stiff_at + i, :, CX:], 5, 10, i)
        strip[9] = extra
        for tile in range(5):
            rows = slice(8 * tile, 8 * tile + 8)
            extra = strip[9, rows, :]
            for i in range(4):
                lane = lanes()
                moved = spin(wide[wide_at + i, rows, CX:], 4 + 64 + 8 * i, 1)
                inside = (lane >= 64 + 8 * i) & (lane < 72 + 8 * i)
                extra = jnp.where(inside, moved, extra)
            strip[9, rows, :] = extra


def start_inner_kernel(wide, *refs):
    tables, solved = refs[:14], refs[14]
    later = Later()
    for z in range(4, 52, GROUP):
        values = forward(wide[z - 4 : z], tables)
        later.flush()
        later.put(solved, slice(z, z + GROUP), values)
    later.flush()


def start_outer_kernel(from_below, from_above, stiff_in, solved_in, inverse, *refs):
    tables, (solved, stiff, low, high, edge) = refs[:14], refs[14:]
    solved[4:52] = solved_in[4:52]
    stiff[6:54] = stiff_in[6:54]
    for strip, first, stiff_at in ((from_below, 0, 1), (from_above, 52, 54)):
        lane = lax.broadcasted_iota(jnp.int32, (EY, CX), 1)
        for i in range(4):
            edge[i, :, :CX] = strip[i, :40]
            moved = spin(strip[9, :40], -(4 + 64 + 8 * i), 1)
            edge[i, :, CX:] = jnp.where((lane >= 124) | (lane < 4), moved, 0.0)
        for i in range(5):
            stiff[stiff_at + i, :, :CX] = strip[4 + i]
            stiff[stiff_at + i, :, CX:] = unpack(strip[9], 5, 10, i)
        solved[first : first + GROUP] = forward(edge[...], tables)
    finish_solve(solved, tables, inverse, Shape(False), low, high)


def weights(b, pair):
    sigma = [jnp.zeros((1, 1), f32)] * ITERS
    delta = None
    current = None
    for turn in range(ITERS):
        zeta = [jnp.ones((1, 1), f32)] + [-s for s in sigma[:turn]]
        following = sum(z * b[i] for i, z in enumerate(zeta))
        for i, z in enumerate(zeta):
            for j in range(turn):
                following = following - z * sigma[j] * pair[i, j]
        if turn == 0:
            delta = zeta
        else:
            ratio = following / current
            delta = [z + ratio * d for z, d in zip(zeta, delta + [jnp.zeros((1, 1), f32)])]
        current = following
        bending = sum(
            delta[i] * delta[j] * pair[i, j] for i in range(turn + 1) for j in range(turn + 1)
        )
        step = current / bending
        sigma = [
            s + step * d for s, d in zip(sigma, delta + [jnp.zeros((1, 1), f32)] * (ITERS - turn - 1))
        ]
    return sigma


def combine_kernel(sums, rhs, u0, u1, u2, w0, w1, w2, answer, rest):
    picked = [
        jnp.sum(jnp.where(lanes()[:1] == i, sums[:1], 0.0), axis=1, keepdims=True)
        for i in range(ITERS * (ITERS + 3) // 2)
    ]
    b, pair, at = [], {}, 0
    for j in range(ITERS):
        b.append(picked[at])
        for i in range(j + 1):
            pair[i, j] = pair[j, i] = picked[at + 1 + i]
        at += j + 2
    s = weights(b, pair)

    def step(z, carry):
        answer[z] = s[0] * u0[z] + s[1] * u1[z] + s[2] * u2[z]
        rest[z] = rhs[z] - (s[0] * w0[z] + s[1] * w1[z] + s[2] * w2[z])
        return carry

    lax.fori_loop(0, CZ, step, 0, unroll=4)


VMEM = pl.BlockSpec(memory_space=pltpu.VMEM)


def call(kernel, shapes, operands, scratch=(), cost=2.0):
    return pl.pallas_call(
        kernel,
        out_shape=[jax.ShapeDtypeStruct(shape, f32) for shape in shapes],
        in_specs=[VMEM] * len(operands),
        out_specs=[VMEM] * len(shapes),
        scratch_shapes=[pltpu.VMEM(shape, f32) for shape in scratch],
        cost_estimate=pl.CostEstimate(
            flops=int(cost * 1e9), bytes_accessed=int(cost * 3.6e6), transcendentals=0
        ),
        compiler_params=pltpu.CompilerParams(vmem_limit_bytes=20 * 2**20),
    )(*operands)


def shifted(block, axis, step):
    count = lax.axis_size(axis)
    return lax.ppermute(block, axis, [(i, (i + step) % count) for i in range(count)])


def swap(low, high, axis):
    return shifted(high, axis, 1), shifted(low, axis, -1)


def ring(values, axes, count, low, size):
    parts = []
    for step in range(1, size):
        route = []
        for i in range(count):
            place = i // low % size
            route.append((i, i + ((place + step) % size - place) * low))
        parts.append(lax.ppermute(values, axes, route))
    return values + sum(parts[1:], parts[0])


def total(values):
    values = ring(values, "gy", 4, 1, 2)
    values = ring(values, ("gx", "gy"), 32, 2, 4)
    values = ring(values, "gx", 8, 2, 4)
    return ring(values, "gz", 4, 1, 4)


CORE = (CZ, CY, CX)
FIELD = (EZ, EY, UX)


def per_device(rhs_field, stiffness):
    *tables, inverse = solve_tables()
    strips = call(start_columns_kernel, [(16, 8, 128)] * 2, [rhs_field, stiffness])
    columns = swap(*strips, "gx")
    fields = [rhs_field, stiffness, *columns]
    strips = call(start_rows_kernel, [(START_Y, 8, 128)] * 2, fields[:2], cost=1.0)
    rows = swap(*strips, "gy")
    strips = call(start_corners_kernel, [(8, 8, 128)] * 2, columns, cost=5.0)
    corners = swap(*strips, "gy")
    wide, stiff, *strips = call(
        start_depth_kernel,
        [(CZ, EY, UX), (UZ, UY, UX)] + [(10, UY, CX)] * 2,
        [*fields, *rows, *corners],
    )
    depths = swap(*strips, "gz")
    solved = call(start_inner_kernel, [FIELD], [wide, *tables], cost=4.0)[0]
    shape = Shape(False)
    solved, stiff, *strips = call(
        start_outer_kernel,
        [FIELD, (UZ, UY, UX)] + [(shape.x_tiles, 8, 128)] * 2,
        [*depths, stiff, solved, inverse, *tables],
        [(4, EY, UX)],
        cost=6.0,
    )
    smooth, image, sums = [], [], []
    for turn in range(ITERS):
        shape = Shape(turn + 1 == ITERS)
        columns = swap(*strips, "gx")
        strips = call(
            functools.partial(row_strips_kernel, shape),
            [(shape.y_tiles, 8, 128)] * 2,
            [solved],
            cost=1.0,
        )
        rows = swap(*strips, "gy")
        strips = call(
            functools.partial(corners_kernel, shape), [(shape.c_tiles, 8, 128)] * 2, columns, cost=5.0
        )
        corners = swap(*strips, "gy")
        widened = call(
            functools.partial(widen_kernel, shape), [(EZ, UY, UX)], [solved, *columns]
        )[0]
        folded, *strips = call(
            functools.partial(depth_strips_kernel, shape),
            [(EZ, UY, UX)] + [(shape.rim + 1, UY, CX)] * 2,
            [widened, *rows, *corners],
            [(4, 2 * shape.x_groups, 8, 128)],
        )
        depths = swap(*strips, "gz")
        products = (turn + 2, 8, 128)
        outs = [CORE, CORE, products]
        if not shape.last:
            outs += [FIELD]
        own, core, part, *fields = call(
            functools.partial(inner_kernel, turn, shape),
            outs,
            [folded, stiff, rhs_field, *smooth] + ([] if shape.last else tables),
            ([] if shape.last else [FIELD]) + [(40, UY, UX)] * 2,
            cost=6.0,
        )
        operands = [folded, *depths, stiff, rhs_field, *smooth]
        operands += [own, core, part]
        scratch = [(14, UY, UX)] * 3
        if shape.last:
            operands += sums
            outs = [CORE, CORE, (8, 128)]
        else:
            operands += [*fields, inverse, *tables]
            following = Shape(turn + 2 == ITERS)
            outs = [CORE, CORE, products, FIELD] + [(following.x_tiles, 8, 128)] * 2
            scratch = [FIELD] + scratch
        own, core, part, *rest = call(
            functools.partial(outer_kernel, turn, shape),
            outs,
            operands,
            scratch,
            cost=8.0,
        )
        if rest:
            solved, *strips = rest
        smooth.append(own)
        image.append(core)
        sums.append(part)
    operands = [total(sums[-1]), rhs_field, *smooth, *image]
    return tuple(call(combine_kernel, [CORE] * 2, operands))


def solution(mesh):
    in_specs = (P("gz", "gy", "gx"), P("gz", "gy", "gx"))
    out_specs = (P("gz", "gy", "gx"), P("gz", "gy", "gx"))
    return jax.shard_map(
        per_device, mesh=mesh, in_specs=in_specs, out_specs=out_specs, check_vma=False
    )
```

```python
import functools

import jax
import jax.numpy as jnp
import numpy as np
from jax import lax
from jax.experimental import pallas as pl
from jax.experimental.pallas import tpu as pltpu
from jax.sharding import PartitionSpec as P

OV = 4
ITERS = 3
CZ, CY, CX = 48, 32, 128
EZ, EY, EX = CZ + 2 * OV, CY + 2 * OV, CX + 2 * OV
UZ, UY, UX = CZ + 12, 48, 256
GROUP = 4
TABLES = 7
CHUNK = 2
INNER = [(z, 4) for z in range(10, 46, 4)]
OUTER = [(0, 6), (6, 4), (46, 6), (52, 4)]


class Shape:
    def __init__(self, last):
        self.rim = 6 if last else 10
        self.halo = 4 if last else 6
        self.width = 4 + self.halo
        self.per = 128 // self.width
        self.x_tiles = -(-EZ // self.per) * 5
        self.x_groups = self.x_tiles // 5
        self.extra_a = EZ if last else EZ + EZ // 4
        self.extra_b = self.extra_a + -(-EZ // 16)
        self.y_tiles = self.extra_b + (0 if last else 1)
        self.cut_near = 4 if last else 2
        self.c_tiles = 2 * self.x_groups + (0 if last else -(-self.x_groups // 2))
        self.last = last


mass_term = 1e-05
split_term = 0.5
bend_mean = 0.1
f32, bf16 = jnp.float32, jnp.bfloat16


def sine_table(length):
    places = np.arange(1, length + 1, dtype=np.float64)
    return np.sqrt(2.0 / (length + 1)) * np.sin(
        np.pi * places[:, None] * places[None, :] / (length + 1)
    )


def eigen_line(length):
    places = np.arange(1, length + 1, dtype=np.float64)
    return 2.0 - 2.0 * np.cos(np.pi * places / (length + 1))


def halves(table):
    high = np.asarray(table, np.float32).astype(jnp.bfloat16)
    low = (np.asarray(table, np.float64) - high.astype(np.float64)).astype(jnp.bfloat16)
    return [jnp.asarray(high), jnp.asarray(low)]


def solve_tables():
    column = np.zeros((UX, UX))
    full = sine_table(EX)
    for lane in range(UX):
        place = lane + OV if lane < CX + OV else lane - UX + OV
        if 0 <= place < EX:
            column[lane, :EX] = full[place]
    rows = np.roll(sine_table(EY), -OV, axis=0)
    row_fwd = np.kron(np.eye(2), rows.T)
    spectrum = (
        eigen_line(EZ)[None, :, None]
        + eigen_line(EY)[:, None, None]
        + eigen_line(EX)[None, None, :]
    )
    inverse = np.zeros((EY, EZ, UX), np.float32)
    inverse[:, :, :EX] = 1.0 / (mass_term + bend_mean * spectrum**2 + split_term * spectrum)
    tables = []
    for table in (column, column.T):
        tables += halves(table)
    for table in (row_fwd, row_fwd.T, sine_table(EZ)):
        high, low = halves(table)
        tables.append(jnp.concatenate([high, low, high], axis=1))
    return tables + [jnp.asarray(inverse)]


def cut(values):
    high = values.astype(bf16)
    return high, (values - high.astype(f32)).astype(bf16)


def mul(a, b):
    return lax.dot_general(a, b, (((1,), (0,)), ((), ())), preferred_element_type=f32)


def mul3(a, b):
    return mul(a[0], b[0]) + (mul(a[0], b[1]) + mul(a[1], b[0]))


def lanes():
    return lax.broadcasted_iota(jnp.int32, (8, 128), 1)


def subs():
    return lax.broadcasted_iota(jnp.int32, (8, 128), 0)


def spin(values, shift, axis):
    size = values.shape[axis]
    shift = shift % size
    return values if shift == 0 else pltpu.roll(values, shift, axis)


def pack(into, values, lead, width, at):
    lane = lax.broadcasted_iota(jnp.int32, values.shape, 1)
    inside = (lane >= width * at) & (lane < width * (at + 1))
    moved = spin(values, lead + width * at, 1)
    return jnp.where(inside, moved, 0.0 if into is None else into)


def unpack(packed, lead, width, at):
    moved = spin(packed, -(lead + width * at), 1)
    lane = lax.broadcasted_iota(jnp.int32, packed.shape, 1)
    return jnp.where((lane >= 128 - lead) | (lane < width - lead), moved, 0.0)


class Later:
    def __init__(self):
        self.kept = []

    def put(self, ref, index, values):
        self.kept.append((ref, index, values))

    def flush(self):
        for ref, index, values in self.kept:
            ref[index] = values
        self.kept = []


def row_product(table, values):
    out, step = [], 2 * EY
    for at in range(0, values.shape[0], step):
        high, low = cut(values[at : at + step])
        out.append(mul(table, jnp.concatenate([high, high, low], axis=0)))
    return jnp.concatenate(out, axis=0)


def depth_product(table, values):
    high = values.astype(bf16).astype(f32)
    return mul(table, jnp.concatenate([high, high, values - high], axis=0).astype(bf16))


def forward(values, tables, later, parts, z):
    count = values.shape[0] * EY
    values = mul3(cut(values.reshape(count, UX)), (tables[0][...], tables[1][...]))
    values = row_product(tables[4][...], values)
    later.flush()
    for side in (0, 1):
        columns = slice(128 * side, 128 * side + 128)
        later.put(parts[side], slice(z * EY, z * EY + count), values[:, columns])


def finish_solve(parts, solved, tables, inverse, shape, low, high):
    column, row, depth = (tables[2][...], tables[3][...]), tables[5][...], tables[6][...]
    for b in range(EY):
        rows = pl.ds(b, EZ, stride=EY)
        values = jnp.concatenate([parts[0][rows, :], parts[1][rows, :]], axis=1)
        values = depth_product(depth, depth_product(depth, values) * inverse[b])
        parts[0][rows, :] = values[:, :CX]
        parts[1][rows, :] = values[:, CX:]

    later = Later()
    for z in range(0, EZ, GROUP):
        rows = slice(z * EY, (z + GROUP) * EY)
        values = jnp.concatenate([parts[0][rows, :], parts[1][rows, :]], axis=1)
        values = mul3(cut(row_product(row, values)), column).reshape(GROUP, EY, UX)
        later.flush()
        later.put(solved, slice(z, z + GROUP), values)
    later.flush()

    lane = lanes()
    for first in range(0, EZ, shape.per):
        for tile in range(5):
            rows = slice(8 * tile, 8 * tile + 8)
            packed = [None, None]
            for j in range(min(shape.per, EZ - first)):
                near, far = solved[first + j, rows, :CX], solved[first + j, rows, CX:]
                packed[0] = pack(
                    packed[0], jnp.where(lane >= 124, far, near), OV, shape.width, j
                )
                packed[1] = pack(
                    packed[1],
                    jnp.where(lane >= 128 - shape.halo, near, far),
                    shape.halo,
                    shape.width,
                    j,
                )
            low[first // shape.per * 5 + tile] = packed[0]
            high[first // shape.per * 5 + tile] = packed[1]


def column_folded(solved, from_left, from_right, shape, z, tile):
    lane, rows = lanes(), slice(8 * tile, 8 * tile + 8)
    at, j = z // shape.per * 5 + tile, z % shape.per
    left = unpack(from_left[at], shape.halo, shape.width, j)
    right = unpack(from_right[at], OV, shape.width, j)
    return (
        solved[z, rows, :CX] + jnp.where(lane < 64, left, right),
        solved[z, rows, CX:] + jnp.where(lane < 64, right, left),
    )


def row_strips_kernel(shape, solved, low, high):
    sub = subs()
    for strip, cut_at, upper, lower, keep in (
        (low, 4, 4, 0, 4),
        (high, shape.cut_near, 3, 4, 2),
    ):
        extra_a = extra_b = None
        for quad in range(EZ // 4):
            rest = [None, None]
            for j in range(4):
                z = 4 * quad + j
                for side in (0, 1):
                    columns = slice(128 * side, 128 * side + 128)
                    lower_tile = solved[z, 8 * lower : 8 * lower + 8, columns]
                    upper_tile = solved[z, 8 * upper : 8 * upper + 8, columns]
                    main = jnp.where(sub >= cut_at, upper_tile, lower_tile)
                    if side == 0:
                        strip[z] = main
                    else:
                        extra_a = pack(extra_a if z % 16 else None, main, OV, 2 * OV, z % 16)
                        if z % 16 == 15 or z + 1 == EZ:
                            strip[shape.extra_a + z // 16] = extra_a
                    if not shape.last:
                        inside = (sub >= 2 * j) & (sub < 2 * j + 2)
                        moved = spin(lower_tile, 2 * j - keep, 0)
                        rest[side] = jnp.where(inside, moved, rest[side] if j else 0.0)
            if not shape.last:
                strip[EZ + quad] = rest[0]
                extra_b = pack(extra_b, rest[1], OV, 2 * OV, quad)
        if not shape.last:
            strip[shape.extra_b] = extra_b


def corners_kernel(shape, from_left, from_right, low, high):
    sub, groups = subs(), shape.x_groups
    for strip, cut_at, upper, lower, keep in (
        (low, 4, 4, 0, 4),
        (high, shape.cut_near, 3, 4, 2),
    ):
        rest = None
        for k in range(2 * groups):
            source = (from_left, from_right)[k // groups]
            lower_tile = source[k % groups * 5 + lower]
            strip[k] = jnp.where(sub >= cut_at, source[k % groups * 5 + upper], lower_tile)
            if shape.last:
                continue
            j = k % 4
            inside = (sub >= 2 * j) & (sub < 2 * j + 2)
            rest = jnp.where(inside, spin(lower_tile, 2 * j - keep, 0), rest if j else 0.0)
            if j == 3 or k + 1 == 2 * groups:
                strip[2 * groups + k // 4] = rest


def widen_kernel(shape, solved, from_left, from_right, folded):
    sub = subs()
    for z in range(EZ):
        for tile in range(5):
            values = column_folded(solved, from_left, from_right, shape, z, tile)
            for side in (0, 1):
                columns = slice(128 * side, 128 * side + 128)
                value = values[side]
                if tile == 4:
                    folded[z, 40:48, columns] = jnp.where(sub >= 4, value, 0.0)
                    value = jnp.where(sub < 4, value, 0.0)
                folded[z, 8 * tile : 8 * tile + 8, columns] = value


def row_part(strip, shape, z, side, keep):
    sub = subs()
    if side == 0:
        main = strip[z]
    else:
        main = unpack(strip[shape.extra_a + z // 16], OV, 2 * OV, z % 16)
    if shape.last:
        return main, jnp.zeros((8, 128), f32)
    if side == 0:
        rest = strip[EZ + z // 4]
    else:
        rest = unpack(strip[shape.extra_b], OV, 2 * OV, z // 4)
    moved = spin(rest, keep - 2 * (z % 4), 0)
    return main, jnp.where((sub >= keep) & (sub < keep + 2), moved, 0.0)


def depth_strips_kernel(
    shape, widened, from_near, from_far, corner_near, corner_far, folded, low, high, corners
):
    sub, lane, cut_at = subs(), lanes(), shape.cut_near
    groups = shape.x_groups
    for k in range(2 * groups):
        for strip, keep in ((corner_near, 2), (corner_far, 4)):
            main, rest = strip[k], 0.0
            if not shape.last:
                moved = spin(strip[2 * groups + k // 4], keep - 2 * (k % 4), 0)
                rest = jnp.where((sub >= keep) & (sub < keep + 2), moved, 0.0)
            if keep == 2:
                corners[0, k] = jnp.where(sub < cut_at, main, rest)
                corners[1, k] = jnp.where(sub >= cut_at, main, 0.0)
            else:
                corners[2, k] = jnp.where(sub >= 4, main, 0.0)
                corners[3, k] = jnp.where(sub < 4, main, rest)
    for z in range(EZ):
        group, j = z // shape.per, z % shape.per
        new = {}
        for side in (0, 1):
            main, rest = row_part(from_near, shape, z, side, 2)
            new[0, side] = jnp.where(sub < cut_at, main, rest)
            new[5, side] = jnp.where(sub >= cut_at, main, 0.0)
            main, rest = row_part(from_far, shape, z, side, 4)
            new[3, side] = jnp.where(sub >= 4, main, 0.0)
            new[4, side] = jnp.where(sub < 4, main, rest)
        for at, tile in enumerate((0, 5, 3, 4)):
            left = unpack(corners[at, group], shape.halo, shape.width, j)
            right = unpack(corners[at, groups + group], OV, shape.width, j)
            new[tile, 0] += jnp.where(lane < 64, left, right)
            new[tile, 1] += jnp.where(lane < 64, right, left)
        for side in (0, 1):
            columns = slice(128 * side, 128 * side + 128)
            for tile in range(6):
                rows = slice(8 * tile, 8 * tile + 8)
                value = widened[z, rows, columns]
                if (tile, side) in new:
                    value = value + new[tile, side]
                folded[z, rows, columns] = value
    for strip, start in ((low, 0), (high, EZ - shape.rim)):
        extra = None
        for i in range(shape.rim):
            strip[i] = folded[start + i, :, :CX]
            extra = pack(extra, folded[start + i, :, CX:], shape.halo, 2 * shape.halo, i)
        strip[shape.rim] = extra


def laplace(below, centre, above):
    beside = below + above
    beside = beside + (pltpu.roll(centre, 1, 0) + pltpu.roll(centre, UY - 1, 0))
    beside = beside + (pltpu.roll(centre, 1, 1) + pltpu.roll(centre, UX - 1, 1))
    return 6.0 * centre - beside


def operate(get, shift, span, flux, weighted, stiffness, wide, core, unroll):
    start, stop = span

    def chunks(body, start, stop, carry):
        size = CHUNK
        while (stop - start) % size:
            size -= 1
        return lax.fori_loop(
            0,
            (stop - start) // size,
            lambda i, c: body(start + size * i, size, c),
            carry,
            unroll=unroll,
        )

    def first(at, size, carry):
        later = Later()
        for z in [at + i for i in range(size)]:
            values = laplace(get(z - 1), get(z), get(z + 1))
            later.put(flux, z - shift, values)
            later.put(weighted, z - shift, stiffness[z] * values)
        later.flush()
        return carry

    chunks(first, start - 1, stop + 1, 0)
    sub = lax.broadcasted_iota(jnp.int32, (8, UX), 0)

    def second(base, size, carry, use_core):
        later = Later()
        for z in [base + i for i in range(size)]:
            own = get(z)
            at = z - shift
            values = laplace(weighted[at - 1], weighted[at], weighted[at + 1])
            values = mass_term * own + values + split_term * flux[at]
            if wide is not None:
                later.put(wide, (z - 2, slice(0, CY)), values[:CY])
                last = jnp.where(sub < 4, values[CY : CY + 8], values[CY + 8 :])
                later.put(wide, (z - 2, slice(CY, EY)), last)
            if use_core:
                carry = core(z, own[:CY, :CX], values[:CY, :CX], carry, later)
        later.flush()
        return carry

    return lambda first_z, last_z, carry, use_core: chunks(
        lambda z, size, c: second(z, size, c, use_core), first_z, last_z, carry
    )


def add_up(total, product):
    return total + ((product[0:8] + product[8:16]) + (product[16:24] + product[24:32]))


def core_step(count, rhs, earlier, smooth, image):
    def step(z, own, core, totals, later):
        at = z - 6
        later.put(smooth, at, own)
        later.put(image, at, core)
        new = [add_up(totals[0], own * rhs[at])]
        for i in range(count):
            new.append(add_up(totals[1 + i], core * earlier[i][at]))
        new.append(add_up(totals[1 + count], core * own))
        return tuple(new)

    return step


def inner_kernel(count, shape, *refs):
    folded, stiffness, rhs = refs[:3]
    earlier, refs = refs[3 : 3 + count], refs[3 + count :]
    tables = ()
    if not shape.last:
        tables, refs = refs[:TABLES], refs[TABLES:]
    smooth, image, sums = refs[:3]
    wide, halves_out = (None, None) if shape.last else (refs[-3], refs[3:5])
    flux, weighted = refs[-2:]
    step = core_step(count, rhs, earlier, smooth, image)
    run = operate(
        lambda z: folded[z - 2], 10, (12, 48), flux, weighted, stiffness, wide, step, 6
    )
    totals = run(12, 48, (jnp.zeros((8, 128), f32),) * (count + 2), True)
    for i, value in enumerate(totals):
        sums[i] = value
    if not shape.last:
        later = Later()
        for z, layers in INNER:
            forward(wide[z : z + layers], tables, later, halves_out, z)
        later.flush()


def outer_kernel(count, shape, *refs):
    folded, from_below, from_above, stiffness, rhs = refs[:5]
    earlier, refs = refs[5 : 5 + count], refs[5 + count :]
    smooth_in, image_in, sums_in = refs[:3]
    refs = refs[3:]
    wide = None
    if shape.last:
        parts, refs = refs[:count], refs[count:]
    else:
        halves_in, inverse = refs[:2], refs[2]
        tables, refs = refs[3 : 3 + TABLES], refs[3 + TABLES :]
        wide, halves_out = refs[-4], refs[-6:-4]
    smooth, image, sums = refs[:3]
    full, flux, weighted = refs[-3:]
    smooth[6:42] = smooth_in[6:42]
    image[6:42] = image_in[6:42]
    edge = 10 - shape.rim
    step = core_step(count, rhs, earlier, smooth, image)
    totals = tuple(sums_in[i] for i in range(count + 2))
    first_z = 6 if shape.last else 2
    for strip, base, shift in ((from_below, edge, 0), (from_above, 50, 46)):
        for z in range(14):
            layer = z + shift
            if not (4 if shape.last else 0) <= layer < (56 if shape.last else 60):
                continue
            at = layer - base
            inside = 2 <= layer < UZ - 2
            if 0 <= at < shape.rim:
                extra = unpack(strip[shape.rim], shape.halo, 2 * shape.halo, at)
                if inside:
                    full[z, :, :CX] = folded[layer - 2, :, :CX] + strip[at]
                    full[z, :, CX:] = folded[layer - 2, :, CX:] + extra
                else:
                    full[z, :, :CX] = strip[at]
                    full[z, :, CX:] = extra
            else:
                full[z] = folded[layer - 2]
        span = (first_z, 12) if shift == 0 else (48, UZ - first_z)
        run = operate(
            lambda z, shift=shift: full[z - shift],
            shift,
            span,
            flux,
            weighted,
            stiffness,
            wide,
            step,
            2,
        )
        if shift == 0:
            if not shape.last:
                run(2, 6, 0, False)
            totals = run(6, 12, totals, True)
        else:
            totals = run(48, 54, totals, True)
            if not shape.last:
                run(54, 58, 0, False)
    if not shape.last:
        for i, value in enumerate(totals):
            sums[i] = value
        solved, low, high = refs[3:6]
        for part, source in zip(halves_out, halves_in):
            part[10 * EY : 46 * EY] = source[10 * EY : 46 * EY]
        later = Later()
        for z, layers in OUTER:
            forward(wide[z : z + layers], tables, later, halves_out, z)
        later.flush()
        finish_solve(
            halves_out, solved, tables, inverse, Shape(count + 2 == ITERS), low, high
        )
        return
    lane = lanes()
    values = [part[i] for part in parts for i in range(part.shape[0])] + list(totals)
    gathered = jnp.zeros((8, 128), f32)
    for i, value in enumerate(values):
        value = jnp.sum(jnp.sum(value, axis=0, keepdims=True), axis=1, keepdims=True)
        gathered = jnp.where(lane == i, value, gathered)
    sums[...] = gathered


def start_columns_kernel(rhs, stiffness, low, high):
    for source, base, width in ((rhs, 0, 4), (stiffness, 8, 5)):
        per = 128 // width
        for first in range(0, CZ, per):
            for tile in range(4):
                packed = [None, None]
                for j in range(min(per, CZ - first)):
                    values = source[first + j, 8 * tile : 8 * tile + 8, :]
                    packed[0] = pack(packed[0], values, 0, width, j)
                    packed[1] = pack(packed[1], values, width, width, j)
                low[base + first // per * 4 + tile] = packed[0]
                high[base + first // per * 4 + tile] = packed[1]


def ends(left, right, width, j):
    lane = lanes()
    left = spin(left, -(width + width * j), 1)
    right = spin(right, -width * j, 1)
    return jnp.where(lane >= 128 - width, left, jnp.where(lane < width, right, 0.0))


def start_extra(from_left, from_right, base, width, z, tile):
    per = 128 // width
    at = base + z // per * 4 + tile
    return ends(from_left[at], from_right[at], width, z % per)


START_RHS, START_ST, START_ONE, START_Y = 0, 24, 48, 54


def start_rows_kernel(rhs, stiffness, low, high):
    sub = subs()
    strips = ((low, 0), (high, 3))

    def pairing(k, carry):
        for source, main_at in ((rhs, START_RHS), (stiffness, START_ST)):
            for strip, tile in strips:
                rows = slice(8 * tile, 8 * tile + 8)
                a, b = source[2 * k, rows, :], source[2 * k + 1, rows, :]
                if tile == 0:
                    strip[main_at + k] = jnp.where(sub < 4, a, spin(b, 4, 0))
                else:
                    strip[main_at + k] = jnp.where(sub < 4, spin(a, -4, 0), b)
        return carry

    lax.fori_loop(0, CZ // 2, pairing, 0, unroll=4)

    def single(k, carry):
        for strip, tile in strips:
            row = jnp.zeros((8, 128), f32)
            for j in range(8):
                values = stiffness[8 * k + j, 8 * tile : 8 * tile + 8, :]
                moved = spin(values, j - (4 if tile == 0 else 3), 0)
                row = jnp.where(sub == j, moved, row)
            strip[START_ONE + k] = row
        return carry

    lax.fori_loop(0, CZ // 8, single, 0, unroll=2)


def start_corners_kernel(from_left, from_right, low, high):
    for strip, tile in ((low, 0), (high, 3)):
        for group in range(4):
            strip[group] = from_left[4 * group + tile]
            strip[4 + group] = from_right[4 * group + tile]


def start_depth_kernel(
    rhs,
    stiffness,
    from_left,
    from_right,
    from_near,
    from_far,
    corner_near,
    corner_far,
    wide,
    stiff,
    low,
    high,
):
    sub = subs()

    def corner(strip, first, width, z):
        per = 128 // width
        at = first + z // per
        return ends(strip[at], strip[4 + at], width, z % per)

    for z in range(CZ):
        for tile in range(4):
            rows = slice(8 * tile, 8 * tile + 8)
            wide[z, rows, :CX] = rhs[z, rows, :]
            stiff[z + 6, rows, :CX] = stiffness[z, rows, :]
            wide[z, rows, CX:] = start_extra(from_left, from_right, 0, 4, z, tile)
            stiff[z + 6, rows, CX:] = start_extra(from_left, from_right, 8, 5, z, tile)
        odd = z % 2
        far, near = from_far[START_RHS + z // 2], from_near[START_RHS + z // 2]
        far, near = (spin(far, 4, 0), near) if odd else (far, spin(near, 4, 0))
        wide[z, 32:40, :CX] = jnp.where(sub < 4, far, near)
        far, near = corner(corner_far, 0, 4, z), corner(corner_near, 0, 4, z)
        wide[z, 32:40, CX:] = jnp.where(sub < 4, far, near)
        far, near = from_far[START_ST + z // 2], from_near[START_ST + z // 2]
        far, near = (spin(far, 4, 0), near) if odd else (far, spin(near, 4, 0))
        one = spin(from_far[START_ONE + z // 8], 4 - z % 8, 0)
        stiff[z + 6, 32:40, :CX] = jnp.where(sub < 4, far, jnp.where(sub == 4, one, 0.0))
        one = spin(from_near[START_ONE + z // 8], 3 - z % 8, 0)
        stiff[z + 6, 40:48, :CX] = jnp.where(sub >= 4, near, jnp.where(sub == 3, one, 0.0))
        far, near = corner(corner_far, 2, 5, z), corner(corner_near, 2, 5, z)
        stiff[z + 6, 32:40, CX:] = jnp.where(sub <= 4, far, 0.0)
        stiff[z + 6, 40:48, CX:] = jnp.where(sub >= 3, near, 0.0)
    blank = jnp.zeros((8, 128), f32)
    for strip, wide_at, stiff_at in ((low, 0, 6), (high, CZ - 4, CZ + 1)):
        extra = None
        for i in range(4):
            strip[i, :40] = wide[wide_at + i, :, :CX]
            strip[i, 40:48] = blank
        for i in range(5):
            strip[4 + i] = stiff[stiff_at + i, :, :CX]
            extra = pack(extra, stiff[stiff_at + i, :, CX:], 5, 10, i)
        strip[9] = extra
        for tile in range(5):
            rows = slice(8 * tile, 8 * tile + 8)
            extra = strip[9, rows, :]
            for i in range(4):
                lane = lanes()
                moved = spin(wide[wide_at + i, rows, CX:], 4 + 64 + 8 * i, 1)
                inside = (lane >= 64 + 8 * i) & (lane < 72 + 8 * i)
                extra = jnp.where(inside, moved, extra)
            strip[9, rows, :] = extra


def start_inner_kernel(wide, *refs):
    tables, halves_out = refs[:TABLES], refs[TABLES:]
    later = Later()
    for z in range(4, 52, GROUP):
        forward(wide[z - 4 : z], tables, later, halves_out, z)
    later.flush()


def start_outer_kernel(from_below, from_above, stiff_in, *refs):
    halves_in, inverse = refs[:2], refs[2]
    tables, refs = refs[3 : 3 + TABLES], refs[3 + TABLES :]
    solved, stiff, low, high, edge = refs[:5]
    halves_out, later = refs[5:], Later()
    for part, source in zip(halves_out, halves_in):
        part[4 * EY : 52 * EY] = source[4 * EY : 52 * EY]
    stiff[6:54] = stiff_in[6:54]
    for strip, first, stiff_at in ((from_below, 0, 1), (from_above, 52, 54)):
        lane = lax.broadcasted_iota(jnp.int32, (EY, CX), 1)
        for i in range(4):
            edge[i, :, :CX] = strip[i, :40]
            moved = spin(strip[9, :40], -(4 + 64 + 8 * i), 1)
            edge[i, :, CX:] = jnp.where((lane >= 124) | (lane < 4), moved, 0.0)
        for i in range(5):
            stiff[stiff_at + i, :, :CX] = strip[4 + i]
            stiff[stiff_at + i, :, CX:] = unpack(strip[9], 5, 10, i)
        forward(edge[...], tables, later, halves_out, first)
        later.flush()
    finish_solve(halves_out, solved, tables, inverse, Shape(False), low, high)


def weights(b, pair):
    sigma = [jnp.zeros((1, 1), f32)] * ITERS
    delta = None
    current = None
    for turn in range(ITERS):
        zeta = [jnp.ones((1, 1), f32)] + [-s for s in sigma[:turn]]
        following = sum(z * b[i] for i, z in enumerate(zeta))
        for i, z in enumerate(zeta):
            for j in range(turn):
                following = following - z * sigma[j] * pair[i, j]
        if turn == 0:
            delta = zeta
        else:
            ratio = following / current
            delta = [z + ratio * d for z, d in zip(zeta, delta + [jnp.zeros((1, 1), f32)])]
        current = following
        bending = sum(
            delta[i] * delta[j] * pair[i, j] for i in range(turn + 1) for j in range(turn + 1)
        )
        step = current / bending
        sigma = [
            s + step * d for s, d in zip(sigma, delta + [jnp.zeros((1, 1), f32)] * (ITERS - turn - 1))
        ]
    return sigma


def combine_kernel(sums, rhs, u0, u1, u2, w0, w1, w2, answer, rest):
    picked = [
        jnp.sum(jnp.where(lanes()[:1] == i, sums[:1], 0.0), axis=1, keepdims=True)
        for i in range(ITERS * (ITERS + 3) // 2)
    ]
    b, pair, at = [], {}, 0
    for j in range(ITERS):
        b.append(picked[at])
        for i in range(j + 1):
            pair[i, j] = pair[j, i] = picked[at + 1 + i]
        at += j + 2
    s = weights(b, pair)

    def step(z, carry):
        answer[z] = s[0] * u0[z] + s[1] * u1[z] + s[2] * u2[z]
        rest[z] = rhs[z] - (s[0] * w0[z] + s[1] * w1[z] + s[2] * w2[z])
        return carry

    lax.fori_loop(0, CZ, step, 0, unroll=4)


VMEM = pl.BlockSpec(memory_space=pltpu.VMEM)


def call(kernel, shapes, operands, scratch=(), cost=2.0):
    return pl.pallas_call(
        kernel,
        out_shape=[jax.ShapeDtypeStruct(shape, f32) for shape in shapes],
        in_specs=[VMEM] * len(operands),
        out_specs=[VMEM] * len(shapes),
        scratch_shapes=[pltpu.VMEM(shape, f32) for shape in scratch],
        cost_estimate=pl.CostEstimate(
            flops=int(cost * 1e9), bytes_accessed=int(cost * 3.6e6), transcendentals=0
        ),
        compiler_params=pltpu.CompilerParams(vmem_limit_bytes=20 * 2**20),
    )(*operands)


def shifted(block, axis, step):
    count = lax.axis_size(axis)
    return lax.ppermute(block, axis, [(i, (i + step) % count) for i in range(count)])


def swap(low, high, axis):
    return shifted(high, axis, 1), shifted(low, axis, -1)


def ring(values, axes, count, low, size):
    parts = []
    for step in range(1, size):
        route = []
        for i in range(count):
            place = i // low % size
            route.append((i, i + ((place + step) % size - place) * low))
        parts.append(lax.ppermute(values, axes, route))
    return values + sum(parts[1:], parts[0])


def total(values):
    values = ring(values, "gy", 4, 1, 2)
    values = ring(values, ("gx", "gy"), 32, 2, 4)
    values = ring(values, "gx", 8, 2, 4)
    return ring(values, "gz", 4, 1, 4)


CORE = (CZ, CY, CX)
FIELD = (EZ, EY, UX)
PART = (EZ * EY, CX)


def per_device(rhs_field, stiffness):
    *tables, inverse = solve_tables()
    strips = call(start_columns_kernel, [(16, 8, 128)] * 2, [rhs_field, stiffness])
    columns = swap(*strips, "gx")
    fields = [rhs_field, stiffness, *columns]
    strips = call(start_rows_kernel, [(START_Y, 8, 128)] * 2, fields[:2], cost=1.0)
    rows = swap(*strips, "gy")
    strips = call(start_corners_kernel, [(8, 8, 128)] * 2, columns, cost=5.0)
    corners = swap(*strips, "gy")
    wide, stiff, *strips = call(
        start_depth_kernel,
        [(CZ, EY, UX), (UZ, UY, UX)] + [(10, UY, CX)] * 2,
        [*fields, *rows, *corners],
    )
    depths = swap(*strips, "gz")
    fields = call(start_inner_kernel, [PART] * 2, [wide, *tables], cost=4.0)
    shape = Shape(False)
    solved, stiff, *strips = call(
        start_outer_kernel,
        [FIELD, (UZ, UY, UX)] + [(shape.x_tiles, 8, 128)] * 2,
        [*depths, stiff, *fields, inverse, *tables],
        [(4, EY, UX), PART, PART],
        cost=6.0,
    )
    smooth, image, sums = [], [], []
    for turn in range(ITERS):
        shape = Shape(turn + 1 == ITERS)
        columns = swap(*strips, "gx")
        strips = call(
            functools.partial(row_strips_kernel, shape),
            [(shape.y_tiles, 8, 128)] * 2,
            [solved],
            cost=1.0,
        )
        rows = swap(*strips, "gy")
        strips = call(
            functools.partial(corners_kernel, shape), [(shape.c_tiles, 8, 128)] * 2, columns, cost=5.0
        )
        corners = swap(*strips, "gy")
        widened = call(
            functools.partial(widen_kernel, shape), [(EZ, UY, UX)], [solved, *columns]
        )[0]
        folded, *strips = call(
            functools.partial(depth_strips_kernel, shape),
            [(EZ, UY, UX)] + [(shape.rim + 1, UY, CX)] * 2,
            [widened, *rows, *corners],
            [(4, 2 * shape.x_groups, 8, 128)],
        )
        depths = swap(*strips, "gz")
        products = (turn + 2, 8, 128)
        outs = [CORE, CORE, products]
        if not shape.last:
            outs += [PART, PART]
        own, core, part, *fields = call(
            functools.partial(inner_kernel, turn, shape),
            outs,
            [folded, stiff, rhs_field, *smooth] + ([] if shape.last else tables),
            ([] if shape.last else [FIELD]) + [(40, UY, UX)] * 2,
            cost=6.0,
        )
        operands = [folded, *depths, stiff, rhs_field, *smooth]
        operands += [own, core, part]
        scratch = [(14, UY, UX)] * 3
        if shape.last:
            operands += sums
            outs = [CORE, CORE, (8, 128)]
        else:
            operands += [*fields, inverse, *tables]
            following = Shape(turn + 2 == ITERS)
            outs = [CORE, CORE, products, FIELD] + [(following.x_tiles, 8, 128)] * 2
            scratch = [PART, PART, FIELD] + scratch
        own, core, part, *rest = call(
            functools.partial(outer_kernel, turn, shape),
            outs,
            operands,
            scratch,
            cost=8.0,
        )
        if rest:
            solved, *strips = rest
        smooth.append(own)
        image.append(core)
        sums.append(part)
    operands = [total(sums[-1]), rhs_field, *smooth, *image]
    return tuple(call(combine_kernel, [CORE] * 2, operands))


def solution(mesh):
    in_specs = (P("gz", "gy", "gx"), P("gz", "gy", "gx"))
    out_specs = (P("gz", "gy", "gx"), P("gz", "gy", "gx"))
    return jax.shard_map(
        per_device, mesh=mesh, in_specs=in_specs, out_specs=out_specs, check_vma=False
    )
```

```python
import functools

import jax
import jax.numpy as jnp
import numpy as np
from jax import lax
from jax.experimental import pallas as pl
from jax.experimental.pallas import tpu as pltpu
from jax.sharding import PartitionSpec as P

OV = 4
ITERS = 3
CZ, CY, CX = 48, 32, 128
EZ, EY, EX = CZ + 2 * OV, CY + 2 * OV, CX + 2 * OV
UZ, UY, UX = CZ + 12, 48, 256
GROUP = 4
PIECES = 6
TABLES = 7
CHUNK = 2
INNER = [(z, 4) for z in range(10, 46, 4)]
OUTER = [(0, 6), (6, 4), (46, 6), (52, 4)]


class Shape:
    def __init__(self, last):
        self.rim = 6 if last else 10
        self.halo = 4 if last else 6
        self.width = 4 + self.halo
        self.per = 128 // self.width
        self.x_tiles = -(-EZ // self.per) * 5
        self.x_groups = self.x_tiles // 5
        self.extra_a = EZ if last else EZ + EZ // 4
        self.extra_b = self.extra_a + -(-EZ // 16)
        self.y_tiles = self.extra_b + (0 if last else 1)
        self.cut_near = 4 if last else 2
        self.c_tiles = 2 * self.x_groups + (0 if last else -(-self.x_groups // 2))
        self.last = last


mass_term = 1e-05
split_term = 0.5
bend_mean = 0.1
f32, bf16 = jnp.float32, jnp.bfloat16


def sine_table(length):
    places = np.arange(1, length + 1, dtype=np.float64)
    return np.sqrt(2.0 / (length + 1)) * np.sin(
        np.pi * places[:, None] * places[None, :] / (length + 1)
    )


def eigen_line(length):
    places = np.arange(1, length + 1, dtype=np.float64)
    return 2.0 - 2.0 * np.cos(np.pi * places / (length + 1))


def halves(table):
    high = np.asarray(table, np.float32).astype(jnp.bfloat16)
    low = (np.asarray(table, np.float64) - high.astype(np.float64)).astype(jnp.bfloat16)
    return [jnp.asarray(high), jnp.asarray(low)]


def solve_tables():
    column = np.zeros((UX, UX))
    full = sine_table(EX)
    for lane in range(UX):
        place = lane + OV if lane < CX + OV else lane - UX + OV
        if 0 <= place < EX:
            column[lane, :EX] = full[place]
    rows = np.roll(sine_table(EY), -OV, axis=0)
    row_fwd = np.kron(np.eye(2), rows.T)
    spectrum = (
        eigen_line(EZ)[None, :, None]
        + eigen_line(EY)[:, None, None]
        + eigen_line(EX)[None, None, :]
    )
    inverse = np.zeros((EY, EZ, UX), np.float32)
    inverse[:, :, :EX] = 1.0 / (mass_term + bend_mean * spectrum**2 + split_term * spectrum)
    tables = []
    for table in (column, column.T):
        tables += halves(table)
    for table in (row_fwd, row_fwd.T, sine_table(EZ)):
        high, low = halves(table)
        tables.append(jnp.concatenate([high, low, high], axis=1))
    return tables + [jnp.asarray(inverse)]


def cut(values):
    high = values.astype(bf16)
    return high, (values - high.astype(f32)).astype(bf16)


def mul(a, b):
    return lax.dot_general(a, b, (((1,), (0,)), ((), ())), preferred_element_type=f32)


def mul3(a, b):
    return mul(a[0], b[0]) + (mul(a[0], b[1]) + mul(a[1], b[0]))


def lanes():
    return lax.broadcasted_iota(jnp.int32, (8, 128), 1)


def subs():
    return lax.broadcasted_iota(jnp.int32, (8, 128), 0)


def spin(values, shift, axis):
    size = values.shape[axis]
    shift = shift % size
    return values if shift == 0 else pltpu.roll(values, shift, axis)


def pack(into, values, lead, width, at):
    lane = lax.broadcasted_iota(jnp.int32, values.shape, 1)
    inside = (lane >= width * at) & (lane < width * (at + 1))
    moved = spin(values, lead + width * at, 1)
    return jnp.where(inside, moved, 0.0 if into is None else into)


def unpack(packed, lead, width, at):
    moved = spin(packed, -(lead + width * at), 1)
    lane = lax.broadcasted_iota(jnp.int32, packed.shape, 1)
    return jnp.where((lane >= 128 - lead) | (lane < width - lead), moved, 0.0)


class Later:
    def __init__(self):
        self.kept = []

    def put(self, ref, index, values):
        self.kept.append((ref, index, values))

    def flush(self):
        for ref, index, values in self.kept:
            ref[index] = values
        self.kept = []


def row_product(table, values):
    out, step = [], 2 * EY
    for at in range(0, values.shape[0], step):
        high, low = cut(values[at : at + step])
        out.append(mul(table, jnp.concatenate([high, high, low], axis=0)))
    return jnp.concatenate(out, axis=0)


def depth_product(table, values):
    high = values.astype(bf16).astype(f32)
    return mul(table, jnp.concatenate([high, high, values - high], axis=0).astype(bf16))


def forward(values, tables, later, parts, z):
    count = values.shape[0] * EY
    values = mul3(cut(values.reshape(count, UX)), (tables[0][...], tables[1][...]))
    values = row_product(tables[4][...], values)
    later.flush()
    for side in (0, 1):
        columns = slice(128 * side, 128 * side + 128)
        later.put(parts[side], slice(z * EY, z * EY + count), values[:, columns])


def finish_solve(parts, solved, tables, inverse, shape, low, high):
    column, row, depth = (tables[2][...], tables[3][...]), tables[5][...], tables[6][...]
    for b in range(EY):
        rows = pl.ds(b, EZ, stride=EY)
        values = jnp.concatenate([parts[0][rows, :], parts[1][rows, :]], axis=1)
        values = depth_product(depth, depth_product(depth, values) * inverse[b])
        parts[0][rows, :] = values[:, :CX]
        parts[1][rows, :] = values[:, CX:]

    later = Later()
    for z in range(0, EZ, GROUP):
        rows = slice(z * EY, (z + GROUP) * EY)
        values = jnp.concatenate([parts[0][rows, :], parts[1][rows, :]], axis=1)
        values = mul3(cut(row_product(row, values)), column).reshape(GROUP, EY, UX)
        later.flush()
        later.put(solved, slice(z, z + GROUP), values)
    later.flush()

    lane = lanes()
    for first in range(0, EZ, shape.per):
        for tile in range(5):
            rows = slice(8 * tile, 8 * tile + 8)
            packed = [None, None]
            for j in range(min(shape.per, EZ - first)):
                near, far = solved[first + j, rows, :CX], solved[first + j, rows, CX:]
                packed[0] = pack(
                    packed[0], jnp.where(lane >= 124, far, near), OV, shape.width, j
                )
                packed[1] = pack(
                    packed[1],
                    jnp.where(lane >= 128 - shape.halo, near, far),
                    shape.halo,
                    shape.width,
                    j,
                )
            low[first // shape.per * 5 + tile] = packed[0]
            high[first // shape.per * 5 + tile] = packed[1]


def column_folded(solved, from_left, from_right, shape, z, tile):
    lane, rows = lanes(), slice(8 * tile, 8 * tile + 8)
    at, j = z // shape.per * 5 + tile, z % shape.per
    left = unpack(from_left[at], shape.halo, shape.width, j)
    right = unpack(from_right[at], OV, shape.width, j)
    return (
        solved[z, rows, :CX] + jnp.where(lane < 64, left, right),
        solved[z, rows, CX:] + jnp.where(lane < 64, right, left),
    )


def row_strips_kernel(shape, solved, low, high):
    sub = subs()
    for strip, cut_at, upper, lower, keep in (
        (low, 4, 4, 0, 4),
        (high, shape.cut_near, 3, 4, 2),
    ):
        extra_a = extra_b = None
        for quad in range(EZ // 4):
            rest = [None, None]
            for j in range(4):
                z = 4 * quad + j
                for side in (0, 1):
                    columns = slice(128 * side, 128 * side + 128)
                    lower_tile = solved[z, 8 * lower : 8 * lower + 8, columns]
                    upper_tile = solved[z, 8 * upper : 8 * upper + 8, columns]
                    main = jnp.where(sub >= cut_at, upper_tile, lower_tile)
                    if side == 0:
                        strip[z] = main
                    else:
                        extra_a = pack(extra_a if z % 16 else None, main, OV, 2 * OV, z % 16)
                        if z % 16 == 15 or z + 1 == EZ:
                            strip[shape.extra_a + z // 16] = extra_a
                    if not shape.last:
                        inside = (sub >= 2 * j) & (sub < 2 * j + 2)
                        moved = spin(lower_tile, 2 * j - keep, 0)
                        rest[side] = jnp.where(inside, moved, rest[side] if j else 0.0)
            if not shape.last:
                strip[EZ + quad] = rest[0]
                extra_b = pack(extra_b, rest[1], OV, 2 * OV, quad)
        if not shape.last:
            strip[shape.extra_b] = extra_b


def corners_kernel(shape, from_left, from_right, low, high):
    sub, groups = subs(), shape.x_groups
    for strip, cut_at, upper, lower, keep in (
        (low, 4, 4, 0, 4),
        (high, shape.cut_near, 3, 4, 2),
    ):
        rest = None
        for k in range(2 * groups):
            source = (from_left, from_right)[k // groups]
            lower_tile = source[k % groups * 5 + lower]
            strip[k] = jnp.where(sub >= cut_at, source[k % groups * 5 + upper], lower_tile)
            if shape.last:
                continue
            j = k % 4
            inside = (sub >= 2 * j) & (sub < 2 * j + 2)
            rest = jnp.where(inside, spin(lower_tile, 2 * j - keep, 0), rest if j else 0.0)
            if j == 3 or k + 1 == 2 * groups:
                strip[2 * groups + k // 4] = rest


def widen_kernel(shape, solved, from_left, from_right, folded):
    sub = subs()
    for z in range(EZ):
        for tile in range(5):
            values = column_folded(solved, from_left, from_right, shape, z, tile)
            for side in (0, 1):
                columns = slice(128 * side, 128 * side + 128)
                value = values[side]
                if tile == 4:
                    folded[z, 40:48, columns] = jnp.where(sub >= 4, value, 0.0)
                    value = jnp.where(sub < 4, value, 0.0)
                folded[z, 8 * tile : 8 * tile + 8, columns] = value


def row_part(strip, shape, z, side, keep):
    sub = subs()
    if side == 0:
        main = strip[z]
    else:
        main = unpack(strip[shape.extra_a + z // 16], OV, 2 * OV, z % 16)
    if shape.last:
        return main, jnp.zeros((8, 128), f32)
    if side == 0:
        rest = strip[EZ + z // 4]
    else:
        rest = unpack(strip[shape.extra_b], OV, 2 * OV, z // 4)
    moved = spin(rest, keep - 2 * (z % 4), 0)
    return main, jnp.where((sub >= keep) & (sub < keep + 2), moved, 0.0)


def depth_strips_kernel(
    shape, widened, from_near, from_far, corner_near, corner_far, folded, low, high, corners
):
    sub, lane, cut_at = subs(), lanes(), shape.cut_near
    groups = shape.x_groups
    for k in range(2 * groups):
        for strip, keep in ((corner_near, 2), (corner_far, 4)):
            main, rest = strip[k], 0.0
            if not shape.last:
                moved = spin(strip[2 * groups + k // 4], keep - 2 * (k % 4), 0)
                rest = jnp.where((sub >= keep) & (sub < keep + 2), moved, 0.0)
            if keep == 2:
                corners[0, k] = jnp.where(sub < cut_at, main, rest)
                corners[1, k] = jnp.where(sub >= cut_at, main, 0.0)
            else:
                corners[2, k] = jnp.where(sub >= 4, main, 0.0)
                corners[3, k] = jnp.where(sub < 4, main, rest)
    for z in range(EZ):
        group, j = z // shape.per, z % shape.per
        new = {}
        for side in (0, 1):
            main, rest = row_part(from_near, shape, z, side, 2)
            new[0, side] = jnp.where(sub < cut_at, main, rest)
            new[5, side] = jnp.where(sub >= cut_at, main, 0.0)
            main, rest = row_part(from_far, shape, z, side, 4)
            new[3, side] = jnp.where(sub >= 4, main, 0.0)
            new[4, side] = jnp.where(sub < 4, main, rest)
        for at, tile in enumerate((0, 5, 3, 4)):
            left = unpack(corners[at, group], shape.halo, shape.width, j)
            right = unpack(corners[at, groups + group], OV, shape.width, j)
            new[tile, 0] += jnp.where(lane < 64, left, right)
            new[tile, 1] += jnp.where(lane < 64, right, left)
        for side in (0, 1):
            columns = slice(128 * side, 128 * side + 128)
            for tile in range(6):
                rows = slice(8 * tile, 8 * tile + 8)
                value = widened[z, rows, columns]
                if (tile, side) in new:
                    value = value + new[tile, side]
                folded[z, rows, columns] = value
    for strip, start in ((low, 0), (high, EZ - shape.rim)):
        extra = None
        for i in range(shape.rim):
            strip[i] = folded[start + i, :, :CX]
            extra = pack(extra, folded[start + i, :, CX:], shape.halo, 2 * shape.halo, i)
        strip[shape.rim] = extra


def laplace(below, centre, above):
    beside = below + above
    beside = beside + (pltpu.roll(centre, 1, 0) + pltpu.roll(centre, UY - 1, 0))
    beside = beside + (pltpu.roll(centre, 1, 1) + pltpu.roll(centre, UX - 1, 1))
    return 6.0 * centre - beside


def operate(get, shift, span, flux, weighted, stiffness, wide, core, unroll):
    start, stop = span

    def chunks(body, start, stop, carry):
        size = CHUNK
        while (stop - start) % size:
            size -= 1
        return lax.fori_loop(
            0,
            (stop - start) // size,
            lambda i, c: body(start + size * i, size, c),
            carry,
            unroll=unroll,
        )

    def first(at, size, carry):
        later = Later()
        for z in [at + i for i in range(size)]:
            values = laplace(get(z - 1), get(z), get(z + 1))
            later.put(flux, z - shift, values)
            later.put(weighted, z - shift, stiffness[z] * values)
        later.flush()
        return carry

    chunks(first, start - 1, stop + 1, 0)
    sub = lax.broadcasted_iota(jnp.int32, (8, UX), 0)

    def second(base, size, carry, use_core):
        later = Later()
        for z in [base + i for i in range(size)]:
            own = get(z)
            at = z - shift
            values = laplace(weighted[at - 1], weighted[at], weighted[at + 1])
            values = mass_term * own + values + split_term * flux[at]
            if wide is not None:
                later.put(wide, (z - 2, slice(0, CY)), values[:CY])
                last = jnp.where(sub < 4, values[CY : CY + 8], values[CY + 8 :])
                later.put(wide, (z - 2, slice(CY, EY)), last)
            if use_core:
                carry = core(z, own[:CY, :CX], values[:CY, :CX], carry, later)
        later.flush()
        return carry

    return lambda first_z, last_z, carry, use_core: chunks(
        lambda z, size, c: second(z, size, c, use_core), first_z, last_z, carry
    )


def add_up(total, product):
    return total + ((product[0:8] + product[8:16]) + (product[16:24] + product[24:32]))


def core_step(count, rhs, earlier, smooth, image):
    def step(z, own, core, totals, later):
        at = z - 6
        later.put(smooth, at, own)
        later.put(image, at, core)
        new = [add_up(totals[0], own * rhs[at])]
        for i in range(count):
            new.append(add_up(totals[1 + i], core * earlier[i][at]))
        new.append(add_up(totals[1 + count], core * own))
        return tuple(new)

    return step


def inner_kernel(count, shape, *refs):
    folded, stiffness, rhs = refs[:3]
    earlier, refs = refs[3 : 3 + count], refs[3 + count :]
    tables = ()
    if not shape.last:
        tables, refs = refs[:TABLES], refs[TABLES:]
    smooth, image, sums = refs[:3]
    wide, halves_out = (None, None) if shape.last else (refs[-3], refs[3:5])
    flux, weighted = refs[-2:]
    step = core_step(count, rhs, earlier, smooth, image)
    run = operate(
        lambda z: folded[z - 2], 10, (12, 48), flux, weighted, stiffness, wide, step, 6
    )
    totals = run(12, 48, (jnp.zeros((8, 128), f32),) * (count + 2), True)
    for i, value in enumerate(totals):
        sums[i] = value
    if not shape.last:
        later = Later()
        for z, layers in INNER:
            forward(wide[z : z + layers], tables, later, halves_out, z)
        later.flush()


def outer_kernel(count, shape, *refs):
    folded, from_below, from_above, stiffness, rhs = refs[:5]
    earlier, refs = refs[5 : 5 + count], refs[5 + count :]
    smooth_in, image_in, sums_in = refs[:3]
    refs = refs[3:]
    wide = None
    if shape.last:
        parts, refs = refs[:count], refs[count:]
    else:
        halves_in, inverse = refs[:2], refs[2]
        tables, refs = refs[3 : 3 + TABLES], refs[3 + TABLES :]
        wide, halves_out = refs[-4], refs[-6:-4]
    smooth, image, sums = refs[:3]
    full, flux, weighted = refs[-3:]
    smooth[6:42] = smooth_in[6:42]
    image[6:42] = image_in[6:42]
    edge = 10 - shape.rim
    step = core_step(count, rhs, earlier, smooth, image)
    totals = tuple(sums_in[i] for i in range(count + 2))
    first_z = 6 if shape.last else 2
    for strip, base, shift in ((from_below, edge, 0), (from_above, 50, 46)):
        for z in range(14):
            layer = z + shift
            if not (4 if shape.last else 0) <= layer < (56 if shape.last else 60):
                continue
            at = layer - base
            inside = 2 <= layer < UZ - 2
            if 0 <= at < shape.rim:
                extra = unpack(strip[shape.rim], shape.halo, 2 * shape.halo, at)
                if inside:
                    full[z, :, :CX] = folded[layer - 2, :, :CX] + strip[at]
                    full[z, :, CX:] = folded[layer - 2, :, CX:] + extra
                else:
                    full[z, :, :CX] = strip[at]
                    full[z, :, CX:] = extra
            else:
                full[z] = folded[layer - 2]
        span = (first_z, 12) if shift == 0 else (48, UZ - first_z)
        run = operate(
            lambda z, shift=shift: full[z - shift],
            shift,
            span,
            flux,
            weighted,
            stiffness,
            wide,
            step,
            2,
        )
        if shift == 0:
            if not shape.last:
                run(2, 6, 0, False)
            totals = run(6, 12, totals, True)
        else:
            totals = run(48, 54, totals, True)
            if not shape.last:
                run(54, 58, 0, False)
    if not shape.last:
        for i, value in enumerate(totals):
            sums[i] = value
        solved, low, high = refs[3:6]
        for part, source in zip(halves_out, halves_in):
            part[10 * EY : 46 * EY] = source[10 * EY : 46 * EY]
        later = Later()
        for z, layers in OUTER:
            forward(wide[z : z + layers], tables, later, halves_out, z)
        later.flush()
        finish_solve(
            halves_out, solved, tables, inverse, Shape(count + 2 == ITERS), low, high
        )
        return
    lane = lanes()
    values = [part[i] for part in parts for i in range(part.shape[0])] + list(totals)
    gathered = jnp.zeros((8, 128), f32)
    for i, value in enumerate(values):
        value = jnp.sum(jnp.sum(value, axis=0, keepdims=True), axis=1, keepdims=True)
        gathered = jnp.where(lane == i, value, gathered)
    sums[...] = gathered


def start_columns_kernel(rhs_in, stiffness_in, low, high, rhs, stiffness, done):
    layers, copies = CZ // PIECES, []
    for i, (source, target) in enumerate(((rhs_in, rhs), (stiffness_in, stiffness))):
        for k in range(PIECES):
            part = pl.ds(k * layers, layers)
            copies.append(
                pltpu.make_async_copy(source.at[part], target.at[part], done.at[i, k])
            )
    for copy in copies:
        copy.start()
    for i, (source, base, width) in enumerate(((rhs, 0, 4), (stiffness, 8, 5))):
        for copy in copies[i * PIECES : (i + 1) * PIECES]:
            copy.wait()
        per = 128 // width
        for first in range(0, CZ, per):
            for tile in range(4):
                packed = [None, None]
                for j in range(min(per, CZ - first)):
                    values = source[first + j, 8 * tile : 8 * tile + 8, :]
                    packed[0] = pack(packed[0], values, 0, width, j)
                    packed[1] = pack(packed[1], values, width, width, j)
                low[base + first // per * 4 + tile] = packed[0]
                high[base + first // per * 4 + tile] = packed[1]


def ends(left, right, width, j):
    lane = lanes()
    left = spin(left, -(width + width * j), 1)
    right = spin(right, -width * j, 1)
    return jnp.where(lane >= 128 - width, left, jnp.where(lane < width, right, 0.0))


def start_extra(from_left, from_right, base, width, z, tile):
    per = 128 // width
    at = base + z // per * 4 + tile
    return ends(from_left[at], from_right[at], width, z % per)


START_RHS, START_ST, START_ONE, START_Y = 0, 24, 48, 54


def start_rows_kernel(rhs, stiffness, low, high):
    sub = subs()
    strips = ((low, 0), (high, 3))

    def pairing(k, carry):
        for source, main_at in ((rhs, START_RHS), (stiffness, START_ST)):
            for strip, tile in strips:
                rows = slice(8 * tile, 8 * tile + 8)
                a, b = source[2 * k, rows, :], source[2 * k + 1, rows, :]
                if tile == 0:
                    strip[main_at + k] = jnp.where(sub < 4, a, spin(b, 4, 0))
                else:
                    strip[main_at + k] = jnp.where(sub < 4, spin(a, -4, 0), b)
        return carry

    lax.fori_loop(0, CZ // 2, pairing, 0, unroll=4)

    def single(k, carry):
        for strip, tile in strips:
            row = jnp.zeros((8, 128), f32)
            for j in range(8):
                values = stiffness[8 * k + j, 8 * tile : 8 * tile + 8, :]
                moved = spin(values, j - (4 if tile == 0 else 3), 0)
                row = jnp.where(sub == j, moved, row)
            strip[START_ONE + k] = row
        return carry

    lax.fori_loop(0, CZ // 8, single, 0, unroll=2)


def start_corners_kernel(from_left, from_right, low, high):
    for strip, tile in ((low, 0), (high, 3)):
        for group in range(4):
            strip[group] = from_left[4 * group + tile]
            strip[4 + group] = from_right[4 * group + tile]


def start_depth_kernel(
    rhs,
    stiffness,
    from_left,
    from_right,
    from_near,
    from_far,
    corner_near,
    corner_far,
    wide,
    stiff,
    low,
    high,
):
    sub = subs()

    def corner(strip, first, width, z):
        per = 128 // width
        at = first + z // per
        return ends(strip[at], strip[4 + at], width, z % per)

    for z in range(CZ):
        for tile in range(4):
            rows = slice(8 * tile, 8 * tile + 8)
            wide[z, rows, :CX] = rhs[z, rows, :]
            stiff[z + 6, rows, :CX] = stiffness[z, rows, :]
            wide[z, rows, CX:] = start_extra(from_left, from_right, 0, 4, z, tile)
            stiff[z + 6, rows, CX:] = start_extra(from_left, from_right, 8, 5, z, tile)
        odd = z % 2
        far, near = from_far[START_RHS + z // 2], from_near[START_RHS + z // 2]
        far, near = (spin(far, 4, 0), near) if odd else (far, spin(near, 4, 0))
        wide[z, 32:40, :CX] = jnp.where(sub < 4, far, near)
        far, near = corner(corner_far, 0, 4, z), corner(corner_near, 0, 4, z)
        wide[z, 32:40, CX:] = jnp.where(sub < 4, far, near)
        far, near = from_far[START_ST + z // 2], from_near[START_ST + z // 2]
        far, near = (spin(far, 4, 0), near) if odd else (far, spin(near, 4, 0))
        one = spin(from_far[START_ONE + z // 8], 4 - z % 8, 0)
        stiff[z + 6, 32:40, :CX] = jnp.where(sub < 4, far, jnp.where(sub == 4, one, 0.0))
        one = spin(from_near[START_ONE + z // 8], 3 - z % 8, 0)
        stiff[z + 6, 40:48, :CX] = jnp.where(sub >= 4, near, jnp.where(sub == 3, one, 0.0))
        far, near = corner(corner_far, 2, 5, z), corner(corner_near, 2, 5, z)
        stiff[z + 6, 32:40, CX:] = jnp.where(sub <= 4, far, 0.0)
        stiff[z + 6, 40:48, CX:] = jnp.where(sub >= 3, near, 0.0)
    blank = jnp.zeros((8, 128), f32)
    for strip, wide_at, stiff_at in ((low, 0, 6), (high, CZ - 4, CZ + 1)):
        extra = None
        for i in range(4):
            strip[i, :40] = wide[wide_at + i, :, :CX]
            strip[i, 40:48] = blank
        for i in range(5):
            strip[4 + i] = stiff[stiff_at + i, :, :CX]
            extra = pack(extra, stiff[stiff_at + i, :, CX:], 5, 10, i)
        strip[9] = extra
        for tile in range(5):
            rows = slice(8 * tile, 8 * tile + 8)
            extra = strip[9, rows, :]
            for i in range(4):
                lane = lanes()
                moved = spin(wide[wide_at + i, rows, CX:], 4 + 64 + 8 * i, 1)
                inside = (lane >= 64 + 8 * i) & (lane < 72 + 8 * i)
                extra = jnp.where(inside, moved, extra)
            strip[9, rows, :] = extra


def start_inner_kernel(wide, *refs):
    tables, halves_out = refs[:TABLES], refs[TABLES:]
    later = Later()
    for z in range(4, 52, GROUP):
        forward(wide[z - 4 : z], tables, later, halves_out, z)
    later.flush()


def start_outer_kernel(from_below, from_above, stiff_in, *refs):
    halves_in, inverse = refs[:2], refs[2]
    tables, refs = refs[3 : 3 + TABLES], refs[3 + TABLES :]
    solved, stiff, low, high, edge = refs[:5]
    halves_out, later = refs[5:], Later()
    for part, source in zip(halves_out, halves_in):
        part[4 * EY : 52 * EY] = source[4 * EY : 52 * EY]
    stiff[6:54] = stiff_in[6:54]
    for strip, first, stiff_at in ((from_below, 0, 1), (from_above, 52, 54)):
        lane = lax.broadcasted_iota(jnp.int32, (EY, CX), 1)
        for i in range(4):
            edge[i, :, :CX] = strip[i, :40]
            moved = spin(strip[9, :40], -(4 + 64 + 8 * i), 1)
            edge[i, :, CX:] = jnp.where((lane >= 124) | (lane < 4), moved, 0.0)
        for i in range(5):
            stiff[stiff_at + i, :, :CX] = strip[4 + i]
            stiff[stiff_at + i, :, CX:] = unpack(strip[9], 5, 10, i)
        forward(edge[...], tables, later, halves_out, first)
        later.flush()
    finish_solve(halves_out, solved, tables, inverse, Shape(False), low, high)


def weights(b, pair):
    sigma = [jnp.zeros((1, 1), f32)] * ITERS
    delta = None
    current = None
    for turn in range(ITERS):
        zeta = [jnp.ones((1, 1), f32)] + [-s for s in sigma[:turn]]
        following = sum(z * b[i] for i, z in enumerate(zeta))
        for i, z in enumerate(zeta):
            for j in range(turn):
                following = following - z * sigma[j] * pair[i, j]
        if turn == 0:
            delta = zeta
        else:
            ratio = following / current
            delta = [z + ratio * d for z, d in zip(zeta, delta + [jnp.zeros((1, 1), f32)])]
        current = following
        bending = sum(
            delta[i] * delta[j] * pair[i, j] for i in range(turn + 1) for j in range(turn + 1)
        )
        step = current / bending
        sigma = [
            s + step * d for s, d in zip(sigma, delta + [jnp.zeros((1, 1), f32)] * (ITERS - turn - 1))
        ]
    return sigma


def combine_kernel(
    sums, rhs, u0, u1, u2, w0, w1, w2, answer_out, rest_out, answer, rest, done
):
    picked = [
        jnp.sum(jnp.where(lanes()[:1] == i, sums[:1], 0.0), axis=1, keepdims=True)
        for i in range(ITERS * (ITERS + 3) // 2)
    ]
    b, pair, at = [], {}, 0
    for j in range(ITERS):
        b.append(picked[at])
        for i in range(j + 1):
            pair[i, j] = pair[j, i] = picked[at + 1 + i]
        at += j + 2
    s = weights(b, pair)

    def step(z, carry):
        answer[z] = s[0] * u0[z] + s[1] * u1[z] + s[2] * u2[z]
        rest[z] = rhs[z] - (s[0] * w0[z] + s[1] * w1[z] + s[2] * w2[z])
        return carry

    layers, copies = CZ // PIECES, []
    for k in range(PIECES):
        lax.fori_loop(k * layers, (k + 1) * layers, step, 0, unroll=4)
        part = pl.ds(k * layers, layers)
        for i, (source, target) in enumerate(((answer, answer_out), (rest, rest_out))):
            copies.append(
                pltpu.make_async_copy(source.at[part], target.at[part], done.at[i, k])
            )
            copies[-1].start()
    for copy in copies:
        copy.wait()


VMEM = pl.BlockSpec(memory_space=pltpu.VMEM)
HBM = pl.BlockSpec(memory_space=pl.ANY)


def call(kernel, shapes, operands, scratch=(), cost=2.0, outside=None):
    return pl.pallas_call(
        kernel,
        out_shape=[jax.ShapeDtypeStruct(shape, f32) for shape in shapes],
        in_specs=[HBM if outside == "in" else VMEM] * len(operands),
        out_specs=[HBM if outside == "out" else VMEM] * len(shapes),
        scratch_shapes=[pltpu.VMEM(shape, f32) for shape in scratch]
        + ([pltpu.SemaphoreType.DMA((2, PIECES))] if outside else []),
        cost_estimate=pl.CostEstimate(
            flops=int(cost * 1e9), bytes_accessed=int(cost * 3.6e6), transcendentals=0
        ),
        compiler_params=pltpu.CompilerParams(vmem_limit_bytes=20 * 2**20),
    )(*operands)


def shifted(block, axis, step):
    count = lax.axis_size(axis)
    return lax.ppermute(block, axis, [(i, (i + step) % count) for i in range(count)])


def swap(low, high, axis):
    return shifted(high, axis, 1), shifted(low, axis, -1)


def exchange(values, axes, count, low, mask):
    route = [(i, i ^ (mask * low)) for i in range(count)]
    return values + lax.ppermute(values, axes, route)


def total(values):
    values = exchange(values, "gy", 4, 1, 1)
    for axes, count, low in ((("gx", "gy"), 32, 2), ("gx", 8, 2), ("gz", 4, 1)):
        for mask in (1, 3):
            values = exchange(values, axes, count, low, mask)
    return values


CORE = (CZ, CY, CX)
FIELD = (EZ, EY, UX)
PART = (EZ * EY, CX)


def per_device(rhs_field, stiffness):
    *tables, inverse = solve_tables()
    *strips, rhs_field, stiffness = call(
        start_columns_kernel,
        [(16, 8, 128)] * 2 + [CORE] * 2,
        [rhs_field, stiffness],
        outside="in",
    )
    columns = swap(*strips, "gx")
    fields = [rhs_field, stiffness, *columns]
    strips = call(start_rows_kernel, [(START_Y, 8, 128)] * 2, fields[:2], cost=1.0)
    rows = swap(*strips, "gy")
    strips = call(start_corners_kernel, [(8, 8, 128)] * 2, columns, cost=5.0)
    corners = swap(*strips, "gy")
    wide, stiff, *strips = call(
        start_depth_kernel,
        [(CZ, EY, UX), (UZ, UY, UX)] + [(10, UY, CX)] * 2,
        [*fields, *rows, *corners],
    )
    depths = swap(*strips, "gz")
    fields = call(start_inner_kernel, [PART] * 2, [wide, *tables], cost=4.0)
    shape = Shape(False)
    solved, stiff, *strips = call(
        start_outer_kernel,
        [FIELD, (UZ, UY, UX)] + [(shape.x_tiles, 8, 128)] * 2,
        [*depths, stiff, *fields, inverse, *tables],
        [(4, EY, UX), PART, PART],
        cost=6.0,
    )
    smooth, image, sums = [], [], []
    for turn in range(ITERS):
        shape = Shape(turn + 1 == ITERS)
        columns = swap(*strips, "gx")
        strips = call(
            functools.partial(row_strips_kernel, shape),
            [(shape.y_tiles, 8, 128)] * 2,
            [solved],
            cost=1.0,
        )
        rows = swap(*strips, "gy")
        strips = call(
            functools.partial(corners_kernel, shape), [(shape.c_tiles, 8, 128)] * 2, columns, cost=5.0
        )
        corners = swap(*strips, "gy")
        widened = call(
            functools.partial(widen_kernel, shape), [(EZ, UY, UX)], [solved, *columns]
        )[0]
        folded, *strips = call(
            functools.partial(depth_strips_kernel, shape),
            [(EZ, UY, UX)] + [(shape.rim + 1, UY, CX)] * 2,
            [widened, *rows, *corners],
            [(4, 2 * shape.x_groups, 8, 128)],
        )
        depths = swap(*strips, "gz")
        products = (turn + 2, 8, 128)
        outs = [CORE, CORE, products]
        if not shape.last:
            outs += [PART, PART]
        own, core, part, *fields = call(
            functools.partial(inner_kernel, turn, shape),
            outs,
            [folded, stiff, rhs_field, *smooth] + ([] if shape.last else tables),
            ([] if shape.last else [FIELD]) + [(40, UY, UX)] * 2,
            cost=6.0,
        )
        operands = [folded, *depths, stiff, rhs_field, *smooth]
        operands += [own, core, part]
        scratch = [(14, UY, UX)] * 3
        if shape.last:
            operands += sums
            outs = [CORE, CORE, (8, 128)]
        else:
            operands += [*fields, inverse, *tables]
            following = Shape(turn + 2 == ITERS)
            outs = [CORE, CORE, products, FIELD] + [(following.x_tiles, 8, 128)] * 2
            scratch = [PART, PART, FIELD] + scratch
        own, core, part, *rest = call(
            functools.partial(outer_kernel, turn, shape),
            outs,
            operands,
            scratch,
            cost=8.0,
        )
        if rest:
            solved, *strips = rest
        smooth.append(own)
        image.append(core)
        sums.append(part)
    operands = [total(sums[-1]), rhs_field, *smooth, *image]
    return tuple(call(combine_kernel, [CORE] * 2, operands, [CORE] * 2, outside="out"))


def solution(mesh):
    in_specs = (P("gz", "gy", "gx"), P("gz", "gy", "gx"))
    out_specs = (P("gz", "gy", "gx"), P("gz", "gy", "gx"))
    return jax.shard_map(
        per_device, mesh=mesh, in_specs=in_specs, out_specs=out_specs, check_vma=False
    )
```

```python
import functools

import jax
import jax.numpy as jnp
import numpy as np
from jax import lax
from jax.experimental import pallas as pl
from jax.experimental.pallas import tpu as pltpu
from jax.sharding import PartitionSpec as P

OV = 4
ITERS = 3
CZ, CY, CX = 48, 32, 128
EZ, EY, EX = CZ + 2 * OV, CY + 2 * OV, CX + 2 * OV
UZ, UY, UX = CZ + 12, 48, 256
GROUP = 4
PIECES = 4
TABLES = 7
CHUNK = 2
INNER = [(z, 4) for z in range(10, 46, 4)]
OUTER = [(0, 6), (6, 4), (46, 6), (52, 4)]


class Shape:
    def __init__(self, last):
        self.rim = 6 if last else 10
        self.halo = 4 if last else 6
        self.width = 4 + self.halo
        self.per = 128 // self.width
        self.x_tiles = -(-EZ // self.per) * 5
        self.x_groups = self.x_tiles // 5
        self.extra_a = EZ if last else EZ + EZ // 4
        self.extra_b = self.extra_a + -(-EZ // 16)
        self.y_tiles = self.extra_b + (0 if last else 1)
        self.cut_near = 4 if last else 2
        self.c_tiles = 2 * self.x_groups + (0 if last else -(-self.x_groups // 2))
        self.last = last


mass_term = 1e-05
split_term = 0.5
bend_mean = 0.1
f32, bf16 = jnp.float32, jnp.bfloat16


def sine_table(length):
    places = np.arange(1, length + 1, dtype=np.float64)
    return np.sqrt(2.0 / (length + 1)) * np.sin(
        np.pi * places[:, None] * places[None, :] / (length + 1)
    )


def eigen_line(length):
    places = np.arange(1, length + 1, dtype=np.float64)
    return 2.0 - 2.0 * np.cos(np.pi * places / (length + 1))


def halves(table):
    high = np.asarray(table, np.float32).astype(jnp.bfloat16)
    low = (np.asarray(table, np.float64) - high.astype(np.float64)).astype(jnp.bfloat16)
    return [jnp.asarray(high), jnp.asarray(low)]


def solve_tables():
    column = np.zeros((UX, UX))
    full = sine_table(EX)
    for lane in range(UX):
        place = lane + OV if lane < CX + OV else lane - UX + OV
        if 0 <= place < EX:
            column[lane, :EX] = full[place]
    rows = np.roll(sine_table(EY), -OV, axis=0)
    row_fwd = np.kron(np.eye(2), rows.T)
    spectrum = (
        eigen_line(EZ)[None, :, None]
        + eigen_line(EY)[:, None, None]
        + eigen_line(EX)[None, None, :]
    )
    inverse = np.zeros((EY, EZ, UX), np.float32)
    inverse[:, :, :EX] = 1.0 / (mass_term + bend_mean * spectrum**2 + split_term * spectrum)
    tables = []
    for table in (column, column.T):
        tables += halves(table)
    for table in (row_fwd, row_fwd.T, sine_table(EZ)):
        high, low = halves(table)
        tables.append(jnp.concatenate([high, low, high], axis=1))
    return tables + [jnp.asarray(inverse)]


def cut(values):
    high = values.astype(bf16)
    return high, (values - high.astype(f32)).astype(bf16)


def mul(a, b):
    return lax.dot_general(a, b, (((1,), (0,)), ((), ())), preferred_element_type=f32)


def mul3(a, b):
    return mul(a[0], b[0]) + (mul(a[0], b[1]) + mul(a[1], b[0]))


def lanes():
    return lax.broadcasted_iota(jnp.int32, (8, 128), 1)


def subs():
    return lax.broadcasted_iota(jnp.int32, (8, 128), 0)


def spin(values, shift, axis):
    size = values.shape[axis]
    shift = shift % size
    return values if shift == 0 else pltpu.roll(values, shift, axis)


def pack(into, values, lead, width, at):
    lane = lax.broadcasted_iota(jnp.int32, values.shape, 1)
    inside = (lane >= width * at) & (lane < width * (at + 1))
    moved = spin(values, lead + width * at, 1)
    return jnp.where(inside, moved, 0.0 if into is None else into)


def unpack(packed, lead, width, at):
    moved = spin(packed, -(lead + width * at), 1)
    lane = lax.broadcasted_iota(jnp.int32, packed.shape, 1)
    return jnp.where((lane >= 128 - lead) | (lane < width - lead), moved, 0.0)


class Later:
    def __init__(self):
        self.kept = []

    def put(self, ref, index, values):
        self.kept.append((ref, index, values))

    def flush(self):
        for ref, index, values in self.kept:
            ref[index] = values
        self.kept = []


def row_product(table, values):
    out, step = [], 2 * EY
    for at in range(0, values.shape[0], step):
        high, low = cut(values[at : at + step])
        out.append(mul(table, jnp.concatenate([high, high, low], axis=0)))
    return jnp.concatenate(out, axis=0)


def depth_product(table, values):
    high = values.astype(bf16).astype(f32)
    return mul(table, jnp.concatenate([high, high, values - high], axis=0).astype(bf16))


def forward(values, tables, later, parts, z):
    count = values.shape[0] * EY
    values = mul3(cut(values.reshape(count, UX)), (tables[0][...], tables[1][...]))
    values = row_product(tables[4][...], values)
    later.flush()
    for side in (0, 1):
        columns = slice(128 * side, 128 * side + 128)
        later.put(parts[side], slice(z * EY, z * EY + count), values[:, columns])


def finish_solve(parts, solved, tables, inverse, shape, low, high):
    column, row, depth = (tables[2][...], tables[3][...]), tables[5][...], tables[6][...]
    for b in range(EY):
        rows = pl.ds(b, EZ, stride=EY)
        values = jnp.concatenate([parts[0][rows, :], parts[1][rows, :]], axis=1)
        values = depth_product(depth, depth_product(depth, values) * inverse[b])
        parts[0][rows, :] = values[:, :CX]
        parts[1][rows, :] = values[:, CX:]

    later = Later()
    for z in range(0, EZ, GROUP):
        rows = slice(z * EY, (z + GROUP) * EY)
        values = jnp.concatenate([parts[0][rows, :], parts[1][rows, :]], axis=1)
        values = mul3(cut(row_product(row, values)), column).reshape(GROUP, EY, UX)
        later.flush()
        later.put(solved, slice(z, z + GROUP), values)
    later.flush()

    lane = lanes()
    for first in range(0, EZ, shape.per):
        for tile in range(5):
            rows = slice(8 * tile, 8 * tile + 8)
            packed = [None, None]
            for j in range(min(shape.per, EZ - first)):
                near, far = solved[first + j, rows, :CX], solved[first + j, rows, CX:]
                packed[0] = pack(
                    packed[0], jnp.where(lane >= 124, far, near), OV, shape.width, j
                )
                packed[1] = pack(
                    packed[1],
                    jnp.where(lane >= 128 - shape.halo, near, far),
                    shape.halo,
                    shape.width,
                    j,
                )
            low[first // shape.per * 5 + tile] = packed[0]
            high[first // shape.per * 5 + tile] = packed[1]


def column_folded(solved, from_left, from_right, shape, z, tile):
    lane, rows = lanes(), slice(8 * tile, 8 * tile + 8)
    at, j = z // shape.per * 5 + tile, z % shape.per
    left = unpack(from_left[at], shape.halo, shape.width, j)
    right = unpack(from_right[at], OV, shape.width, j)
    return (
        solved[z, rows, :CX] + jnp.where(lane < 64, left, right),
        solved[z, rows, CX:] + jnp.where(lane < 64, right, left),
    )


def row_strips_kernel(shape, solved, low, high):
    sub = subs()
    for strip, cut_at, upper, lower, keep in (
        (low, 4, 4, 0, 4),
        (high, shape.cut_near, 3, 4, 2),
    ):
        extra_a = extra_b = None
        for quad in range(EZ // 4):
            rest = [None, None]
            for j in range(4):
                z = 4 * quad + j
                for side in (0, 1):
                    columns = slice(128 * side, 128 * side + 128)
                    lower_tile = solved[z, 8 * lower : 8 * lower + 8, columns]
                    upper_tile = solved[z, 8 * upper : 8 * upper + 8, columns]
                    main = jnp.where(sub >= cut_at, upper_tile, lower_tile)
                    if side == 0:
                        strip[z] = main
                    else:
                        extra_a = pack(extra_a if z % 16 else None, main, OV, 2 * OV, z % 16)
                        if z % 16 == 15 or z + 1 == EZ:
                            strip[shape.extra_a + z // 16] = extra_a
                    if not shape.last:
                        inside = (sub >= 2 * j) & (sub < 2 * j + 2)
                        moved = spin(lower_tile, 2 * j - keep, 0)
                        rest[side] = jnp.where(inside, moved, rest[side] if j else 0.0)
            if not shape.last:
                strip[EZ + quad] = rest[0]
                extra_b = pack(extra_b, rest[1], OV, 2 * OV, quad)
        if not shape.last:
            strip[shape.extra_b] = extra_b


def corners_kernel(shape, from_left, from_right, low, high):
    sub, groups = subs(), shape.x_groups
    for strip, cut_at, upper, lower, keep in (
        (low, 4, 4, 0, 4),
        (high, shape.cut_near, 3, 4, 2),
    ):
        rest = None
        for k in range(2 * groups):
            source = (from_left, from_right)[k // groups]
            lower_tile = source[k % groups * 5 + lower]
            strip[k] = jnp.where(sub >= cut_at, source[k % groups * 5 + upper], lower_tile)
            if shape.last:
                continue
            j = k % 4
            inside = (sub >= 2 * j) & (sub < 2 * j + 2)
            rest = jnp.where(inside, spin(lower_tile, 2 * j - keep, 0), rest if j else 0.0)
            if j == 3 or k + 1 == 2 * groups:
                strip[2 * groups + k // 4] = rest


def widen_kernel(shape, solved, from_left, from_right, folded):
    sub = subs()
    for z in range(EZ):
        for tile in range(5):
            values = column_folded(solved, from_left, from_right, shape, z, tile)
            for side in (0, 1):
                columns = slice(128 * side, 128 * side + 128)
                value = values[side]
                if tile == 4:
                    folded[z, 40:48, columns] = jnp.where(sub >= 4, value, 0.0)
                    value = jnp.where(sub < 4, value, 0.0)
                folded[z, 8 * tile : 8 * tile + 8, columns] = value


def row_part(strip, shape, z, side, keep):
    sub = subs()
    if side == 0:
        main = strip[z]
    else:
        main = unpack(strip[shape.extra_a + z // 16], OV, 2 * OV, z % 16)
    if shape.last:
        return main, jnp.zeros((8, 128), f32)
    if side == 0:
        rest = strip[EZ + z // 4]
    else:
        rest = unpack(strip[shape.extra_b], OV, 2 * OV, z // 4)
    moved = spin(rest, keep - 2 * (z % 4), 0)
    return main, jnp.where((sub >= keep) & (sub < keep + 2), moved, 0.0)


def depth_strips_kernel(
    shape, widened, from_near, from_far, corner_near, corner_far, folded, low, high, corners
):
    sub, lane, cut_at = subs(), lanes(), shape.cut_near
    groups = shape.x_groups
    for k in range(2 * groups):
        for strip, keep in ((corner_near, 2), (corner_far, 4)):
            main, rest = strip[k], 0.0
            if not shape.last:
                moved = spin(strip[2 * groups + k // 4], keep - 2 * (k % 4), 0)
                rest = jnp.where((sub >= keep) & (sub < keep + 2), moved, 0.0)
            if keep == 2:
                corners[0, k] = jnp.where(sub < cut_at, main, rest)
                corners[1, k] = jnp.where(sub >= cut_at, main, 0.0)
            else:
                corners[2, k] = jnp.where(sub >= 4, main, 0.0)
                corners[3, k] = jnp.where(sub < 4, main, rest)
    for z in range(EZ):
        group, j = z // shape.per, z % shape.per
        new = {}
        for side in (0, 1):
            main, rest = row_part(from_near, shape, z, side, 2)
            new[0, side] = jnp.where(sub < cut_at, main, rest)
            new[5, side] = jnp.where(sub >= cut_at, main, 0.0)
            main, rest = row_part(from_far, shape, z, side, 4)
            new[3, side] = jnp.where(sub >= 4, main, 0.0)
            new[4, side] = jnp.where(sub < 4, main, rest)
        for at, tile in enumerate((0, 5, 3, 4)):
            left = unpack(corners[at, group], shape.halo, shape.width, j)
            right = unpack(corners[at, groups + group], OV, shape.width, j)
            new[tile, 0] += jnp.where(lane < 64, left, right)
            new[tile, 1] += jnp.where(lane < 64, right, left)
        for side in (0, 1):
            columns = slice(128 * side, 128 * side + 128)
            for tile in range(6):
                rows = slice(8 * tile, 8 * tile + 8)
                value = widened[z, rows, columns]
                if (tile, side) in new:
                    value = value + new[tile, side]
                folded[z, rows, columns] = value
    for strip, start in ((low, 0), (high, EZ - shape.rim)):
        extra = None
        for i in range(shape.rim):
            strip[i] = folded[start + i, :, :CX]
            extra = pack(extra, folded[start + i, :, CX:], shape.halo, 2 * shape.halo, i)
        strip[shape.rim] = extra


def laplace(below, centre, above):
    beside = below + above
    beside = beside + (pltpu.roll(centre, 1, 0) + pltpu.roll(centre, UY - 1, 0))
    beside = beside + (pltpu.roll(centre, 1, 1) + pltpu.roll(centre, UX - 1, 1))
    return 6.0 * centre - beside


def operate(get, shift, span, flux, weighted, stiffness, wide, core, unroll):
    start, stop = span

    def chunks(body, start, stop, carry):
        size = CHUNK
        while (stop - start) % size:
            size -= 1
        return lax.fori_loop(
            0,
            (stop - start) // size,
            lambda i, c: body(start + size * i, size, c),
            carry,
            unroll=unroll,
        )

    def first(at, size, carry):
        later = Later()
        for z in [at + i for i in range(size)]:
            values = laplace(get(z - 1), get(z), get(z + 1))
            later.put(flux, z - shift, values)
            later.put(weighted, z - shift, stiffness[z] * values)
        later.flush()
        return carry

    chunks(first, start - 1, stop + 1, 0)
    sub = lax.broadcasted_iota(jnp.int32, (8, UX), 0)

    def second(base, size, carry, use_core):
        later = Later()
        for z in [base + i for i in range(size)]:
            own = get(z)
            at = z - shift
            values = laplace(weighted[at - 1], weighted[at], weighted[at + 1])
            values = mass_term * own + values + split_term * flux[at]
            if wide is not None:
                later.put(wide, (z - 2, slice(0, CY)), values[:CY])
                last = jnp.where(sub < 4, values[CY : CY + 8], values[CY + 8 :])
                later.put(wide, (z - 2, slice(CY, EY)), last)
            if use_core:
                carry = core(z, own[:CY, :CX], values[:CY, :CX], carry, later)
        later.flush()
        return carry

    return lambda first_z, last_z, carry, use_core: chunks(
        lambda z, size, c: second(z, size, c, use_core), first_z, last_z, carry
    )


def add_up(total, product):
    return total + ((product[0:8] + product[8:16]) + (product[16:24] + product[24:32]))


def core_step(count, rhs, earlier, smooth, image):
    def step(z, own, core, totals, later):
        at = z - 6
        later.put(smooth, at, own)
        later.put(image, at, core)
        new = [add_up(totals[0], own * rhs[at])]
        for i in range(count):
            new.append(add_up(totals[1 + i], core * earlier[i][at]))
        new.append(add_up(totals[1 + count], core * own))
        return tuple(new)

    return step


def inner_kernel(count, shape, *refs):
    folded, stiffness, rhs = refs[:3]
    earlier, refs = refs[3 : 3 + count], refs[3 + count :]
    tables = ()
    if not shape.last:
        tables, refs = refs[:TABLES], refs[TABLES:]
    smooth, image, sums = refs[:3]
    wide, halves_out = (None, None) if shape.last else (refs[-3], refs[3:5])
    flux, weighted = refs[-2:]
    step = core_step(count, rhs, earlier, smooth, image)
    run = operate(
        lambda z: folded[z - 2], 10, (12, 48), flux, weighted, stiffness, wide, step, 6
    )
    totals = run(12, 48, (jnp.zeros((8, 128), f32),) * (count + 2), True)
    for i, value in enumerate(totals):
        sums[i] = value
    if not shape.last:
        later = Later()
        for z, layers in INNER:
            forward(wide[z : z + layers], tables, later, halves_out, z)
        later.flush()


def outer_kernel(count, shape, *refs):
    folded, from_below, from_above, stiffness, rhs = refs[:5]
    earlier, refs = refs[5 : 5 + count], refs[5 + count :]
    smooth_in, image_in, sums_in = refs[:3]
    refs = refs[3:]
    wide = None
    if shape.last:
        parts, refs = refs[:count], refs[count:]
    else:
        halves_in, inverse = refs[:2], refs[2]
        tables, refs = refs[3 : 3 + TABLES], refs[3 + TABLES :]
        wide, halves_out = refs[-4], refs[-6:-4]
    smooth, image, sums = refs[:3]
    full, flux, weighted = refs[-3:]
    smooth[6:42] = smooth_in[6:42]
    image[6:42] = image_in[6:42]
    edge = 10 - shape.rim
    step = core_step(count, rhs, earlier, smooth, image)
    totals = tuple(sums_in[i] for i in range(count + 2))
    first_z = 6 if shape.last else 2
    for strip, base, shift, to in ((from_below, edge, 0, 0), (from_above, 50, 46, 14)):
        for z in range(14):
            layer, place = z + shift, z + to
            if not (4 if shape.last else 0) <= layer < (56 if shape.last else 60):
                continue
            at = layer - base
            inside = 2 <= layer < UZ - 2
            if 0 <= at < shape.rim:
                extra = unpack(strip[shape.rim], shape.halo, 2 * shape.halo, at)
                if inside:
                    full[place, :, :CX] = folded[layer - 2, :, :CX] + strip[at]
                    full[place, :, CX:] = folded[layer - 2, :, CX:] + extra
                else:
                    full[place, :, :CX] = strip[at]
                    full[place, :, CX:] = extra
            else:
                full[place] = folded[layer - 2]

    def both(i, low_z, high_z):
        return ((low_z + i, low_z + i), (high_z + i, high_z + i - 32))

    def first(i, carry):
        later = Later()
        for z, at in both(i, first_z - 1, 47):
            values = laplace(full[at - 1], full[at], full[at + 1])
            later.put(flux, at, values)
            later.put(weighted, at, stiffness[z] * values)
        later.flush()
        return carry

    lax.fori_loop(0, 14 - first_z, first, 0, unroll=2)
    sub = lax.broadcasted_iota(jnp.int32, (8, UX), 0)

    def second(i, carry, cores):
        later = Later()
        for (z, at), use_core in zip(both(i, first_z, 48), cores):
            own = full[at]
            values = laplace(weighted[at - 1], weighted[at], weighted[at + 1])
            values = mass_term * own + values + split_term * flux[at]
            if wide is not None:
                later.put(wide, (z - 2, slice(0, CY)), values[:CY])
                last = jnp.where(sub < 4, values[CY : CY + 8], values[CY + 8 :])
                later.put(wide, (z - 2, slice(CY, EY)), last)
            if use_core:
                carry = step(z, own[:CY, :CX], values[:CY, :CX], carry, later)
        later.flush()
        return carry

    if shape.last:
        spans = ((0, 6, (True, True)),)
    else:
        spans = ((0, 4, (False, True)), (4, 6, (True, True)), (6, 10, (True, False)))
    for start, stop, cores in spans:
        totals = lax.fori_loop(
            start, stop, functools.partial(second, cores=cores), totals, unroll=2
        )
    if not shape.last:
        for i, value in enumerate(totals):
            sums[i] = value
        solved, low, high = refs[3:6]
        for part, source in zip(halves_out, halves_in):
            part[10 * EY : 46 * EY] = source[10 * EY : 46 * EY]
        later = Later()
        for z, layers in OUTER:
            forward(wide[z : z + layers], tables, later, halves_out, z)
        later.flush()
        finish_solve(
            halves_out, solved, tables, inverse, Shape(count + 2 == ITERS), low, high
        )
        return
    lane = lanes()
    values = [part[i] for part in parts for i in range(part.shape[0])] + list(totals)
    gathered = jnp.zeros((8, 128), f32)
    for i, value in enumerate(values):
        value = jnp.sum(jnp.sum(value, axis=0, keepdims=True), axis=1, keepdims=True)
        gathered = jnp.where(lane == i, value, gathered)
    sums[...] = gathered


def start_columns_kernel(rhs, stiffness, low, high):
    for source, base, width in ((rhs, 0, 4), (stiffness, 8, 5)):
        per = 128 // width
        for first in range(0, CZ, per):
            for tile in range(4):
                packed = [None, None]
                for j in range(min(per, CZ - first)):
                    values = source[first + j, 8 * tile : 8 * tile + 8, :]
                    packed[0] = pack(packed[0], values, 0, width, j)
                    packed[1] = pack(packed[1], values, width, width, j)
                low[base + first // per * 4 + tile] = packed[0]
                high[base + first // per * 4 + tile] = packed[1]


def ends(left, right, width, j):
    lane = lanes()
    left = spin(left, -(width + width * j), 1)
    right = spin(right, -width * j, 1)
    return jnp.where(lane >= 128 - width, left, jnp.where(lane < width, right, 0.0))


def start_extra(from_left, from_right, base, width, z, tile):
    per = 128 // width
    at = base + z // per * 4 + tile
    return ends(from_left[at], from_right[at], width, z % per)


START_RHS, START_ST, START_ONE, START_Y = 0, 24, 48, 54


def start_rows_kernel(rhs, stiffness, low, high):
    sub = subs()
    strips = ((low, 0), (high, 3))

    def pairing(k, carry):
        for source, main_at in ((rhs, START_RHS), (stiffness, START_ST)):
            for strip, tile in strips:
                rows = slice(8 * tile, 8 * tile + 8)
                a, b = source[2 * k, rows, :], source[2 * k + 1, rows, :]
                if tile == 0:
                    strip[main_at + k] = jnp.where(sub < 4, a, spin(b, 4, 0))
                else:
                    strip[main_at + k] = jnp.where(sub < 4, spin(a, -4, 0), b)
        return carry

    lax.fori_loop(0, CZ // 2, pairing, 0, unroll=4)

    def single(k, carry):
        for strip, tile in strips:
            row = jnp.zeros((8, 128), f32)
            for j in range(8):
                values = stiffness[8 * k + j, 8 * tile : 8 * tile + 8, :]
                moved = spin(values, j - (4 if tile == 0 else 3), 0)
                row = jnp.where(sub == j, moved, row)
            strip[START_ONE + k] = row
        return carry

    lax.fori_loop(0, CZ // 8, single, 0, unroll=2)


def start_corners_kernel(from_left, from_right, low, high):
    for strip, tile in ((low, 0), (high, 3)):
        for group in range(4):
            strip[group] = from_left[4 * group + tile]
            strip[4 + group] = from_right[4 * group + tile]


def start_depth_kernel(
    rhs,
    stiffness,
    from_left,
    from_right,
    from_near,
    from_far,
    corner_near,
    corner_far,
    wide,
    stiff,
    low,
    high,
):
    sub = subs()

    def corner(strip, first, width, z):
        per = 128 // width
        at = first + z // per
        return ends(strip[at], strip[4 + at], width, z % per)

    for z in range(CZ):
        for tile in range(4):
            rows = slice(8 * tile, 8 * tile + 8)
            wide[z, rows, :CX] = rhs[z, rows, :]
            stiff[z + 6, rows, :CX] = stiffness[z, rows, :]
            wide[z, rows, CX:] = start_extra(from_left, from_right, 0, 4, z, tile)
            stiff[z + 6, rows, CX:] = start_extra(from_left, from_right, 8, 5, z, tile)
        odd = z % 2
        far, near = from_far[START_RHS + z // 2], from_near[START_RHS + z // 2]
        far, near = (spin(far, 4, 0), near) if odd else (far, spin(near, 4, 0))
        wide[z, 32:40, :CX] = jnp.where(sub < 4, far, near)
        far, near = corner(corner_far, 0, 4, z), corner(corner_near, 0, 4, z)
        wide[z, 32:40, CX:] = jnp.where(sub < 4, far, near)
        far, near = from_far[START_ST + z // 2], from_near[START_ST + z // 2]
        far, near = (spin(far, 4, 0), near) if odd else (far, spin(near, 4, 0))
        one = spin(from_far[START_ONE + z // 8], 4 - z % 8, 0)
        stiff[z + 6, 32:40, :CX] = jnp.where(sub < 4, far, jnp.where(sub == 4, one, 0.0))
        one = spin(from_near[START_ONE + z // 8], 3 - z % 8, 0)
        stiff[z + 6, 40:48, :CX] = jnp.where(sub >= 4, near, jnp.where(sub == 3, one, 0.0))
        far, near = corner(corner_far, 2, 5, z), corner(corner_near, 2, 5, z)
        stiff[z + 6, 32:40, CX:] = jnp.where(sub <= 4, far, 0.0)
        stiff[z + 6, 40:48, CX:] = jnp.where(sub >= 3, near, 0.0)
    blank = jnp.zeros((8, 128), f32)
    for strip, wide_at, stiff_at in ((low, 0, 6), (high, CZ - 4, CZ + 1)):
        extra = None
        for i in range(4):
            strip[i, :40] = wide[wide_at + i, :, :CX]
            strip[i, 40:48] = blank
        for i in range(5):
            strip[4 + i] = stiff[stiff_at + i, :, :CX]
            extra = pack(extra, stiff[stiff_at + i, :, CX:], 5, 10, i)
        strip[9] = extra
        for tile in range(5):
            rows = slice(8 * tile, 8 * tile + 8)
            extra = strip[9, rows, :]
            for i in range(4):
                lane = lanes()
                moved = spin(wide[wide_at + i, rows, CX:], 4 + 64 + 8 * i, 1)
                inside = (lane >= 64 + 8 * i) & (lane < 72 + 8 * i)
                extra = jnp.where(inside, moved, extra)
            strip[9, rows, :] = extra


def start_inner_kernel(wide, *refs):
    tables, halves_out = refs[:TABLES], refs[TABLES:]
    later = Later()
    for z in range(4, 52, GROUP):
        forward(wide[z - 4 : z], tables, later, halves_out, z)
    later.flush()


def start_outer_kernel(from_below, from_above, stiff_in, *refs):
    halves_in, inverse = refs[:2], refs[2]
    tables, refs = refs[3 : 3 + TABLES], refs[3 + TABLES :]
    solved, stiff, low, high, edge = refs[:5]
    halves_out, later = refs[5:], Later()
    for part, source in zip(halves_out, halves_in):
        part[4 * EY : 52 * EY] = source[4 * EY : 52 * EY]
    stiff[6:54] = stiff_in[6:54]
    for strip, first, stiff_at in ((from_below, 0, 1), (from_above, 52, 54)):
        lane = lax.broadcasted_iota(jnp.int32, (EY, CX), 1)
        for i in range(4):
            edge[i, :, :CX] = strip[i, :40]
            moved = spin(strip[9, :40], -(4 + 64 + 8 * i), 1)
            edge[i, :, CX:] = jnp.where((lane >= 124) | (lane < 4), moved, 0.0)
        for i in range(5):
            stiff[stiff_at + i, :, :CX] = strip[4 + i]
            stiff[stiff_at + i, :, CX:] = unpack(strip[9], 5, 10, i)
        forward(edge[...], tables, later, halves_out, first)
        later.flush()
    finish_solve(halves_out, solved, tables, inverse, Shape(False), low, high)


def weights(b, pair):
    sigma = [jnp.zeros((1, 1), f32)] * ITERS
    delta = None
    current = None
    for turn in range(ITERS):
        zeta = [jnp.ones((1, 1), f32)] + [-s for s in sigma[:turn]]
        following = sum(z * b[i] for i, z in enumerate(zeta))
        for i, z in enumerate(zeta):
            for j in range(turn):
                following = following - z * sigma[j] * pair[i, j]
        if turn == 0:
            delta = zeta
        else:
            ratio = following / current
            delta = [z + ratio * d for z, d in zip(zeta, delta + [jnp.zeros((1, 1), f32)])]
        current = following
        bending = sum(
            delta[i] * delta[j] * pair[i, j] for i in range(turn + 1) for j in range(turn + 1)
        )
        step = current / bending
        sigma = [
            s + step * d for s, d in zip(sigma, delta + [jnp.zeros((1, 1), f32)] * (ITERS - turn - 1))
        ]
    return sigma


def combine_kernel(
    sums, rhs, u0, u1, u2, w0, w1, w2, answer_out, rest_out, answer, rest, done
):
    picked = [
        jnp.sum(jnp.where(lanes()[:1] == i, sums[:1], 0.0), axis=1, keepdims=True)
        for i in range(ITERS * (ITERS + 3) // 2)
    ]
    b, pair, at = [], {}, 0
    for j in range(ITERS):
        b.append(picked[at])
        for i in range(j + 1):
            pair[i, j] = pair[j, i] = picked[at + 1 + i]
        at += j + 2
    s = weights(b, pair)

    def step(z, carry):
        answer[z] = s[0] * u0[z] + s[1] * u1[z] + s[2] * u2[z]
        rest[z] = rhs[z] - (s[0] * w0[z] + s[1] * w1[z] + s[2] * w2[z])
        return carry

    layers, copies = CZ // PIECES, []
    for k in range(PIECES):
        lax.fori_loop(k * layers, (k + 1) * layers, step, 0, unroll=4)
        part = pl.ds(k * layers, layers)
        for i, (source, target) in enumerate(((answer, answer_out), (rest, rest_out))):
            copies.append(
                pltpu.make_async_copy(source.at[part], target.at[part], done.at[i, k])
            )
            copies[-1].start()
    for copy in copies:
        copy.wait()


VMEM = pl.BlockSpec(memory_space=pltpu.VMEM)
HBM = pl.BlockSpec(memory_space=pl.ANY)


def call(kernel, shapes, operands, scratch=(), cost=2.0, outside=False):
    return pl.pallas_call(
        kernel,
        out_shape=[jax.ShapeDtypeStruct(shape, f32) for shape in shapes],
        in_specs=[VMEM] * len(operands),
        out_specs=[HBM if outside else VMEM] * len(shapes),
        scratch_shapes=[pltpu.VMEM(shape, f32) for shape in scratch]
        + ([pltpu.SemaphoreType.DMA((2, PIECES))] if outside else []),
        cost_estimate=pl.CostEstimate(
            flops=int(cost * 1e9), bytes_accessed=int(cost * 3.6e6), transcendentals=0
        ),
        compiler_params=pltpu.CompilerParams(vmem_limit_bytes=24 * 2**20),
    )(*operands)


def shifted(block, axis, step):
    count = lax.axis_size(axis)
    return lax.ppermute(block, axis, [(i, (i + step) % count) for i in range(count)])


def swap(low, high, axis):
    return shifted(high, axis, 1), shifted(low, axis, -1)


def ring(values, axes, count, low, size):
    parts = []
    for step in range(1, size):
        route = []
        for i in range(count):
            place = i // low % size
            route.append((i, i + ((place + step) % size - place) * low))
        parts.append(lax.ppermute(values, axes, route))
    return values + sum(parts[1:], parts[0])


def total(values):
    values = ring(values, "gy", 4, 1, 2)
    values = ring(values, ("gx", "gy"), 32, 2, 4)
    values = ring(values, "gx", 8, 2, 4)
    return ring(values, "gz", 4, 1, 4)


CORE = (CZ, CY, CX)
FIELD = (EZ, EY, UX)
PART = (EZ * EY, CX)


def per_device(rhs_field, stiffness):
    *tables, inverse = solve_tables()
    strips = call(start_columns_kernel, [(16, 8, 128)] * 2, [rhs_field, stiffness])
    columns = swap(*strips, "gx")
    fields = [rhs_field, stiffness, *columns]
    strips = call(start_rows_kernel, [(START_Y, 8, 128)] * 2, fields[:2], cost=1.0)
    rows = swap(*strips, "gy")
    strips = call(start_corners_kernel, [(8, 8, 128)] * 2, columns, cost=5.0)
    corners = swap(*strips, "gy")
    wide, stiff, *strips = call(
        start_depth_kernel,
        [(CZ, EY, UX), (UZ, UY, UX)] + [(10, UY, CX)] * 2,
        [*fields, *rows, *corners],
    )
    depths = swap(*strips, "gz")
    fields = call(start_inner_kernel, [PART] * 2, [wide, *tables], cost=4.0)
    shape = Shape(False)
    solved, stiff, *strips = call(
        start_outer_kernel,
        [FIELD, (UZ, UY, UX)] + [(shape.x_tiles, 8, 128)] * 2,
        [*depths, stiff, *fields, inverse, *tables],
        [(4, EY, UX), PART, PART],
        cost=6.0,
    )
    smooth, image, sums = [], [], []
    for turn in range(ITERS):
        shape = Shape(turn + 1 == ITERS)
        columns = swap(*strips, "gx")
        strips = call(
            functools.partial(row_strips_kernel, shape),
            [(shape.y_tiles, 8, 128)] * 2,
            [solved],
            cost=1.0,
        )
        rows = swap(*strips, "gy")
        strips = call(
            functools.partial(corners_kernel, shape), [(shape.c_tiles, 8, 128)] * 2, columns, cost=5.0
        )
        corners = swap(*strips, "gy")
        widened = call(
            functools.partial(widen_kernel, shape), [(EZ, UY, UX)], [solved, *columns]
        )[0]
        folded, *strips = call(
            functools.partial(depth_strips_kernel, shape),
            [(EZ, UY, UX)] + [(shape.rim + 1, UY, CX)] * 2,
            [widened, *rows, *corners],
            [(4, 2 * shape.x_groups, 8, 128)],
        )
        depths = swap(*strips, "gz")
        products = (turn + 2, 8, 128)
        outs = [CORE, CORE, products]
        if not shape.last:
            outs += [PART, PART]
        own, core, part, *fields = call(
            functools.partial(inner_kernel, turn, shape),
            outs,
            [folded, stiff, rhs_field, *smooth] + ([] if shape.last else tables),
            ([] if shape.last else [FIELD]) + [(40, UY, UX)] * 2,
            cost=6.0,
        )
        operands = [folded, *depths, stiff, rhs_field, *smooth]
        operands += [own, core, part]
        scratch = [(28, UY, UX)] * 3
        if shape.last:
            operands += sums
            outs = [CORE, CORE, (8, 128)]
        else:
            operands += [*fields, inverse, *tables]
            following = Shape(turn + 2 == ITERS)
            outs = [CORE, CORE, products, FIELD] + [(following.x_tiles, 8, 128)] * 2
            scratch = [PART, PART, FIELD] + scratch
        own, core, part, *rest = call(
            functools.partial(outer_kernel, turn, shape),
            outs,
            operands,
            scratch,
            cost=8.0,
        )
        if rest:
            solved, *strips = rest
        smooth.append(own)
        image.append(core)
        sums.append(part)
    operands = [total(sums[-1]), rhs_field, *smooth, *image]
    return tuple(call(combine_kernel, [CORE] * 2, operands, [CORE] * 2, outside=True))


def solution(mesh):
    in_specs = (P("gz", "gy", "gx"), P("gz", "gy", "gx"))
    out_specs = (P("gz", "gy", "gx"), P("gz", "gy", "gx"))
    return jax.shard_map(
        per_device, mesh=mesh, in_specs=in_specs, out_specs=out_specs, check_vma=False
    )
```

```python
import functools

import jax
import jax.numpy as jnp
import numpy as np
from jax import lax
from jax.experimental import pallas as pl
from jax.experimental.pallas import tpu as pltpu
from jax.sharding import PartitionSpec as P

OV = 4
ITERS = 3
CZ, CY, CX = 48, 32, 128
EZ, EY, EX = CZ + 2 * OV, CY + 2 * OV, CX + 2 * OV
UZ, UY, UX = CZ + 12, 48, 256
GROUP = 4
PIECES = 4
TABLES = 7
CHUNK = 2
INNER = [(z, 4) for z in range(10, 46, 4)]
OUTER = [(0, 6), (6, 4), (46, 6), (52, 4)]


class Shape:
    def __init__(self, last):
        self.rim = 6 if last else 10
        self.halo = 4 if last else 6
        self.width = 4 + self.halo
        self.per = 128 // self.width
        self.x_tiles = -(-EZ // self.per) * 5
        self.x_groups = self.x_tiles // 5
        self.extra_a = EZ if last else EZ + EZ // 4
        self.extra_b = self.extra_a + -(-EZ // 16)
        self.y_tiles = self.extra_b + (0 if last else 1)
        self.cut_near = 4 if last else 2
        self.c_tiles = 2 * self.x_groups + (0 if last else -(-self.x_groups // 2))
        self.last = last


mass_term = 1e-05
split_term = 0.5
bend_mean = 0.1
f32, bf16 = jnp.float32, jnp.bfloat16


def sine_table(length):
    places = np.arange(1, length + 1, dtype=np.float64)
    return np.sqrt(2.0 / (length + 1)) * np.sin(
        np.pi * places[:, None] * places[None, :] / (length + 1)
    )


def eigen_line(length):
    places = np.arange(1, length + 1, dtype=np.float64)
    return 2.0 - 2.0 * np.cos(np.pi * places / (length + 1))


def halves(table):
    high = np.asarray(table, np.float32).astype(jnp.bfloat16)
    low = (np.asarray(table, np.float64) - high.astype(np.float64)).astype(jnp.bfloat16)
    return [jnp.asarray(high), jnp.asarray(low)]


def solve_tables():
    column = np.zeros((UX, UX))
    full = sine_table(EX)
    for lane in range(UX):
        place = lane + OV if lane < CX + OV else lane - UX + OV
        if 0 <= place < EX:
            column[lane, :EX] = full[place]
    rows = np.roll(sine_table(EY), -OV, axis=0)
    row_fwd = np.kron(np.eye(2), rows.T)
    spectrum = (
        eigen_line(EZ)[None, :, None]
        + eigen_line(EY)[:, None, None]
        + eigen_line(EX)[None, None, :]
    )
    inverse = np.zeros((EY, EZ, UX), np.float32)
    inverse[:, :, :EX] = 1.0 / (mass_term + bend_mean * spectrum**2 + split_term * spectrum)
    tables = []
    for table in (column, column.T):
        tables += halves(table)
    for table in (row_fwd, row_fwd.T, sine_table(EZ)):
        high, low = halves(table)
        tables.append(jnp.concatenate([high, low, high], axis=1))
    return tables + [jnp.asarray(inverse)]


def cut(values):
    high = values.astype(bf16)
    return high, (values - high.astype(f32)).astype(bf16)


def mul(a, b):
    return lax.dot_general(a, b, (((1,), (0,)), ((), ())), preferred_element_type=f32)


def mul3(a, b):
    return mul(a[0], b[0]) + (mul(a[0], b[1]) + mul(a[1], b[0]))


def lanes():
    return lax.broadcasted_iota(jnp.int32, (8, 128), 1)


def subs():
    return lax.broadcasted_iota(jnp.int32, (8, 128), 0)


def spin(values, shift, axis):
    size = values.shape[axis]
    shift = shift % size
    return values if shift == 0 else pltpu.roll(values, shift, axis)


def pack(into, values, lead, width, at):
    lane = lax.broadcasted_iota(jnp.int32, values.shape, 1)
    inside = (lane >= width * at) & (lane < width * (at + 1))
    moved = spin(values, lead + width * at, 1)
    return jnp.where(inside, moved, 0.0 if into is None else into)


def unpack(packed, lead, width, at):
    moved = spin(packed, -(lead + width * at), 1)
    lane = lax.broadcasted_iota(jnp.int32, packed.shape, 1)
    return jnp.where((lane >= 128 - lead) | (lane < width - lead), moved, 0.0)


class Later:
    def __init__(self):
        self.kept = []

    def put(self, ref, index, values):
        self.kept.append((ref, index, values))

    def flush(self):
        for ref, index, values in self.kept:
            ref[index] = values
        self.kept = []


def row_product(table, values):
    out, step = [], 2 * EY
    for at in range(0, values.shape[0], step):
        high, low = cut(values[at : at + step])
        out.append(mul(table, jnp.concatenate([high, high, low], axis=0)))
    return jnp.concatenate(out, axis=0)


def depth_product(table, values):
    high = values.astype(bf16).astype(f32)
    return mul(table, jnp.concatenate([high, high, values - high], axis=0).astype(bf16))


def forward(values, tables, later, parts, z):
    count = values.shape[0] * EY
    values = mul3(cut(values.reshape(count, UX)), (tables[0][...], tables[1][...]))
    values = row_product(tables[4][...], values)
    later.flush()
    for side in (0, 1):
        columns = slice(128 * side, 128 * side + 128)
        later.put(parts[side], slice(z * EY, z * EY + count), values[:, columns])


def finish_solve(parts, solved, tables, inverse, shape, low, high):
    column, row, depth = (tables[2][...], tables[3][...]), tables[5][...], tables[6][...]
    for b in range(EY):
        rows = pl.ds(b, EZ, stride=EY)
        values = jnp.concatenate([parts[0][rows, :], parts[1][rows, :]], axis=1)
        values = depth_product(depth, depth_product(depth, values) * inverse[b])
        parts[0][rows, :] = values[:, :CX]
        parts[1][rows, :] = values[:, CX:]

    later = Later()
    for z in range(0, EZ, GROUP):
        rows = slice(z * EY, (z + GROUP) * EY)
        values = jnp.concatenate([parts[0][rows, :], parts[1][rows, :]], axis=1)
        values = mul3(cut(row_product(row, values)), column).reshape(GROUP, EY, UX)
        later.flush()
        later.put(solved, slice(z, z + GROUP), values)
    later.flush()

    lane = lanes()
    for first in range(0, EZ, shape.per):
        for tile in range(5):
            rows = slice(8 * tile, 8 * tile + 8)
            packed = [None, None]
            for j in range(min(shape.per, EZ - first)):
                near, far = solved[first + j, rows, :CX], solved[first + j, rows, CX:]
                packed[0] = pack(
                    packed[0], jnp.where(lane >= 124, far, near), OV, shape.width, j
                )
                packed[1] = pack(
                    packed[1],
                    jnp.where(lane >= 128 - shape.halo, near, far),
                    shape.halo,
                    shape.width,
                    j,
                )
            low[first // shape.per * 5 + tile] = packed[0]
            high[first // shape.per * 5 + tile] = packed[1]


def column_folded(solved, from_left, from_right, shape, z, tile):
    lane, rows = lanes(), slice(8 * tile, 8 * tile + 8)
    at, j = z // shape.per * 5 + tile, z % shape.per
    left = unpack(from_left[at], shape.halo, shape.width, j)
    right = unpack(from_right[at], OV, shape.width, j)
    return (
        solved[z, rows, :CX] + jnp.where(lane < 64, left, right),
        solved[z, rows, CX:] + jnp.where(lane < 64, right, left),
    )


def row_strips_kernel(shape, solved, low, high):
    sub = subs()
    for strip, cut_at, upper, lower, keep in (
        (low, 4, 4, 0, 4),
        (high, shape.cut_near, 3, 4, 2),
    ):
        extra_a = extra_b = None
        for quad in range(EZ // 4):
            rest = [None, None]
            for j in range(4):
                z = 4 * quad + j
                for side in (0, 1):
                    columns = slice(128 * side, 128 * side + 128)
                    lower_tile = solved[z, 8 * lower : 8 * lower + 8, columns]
                    upper_tile = solved[z, 8 * upper : 8 * upper + 8, columns]
                    main = jnp.where(sub >= cut_at, upper_tile, lower_tile)
                    if side == 0:
                        strip[z] = main
                    else:
                        extra_a = pack(extra_a if z % 16 else None, main, OV, 2 * OV, z % 16)
                        if z % 16 == 15 or z + 1 == EZ:
                            strip[shape.extra_a + z // 16] = extra_a
                    if not shape.last:
                        inside = (sub >= 2 * j) & (sub < 2 * j + 2)
                        moved = spin(lower_tile, 2 * j - keep, 0)
                        rest[side] = jnp.where(inside, moved, rest[side] if j else 0.0)
            if not shape.last:
                strip[EZ + quad] = rest[0]
                extra_b = pack(extra_b, rest[1], OV, 2 * OV, quad)
        if not shape.last:
            strip[shape.extra_b] = extra_b


def corners_kernel(shape, from_left, from_right, low, high):
    sub, groups = subs(), shape.x_groups
    for strip, cut_at, upper, lower, keep in (
        (low, 4, 4, 0, 4),
        (high, shape.cut_near, 3, 4, 2),
    ):
        rest = None
        for k in range(2 * groups):
            source = (from_left, from_right)[k // groups]
            lower_tile = source[k % groups * 5 + lower]
            strip[k] = jnp.where(sub >= cut_at, source[k % groups * 5 + upper], lower_tile)
            if shape.last:
                continue
            j = k % 4
            inside = (sub >= 2 * j) & (sub < 2 * j + 2)
            rest = jnp.where(inside, spin(lower_tile, 2 * j - keep, 0), rest if j else 0.0)
            if j == 3 or k + 1 == 2 * groups:
                strip[2 * groups + k // 4] = rest


def widen_kernel(shape, solved, from_left, from_right, folded):
    sub = subs()
    for z in range(EZ):
        for tile in range(5):
            values = column_folded(solved, from_left, from_right, shape, z, tile)
            for side in (0, 1):
                columns = slice(128 * side, 128 * side + 128)
                value = values[side]
                if tile == 4:
                    folded[z, 40:48, columns] = jnp.where(sub >= 4, value, 0.0)
                    value = jnp.where(sub < 4, value, 0.0)
                folded[z, 8 * tile : 8 * tile + 8, columns] = value


def row_part(strip, shape, z, side, keep):
    sub = subs()
    if side == 0:
        main = strip[z]
    else:
        main = unpack(strip[shape.extra_a + z // 16], OV, 2 * OV, z % 16)
    if shape.last:
        return main, jnp.zeros((8, 128), f32)
    if side == 0:
        rest = strip[EZ + z // 4]
    else:
        rest = unpack(strip[shape.extra_b], OV, 2 * OV, z // 4)
    moved = spin(rest, keep - 2 * (z % 4), 0)
    return main, jnp.where((sub >= keep) & (sub < keep + 2), moved, 0.0)


def depth_strips_kernel(
    shape, widened, from_near, from_far, corner_near, corner_far, folded, low, high, corners
):
    sub, lane, cut_at = subs(), lanes(), shape.cut_near
    groups = shape.x_groups
    for k in range(2 * groups):
        for strip, keep in ((corner_near, 2), (corner_far, 4)):
            main, rest = strip[k], 0.0
            if not shape.last:
                moved = spin(strip[2 * groups + k // 4], keep - 2 * (k % 4), 0)
                rest = jnp.where((sub >= keep) & (sub < keep + 2), moved, 0.0)
            if keep == 2:
                corners[0, k] = jnp.where(sub < cut_at, main, rest)
                corners[1, k] = jnp.where(sub >= cut_at, main, 0.0)
            else:
                corners[2, k] = jnp.where(sub >= 4, main, 0.0)
                corners[3, k] = jnp.where(sub < 4, main, rest)
    for z in range(EZ):
        group, j = z // shape.per, z % shape.per
        new = {}
        for side in (0, 1):
            main, rest = row_part(from_near, shape, z, side, 2)
            new[0, side] = jnp.where(sub < cut_at, main, rest)
            new[5, side] = jnp.where(sub >= cut_at, main, 0.0)
            main, rest = row_part(from_far, shape, z, side, 4)
            new[3, side] = jnp.where(sub >= 4, main, 0.0)
            new[4, side] = jnp.where(sub < 4, main, rest)
        for at, tile in enumerate((0, 5, 3, 4)):
            left = unpack(corners[at, group], shape.halo, shape.width, j)
            right = unpack(corners[at, groups + group], OV, shape.width, j)
            new[tile, 0] += jnp.where(lane < 64, left, right)
            new[tile, 1] += jnp.where(lane < 64, right, left)
        for side in (0, 1):
            columns = slice(128 * side, 128 * side + 128)
            for tile in range(6):
                rows = slice(8 * tile, 8 * tile + 8)
                value = widened[z, rows, columns]
                if (tile, side) in new:
                    value = value + new[tile, side]
                folded[z, rows, columns] = value
    for strip, start in ((low, 0), (high, EZ - shape.rim)):
        extra = None
        for i in range(shape.rim):
            strip[i] = folded[start + i, :, :CX]
            extra = pack(extra, folded[start + i, :, CX:], shape.halo, 2 * shape.halo, i)
        strip[shape.rim] = extra


def laplace(below, centre, above):
    beside = below + above
    beside = beside + (pltpu.roll(centre, 1, 0) + pltpu.roll(centre, UY - 1, 0))
    beside = beside + (pltpu.roll(centre, 1, 1) + pltpu.roll(centre, UX - 1, 1))
    return 6.0 * centre - beside


def operate(get, shift, span, flux, weighted, stiffness, wide, core, unroll):
    start, stop = span

    def chunks(body, start, stop, carry):
        size = CHUNK
        while (stop - start) % size:
            size -= 1
        return lax.fori_loop(
            0,
            (stop - start) // size,
            lambda i, c: body(start + size * i, size, c),
            carry,
            unroll=unroll,
        )

    def first(at, size, carry):
        later = Later()
        for z in [at + i for i in range(size)]:
            values = laplace(get(z - 1), get(z), get(z + 1))
            later.put(flux, z - shift, values)
            later.put(weighted, z - shift, stiffness[z] * values)
        later.flush()
        return carry

    chunks(first, start - 1, stop + 1, 0)
    sub = lax.broadcasted_iota(jnp.int32, (8, UX), 0)

    def second(base, size, carry, use_core):
        later = Later()
        for z in [base + i for i in range(size)]:
            own = get(z)
            at = z - shift
            values = laplace(weighted[at - 1], weighted[at], weighted[at + 1])
            values = mass_term * own + values + split_term * flux[at]
            if wide is not None:
                later.put(wide, (z - 2, slice(0, CY)), values[:CY])
                last = jnp.where(sub < 4, values[CY : CY + 8], values[CY + 8 :])
                later.put(wide, (z - 2, slice(CY, EY)), last)
            if use_core:
                carry = core(z, own[:CY, :CX], values[:CY, :CX], carry, later)
        later.flush()
        return carry

    return lambda first_z, last_z, carry, use_core: chunks(
        lambda z, size, c: second(z, size, c, use_core), first_z, last_z, carry
    )


def add_up(total, product):
    return total + ((product[0:8] + product[8:16]) + (product[16:24] + product[24:32]))


def core_step(count, rhs, earlier, smooth, image):
    def step(z, own, core, totals, later):
        at = z - 6
        later.put(smooth, at, own)
        later.put(image, at, core)
        new = [add_up(totals[0], own * rhs[at])]
        for i in range(count):
            new.append(add_up(totals[1 + i], core * earlier[i][at]))
        new.append(add_up(totals[1 + count], core * own))
        return tuple(new)

    return step


def inner_kernel(count, shape, *refs):
    folded, stiffness, rhs = refs[:3]
    earlier, refs = refs[3 : 3 + count], refs[3 + count :]
    tables = ()
    if not shape.last:
        tables, refs = refs[:TABLES], refs[TABLES:]
    smooth, image, sums = refs[:3]
    wide, halves_out = (None, None) if shape.last else (refs[-3], refs[3:5])
    flux, weighted = refs[-2:]
    step = core_step(count, rhs, earlier, smooth, image)
    run = operate(
        lambda z: folded[z - 2], 10, (12, 48), flux, weighted, stiffness, wide, step, 6
    )
    totals = run(12, 48, (jnp.zeros((8, 128), f32),) * (count + 2), True)
    for i, value in enumerate(totals):
        sums[i] = value
    if not shape.last:
        later = Later()
        for z, layers in INNER:
            forward(wide[z : z + layers], tables, later, halves_out, z)
        later.flush()


def outer_kernel(count, shape, *refs):
    folded, from_below, from_above, stiffness, rhs = refs[:5]
    earlier, refs = refs[5 : 5 + count], refs[5 + count :]
    smooth_in, image_in, sums_in = refs[:3]
    refs = refs[3:]
    wide = None
    if shape.last:
        parts, refs = refs[:count], refs[count:]
    else:
        halves_in, inverse = refs[:2], refs[2]
        tables, refs = refs[3 : 3 + TABLES], refs[3 + TABLES :]
        wide, halves_out = refs[-4], refs[-6:-4]
    smooth, image, sums = refs[:3]
    full, flux, weighted = refs[-3:]
    smooth[6:42] = smooth_in[6:42]
    image[6:42] = image_in[6:42]
    edge = 10 - shape.rim
    step = core_step(count, rhs, earlier, smooth, image)
    totals = tuple(sums_in[i] for i in range(count + 2))
    first_z = 6 if shape.last else 2
    for strip, base, shift in ((from_below, edge, 0), (from_above, 50, 46)):
        for z in range(14):
            layer = z + shift
            if not (4 if shape.last else 0) <= layer < (56 if shape.last else 60):
                continue
            at = layer - base
            inside = 2 <= layer < UZ - 2
            if 0 <= at < shape.rim:
                extra = unpack(strip[shape.rim], shape.halo, 2 * shape.halo, at)
                if inside:
                    full[z, :, :CX] = folded[layer - 2, :, :CX] + strip[at]
                    full[z, :, CX:] = folded[layer - 2, :, CX:] + extra
                else:
                    full[z, :, :CX] = strip[at]
                    full[z, :, CX:] = extra
            else:
                full[z] = folded[layer - 2]
        span = (first_z, 12) if shift == 0 else (48, UZ - first_z)
        run = operate(
            lambda z, shift=shift: full[z - shift],
            shift,
            span,
            flux,
            weighted,
            stiffness,
            wide,
            step,
            2,
        )
        if shift == 0:
            if not shape.last:
                run(2, 6, 0, False)
            totals = run(6, 12, totals, True)
        else:
            totals = run(48, 54, totals, True)
            if not shape.last:
                run(54, 58, 0, False)
    if not shape.last:
        for i, value in enumerate(totals):
            sums[i] = value
        solved, low, high = refs[3:6]
        for part, source in zip(halves_out, halves_in):
            part[10 * EY : 46 * EY] = source[10 * EY : 46 * EY]
        later = Later()
        for z, layers in OUTER:
            forward(wide[z : z + layers], tables, later, halves_out, z)
        later.flush()
        finish_solve(
            halves_out, solved, tables, inverse, Shape(count + 2 == ITERS), low, high
        )
        return
    lane = lanes()
    values = [part[i] for part in parts for i in range(part.shape[0])] + list(totals)
    gathered = jnp.zeros((8, 128), f32)
    for i, value in enumerate(values):
        value = jnp.sum(jnp.sum(value, axis=0, keepdims=True), axis=1, keepdims=True)
        gathered = jnp.where(lane == i, value, gathered)
    sums[...] = gathered


def start_columns_kernel(rhs, stiffness, low, high):
    for source, base, width in ((rhs, 0, 4), (stiffness, 8, 5)):
        per = 128 // width
        for first in range(0, CZ, per):
            for tile in range(4):
                packed = [None, None]
                for j in range(min(per, CZ - first)):
                    values = source[first + j, 8 * tile : 8 * tile + 8, :]
                    packed[0] = pack(packed[0], values, 0, width, j)
                    packed[1] = pack(packed[1], values, width, width, j)
                low[base + first // per * 4 + tile] = packed[0]
                high[base + first // per * 4 + tile] = packed[1]


def ends(left, right, width, j):
    lane = lanes()
    left = spin(left, -(width + width * j), 1)
    right = spin(right, -width * j, 1)
    return jnp.where(lane >= 128 - width, left, jnp.where(lane < width, right, 0.0))


def start_extra(from_left, from_right, base, width, z, tile):
    per = 128 // width
    at = base + z // per * 4 + tile
    return ends(from_left[at], from_right[at], width, z % per)


START_RHS, START_ST, START_ONE, START_Y = 0, 24, 48, 54


def start_rows_kernel(rhs, stiffness, low, high):
    sub = subs()
    strips = ((low, 0), (high, 3))

    def pairing(k, carry):
        for source, main_at in ((rhs, START_RHS), (stiffness, START_ST)):
            for strip, tile in strips:
                rows = slice(8 * tile, 8 * tile + 8)
                a, b = source[2 * k, rows, :], source[2 * k + 1, rows, :]
                if tile == 0:
                    strip[main_at + k] = jnp.where(sub < 4, a, spin(b, 4, 0))
                else:
                    strip[main_at + k] = jnp.where(sub < 4, spin(a, -4, 0), b)
        return carry

    lax.fori_loop(0, CZ // 2, pairing, 0, unroll=4)

    def single(k, carry):
        for strip, tile in strips:
            row = jnp.zeros((8, 128), f32)
            for j in range(8):
                values = stiffness[8 * k + j, 8 * tile : 8 * tile + 8, :]
                moved = spin(values, j - (4 if tile == 0 else 3), 0)
                row = jnp.where(sub == j, moved, row)
            strip[START_ONE + k] = row
        return carry

    lax.fori_loop(0, CZ // 8, single, 0, unroll=2)


def start_corners_kernel(from_left, from_right, low, high):
    for strip, tile in ((low, 0), (high, 3)):
        for group in range(4):
            strip[group] = from_left[4 * group + tile]
            strip[4 + group] = from_right[4 * group + tile]


def start_depth_kernel(
    rhs,
    stiffness,
    from_left,
    from_right,
    from_near,
    from_far,
    corner_near,
    corner_far,
    wide,
    stiff,
    low,
    high,
):
    sub = subs()

    def corner(strip, first, width, z):
        per = 128 // width
        at = first + z // per
        return ends(strip[at], strip[4 + at], width, z % per)

    for z in range(CZ):
        for tile in range(4):
            rows = slice(8 * tile, 8 * tile + 8)
            wide[z, rows, :CX] = rhs[z, rows, :]
            stiff[z + 6, rows, :CX] = stiffness[z, rows, :]
            wide[z, rows, CX:] = start_extra(from_left, from_right, 0, 4, z, tile)
            stiff[z + 6, rows, CX:] = start_extra(from_left, from_right, 8, 5, z, tile)
        odd = z % 2
        far, near = from_far[START_RHS + z // 2], from_near[START_RHS + z // 2]
        far, near = (spin(far, 4, 0), near) if odd else (far, spin(near, 4, 0))
        wide[z, 32:40, :CX] = jnp.where(sub < 4, far, near)
        far, near = corner(corner_far, 0, 4, z), corner(corner_near, 0, 4, z)
        wide[z, 32:40, CX:] = jnp.where(sub < 4, far, near)
        far, near = from_far[START_ST + z // 2], from_near[START_ST + z // 2]
        far, near = (spin(far, 4, 0), near) if odd else (far, spin(near, 4, 0))
        one = spin(from_far[START_ONE + z // 8], 4 - z % 8, 0)
        stiff[z + 6, 32:40, :CX] = jnp.where(sub < 4, far, jnp.where(sub == 4, one, 0.0))
        one = spin(from_near[START_ONE + z // 8], 3 - z % 8, 0)
        stiff[z + 6, 40:48, :CX] = jnp.where(sub >= 4, near, jnp.where(sub == 3, one, 0.0))
        far, near = corner(corner_far, 2, 5, z), corner(corner_near, 2, 5, z)
        stiff[z + 6, 32:40, CX:] = jnp.where(sub <= 4, far, 0.0)
        stiff[z + 6, 40:48, CX:] = jnp.where(sub >= 3, near, 0.0)
    blank = jnp.zeros((8, 128), f32)
    for strip, wide_at, stiff_at in ((low, 0, 6), (high, CZ - 4, CZ + 1)):
        extra = None
        for i in range(4):
            strip[i, :40] = wide[wide_at + i, :, :CX]
            strip[i, 40:48] = blank
        for i in range(5):
            strip[4 + i] = stiff[stiff_at + i, :, :CX]
            extra = pack(extra, stiff[stiff_at + i, :, CX:], 5, 10, i)
        strip[9] = extra
        for tile in range(5):
            rows = slice(8 * tile, 8 * tile + 8)
            extra = strip[9, rows, :]
            for i in range(4):
                lane = lanes()
                moved = spin(wide[wide_at + i, rows, CX:], 4 + 64 + 8 * i, 1)
                inside = (lane >= 64 + 8 * i) & (lane < 72 + 8 * i)
                extra = jnp.where(inside, moved, extra)
            strip[9, rows, :] = extra


def start_inner_kernel(wide, *refs):
    tables, halves_out = refs[:TABLES], refs[TABLES:]
    later = Later()
    for z in range(4, 52, GROUP):
        forward(wide[z - 4 : z], tables, later, halves_out, z)
    later.flush()


def start_outer_kernel(from_below, from_above, stiff_in, *refs):
    halves_in, inverse = refs[:2], refs[2]
    tables, refs = refs[3 : 3 + TABLES], refs[3 + TABLES :]
    solved, stiff, low, high, edge = refs[:5]
    halves_out, later = refs[5:], Later()
    for part, source in zip(halves_out, halves_in):
        part[4 * EY : 52 * EY] = source[4 * EY : 52 * EY]
    stiff[6:54] = stiff_in[6:54]
    for strip, first, stiff_at in ((from_below, 0, 1), (from_above, 52, 54)):
        lane = lax.broadcasted_iota(jnp.int32, (EY, CX), 1)
        for i in range(4):
            edge[i, :, :CX] = strip[i, :40]
            moved = spin(strip[9, :40], -(4 + 64 + 8 * i), 1)
            edge[i, :, CX:] = jnp.where((lane >= 124) | (lane < 4), moved, 0.0)
        for i in range(5):
            stiff[stiff_at + i, :, :CX] = strip[4 + i]
            stiff[stiff_at + i, :, CX:] = unpack(strip[9], 5, 10, i)
        forward(edge[...], tables, later, halves_out, first)
        later.flush()
    finish_solve(halves_out, solved, tables, inverse, Shape(False), low, high)


def weights(b, pair):
    sigma = [jnp.zeros((1, 1), f32)] * ITERS
    delta = None
    current = None
    for turn in range(ITERS):
        zeta = [jnp.ones((1, 1), f32)] + [-s for s in sigma[:turn]]
        following = sum(z * b[i] for i, z in enumerate(zeta))
        for i, z in enumerate(zeta):
            for j in range(turn):
                following = following - z * sigma[j] * pair[i, j]
        if turn == 0:
            delta = zeta
        else:
            ratio = following / current
            delta = [z + ratio * d for z, d in zip(zeta, delta + [jnp.zeros((1, 1), f32)])]
        current = following
        bending = sum(
            delta[i] * delta[j] * pair[i, j] for i in range(turn + 1) for j in range(turn + 1)
        )
        step = current / bending
        sigma = [
            s + step * d for s, d in zip(sigma, delta + [jnp.zeros((1, 1), f32)] * (ITERS - turn - 1))
        ]
    return sigma


def combine_kernel(
    sums, rhs, u0, u1, u2, w0, w1, w2, answer_out, rest_out, answer, rest, done
):
    picked = [
        jnp.sum(jnp.where(lanes()[:1] == i, sums[:1], 0.0), axis=1, keepdims=True)
        for i in range(ITERS * (ITERS + 3) // 2)
    ]
    b, pair, at = [], {}, 0
    for j in range(ITERS):
        b.append(picked[at])
        for i in range(j + 1):
            pair[i, j] = pair[j, i] = picked[at + 1 + i]
        at += j + 2
    s = weights(b, pair)

    def step(z, carry):
        answer[z] = s[0] * u0[z] + s[1] * u1[z] + s[2] * u2[z]
        rest[z] = rhs[z] - (s[0] * w0[z] + s[1] * w1[z] + s[2] * w2[z])
        return carry

    layers, copies = CZ // PIECES, []
    for k in range(PIECES):
        lax.fori_loop(k * layers, (k + 1) * layers, step, 0, unroll=4)
        part = pl.ds(k * layers, layers)
        for i, (source, target) in enumerate(((answer, answer_out), (rest, rest_out))):
            copies.append(
                pltpu.make_async_copy(source.at[part], target.at[part], done.at[i, k])
            )
            copies[-1].start()
    for copy in copies:
        copy.wait()


VMEM = pl.BlockSpec(memory_space=pltpu.VMEM)
HBM = pl.BlockSpec(memory_space=pl.ANY)


def call(kernel, shapes, operands, scratch=(), cost=2.0, outside=False):
    return pl.pallas_call(
        kernel,
        out_shape=[jax.ShapeDtypeStruct(shape, f32) for shape in shapes],
        in_specs=[VMEM] * len(operands),
        out_specs=[HBM if outside else VMEM] * len(shapes),
        scratch_shapes=[pltpu.VMEM(shape, f32) for shape in scratch]
        + ([pltpu.SemaphoreType.DMA((2, PIECES))] if outside else []),
        cost_estimate=pl.CostEstimate(
            flops=int(cost * 1e9), bytes_accessed=int(cost * 3.6e6), transcendentals=0
        ),
        compiler_params=pltpu.CompilerParams(vmem_limit_bytes=20 * 2**20),
    )(*operands)


def shifted(block, axis, step):
    count = lax.axis_size(axis)
    return lax.ppermute(block, axis, [(i, (i + step) % count) for i in range(count)])


def swap(low, high, axis):
    return shifted(high, axis, 1), shifted(low, axis, -1)


def ring(values, axes, count, low, size):
    parts = []
    for step in range(1, size):
        route = []
        for i in range(count):
            place = i // low % size
            route.append((i, i + ((place + step) % size - place) * low))
        parts.append(lax.ppermute(values, axes, route))
    return values + sum(parts[1:], parts[0])


def total(values):
    values = ring(values, "gy", 4, 1, 2)
    values = ring(values, ("gx", "gy"), 32, 2, 4)
    values = ring(values, "gx", 8, 2, 4)
    return ring(values, "gz", 4, 1, 4)


CORE = (CZ, CY, CX)
FIELD = (EZ, EY, UX)
PART = (EZ * EY, CX)


def per_device(rhs_field, stiffness):
    *tables, inverse = solve_tables()
    strips = call(start_columns_kernel, [(16, 8, 128)] * 2, [rhs_field, stiffness])
    columns = swap(*strips, "gx")
    fields = [rhs_field, stiffness, *columns]
    strips = call(start_rows_kernel, [(START_Y, 8, 128)] * 2, fields[:2], cost=1.0)
    rows = swap(*strips, "gy")
    strips = call(start_corners_kernel, [(8, 8, 128)] * 2, columns, cost=5.0)
    corners = swap(*strips, "gy")
    wide, stiff, *strips = call(
        start_depth_kernel,
        [(CZ, EY, UX), (UZ, UY, UX)] + [(10, UY, CX)] * 2,
        [*fields, *rows, *corners],
    )
    depths = swap(*strips, "gz")
    fields = call(start_inner_kernel, [PART] * 2, [wide, *tables], cost=4.0)
    shape = Shape(False)
    solved, stiff, *strips = call(
        start_outer_kernel,
        [FIELD, (UZ, UY, UX)] + [(shape.x_tiles, 8, 128)] * 2,
        [*depths, stiff, *fields, inverse, *tables],
        [(4, EY, UX), PART, PART],
        cost=6.0,
    )
    smooth, image, sums = [], [], []
    for turn in range(ITERS):
        shape = Shape(turn + 1 == ITERS)
        columns = swap(*strips, "gx")
        strips = call(
            functools.partial(row_strips_kernel, shape),
            [(shape.y_tiles, 8, 128)] * 2,
            [solved],
            cost=1.0,
        )
        rows = swap(*strips, "gy")
        strips = call(
            functools.partial(corners_kernel, shape), [(shape.c_tiles, 8, 128)] * 2, columns, cost=5.0
        )
        corners = swap(*strips, "gy")
        widened = call(
            functools.partial(widen_kernel, shape), [(EZ, UY, UX)], [solved, *columns]
        )[0]
        folded, *strips = call(
            functools.partial(depth_strips_kernel, shape),
            [(EZ, UY, UX)] + [(shape.rim + 1, UY, CX)] * 2,
            [widened, *rows, *corners],
            [(4, 2 * shape.x_groups, 8, 128)],
        )
        depths = swap(*strips, "gz")
        products = (turn + 2, 8, 128)
        outs = [CORE, CORE, products]
        if not shape.last:
            outs += [PART, PART]
        own, core, part, *fields = call(
            functools.partial(inner_kernel, turn, shape),
            outs,
            [folded, stiff, rhs_field, *smooth] + ([] if shape.last else tables),
            ([] if shape.last else [FIELD]) + [(40, UY, UX)] * 2,
            cost=6.0,
        )
        operands = [folded, *depths, stiff, rhs_field, *smooth]
        operands += [own, core, part]
        scratch = [(14, UY, UX)] * 3
        if shape.last:
            operands += sums
            outs = [CORE, CORE, (8, 128)]
        else:
            operands += [*fields, inverse, *tables]
            following = Shape(turn + 2 == ITERS)
            outs = [CORE, CORE, products, FIELD] + [(following.x_tiles, 8, 128)] * 2
            scratch = [PART, PART, FIELD] + scratch
        own, core, part, *rest = call(
            functools.partial(outer_kernel, turn, shape),
            outs,
            operands,
            scratch,
            cost=8.0,
        )
        if rest:
            solved, *strips = rest
        smooth.append(own)
        image.append(core)
        sums.append(part)
    operands = [total(sums[-1]), rhs_field, *smooth, *image]
    return tuple(call(combine_kernel, [CORE] * 2, operands, [CORE] * 2, outside=True))


def solution(mesh):
    in_specs = (P("gz", "gy", "gx"), P("gz", "gy", "gx"))
    out_specs = (P("gz", "gy", "gx"), P("gz", "gy", "gx"))
    return jax.shard_map(
        per_device, mesh=mesh, in_specs=in_specs, out_specs=out_specs, check_vma=False
    )
```
